256 devices in a mesh: row: 32 (over z_lo, y, core), col: 8 (over z_hi, x).
Axes of the slice: x: 4, y: 4, z: 8 (z_hi: 2, z_lo: 4; z = z_hi * 4 + z_lo), core: 2. Of those that a mesh axis runs over, the one named last changes fastest.
Arguments:
- mask_params: float32 [2048, 1200], P('row', 'col'), may hold values from -6 to 6
- target_bits: int32 [2048, 40], P('row', 'col'), may hold values from 0 to 1073741823
- kern_real: float32 [64, 768], replicated, may hold values from -0.09375 to 0.09375
- kern_imag: float32 [64, 768], replicated, may hold values from -0.09375 to 0.09375
- socs_weights: float32 [12], replicated, may hold values from 0.02 to 0.2
Outputs:
- mask_grad: float32 [2048, 1200], P('row', 'col')
- intensity: float32 [2048, 1200], P('row', 'col')
The draws below stay inside these ranges and needn't reach their ends.
All inputs are finite; a program needn't handle non-finite values.
Results may differ from the reference program's by a relative error of at most 0.0002.
Values sent between devices are 32-bit elements; how exact they have to be, the bound alone decides.
No kernel may reach another device: no remote copies, remote signals or barrier semaphores. Data moves between devices by JAX's collectives and lax.ppermute only.
A program may use at most 128 MiB of HBM per device.

```python
import math
import jax
import jax.numpy as jnp
from jax import lax

H = 32
NK = 12
ITERS = 3
KS = 64
NR = 2048
NC = 1200


def place_ends(drawn, stream_key, smallest, top_value):
    longest = drawn.shape.index(max(drawn.shape))
    spots = []
    for shift in (0, 1):
        where = [jax.random.randint(jax.random.fold_in(stream_key, axis), (), 0, length) for axis, length in enumerate(drawn.shape)]
        where[longest] = (where[longest] + shift) % drawn.shape[longest]
        spots.append(tuple(where))
    return drawn.at[spots[0]].set(smallest).at[spots[1]].set(top_value)


def block_scale(own_key, dims, pieces, smallest, high):
    gain, own = 1.0, jax.random.fold_in(own_key, 6)
    for position, blocks in pieces:
        draws = jnp.exp(jax.random.uniform(jax.random.fold_in(own, position), (blocks,), jnp.float32, smallest / len(pieces), high / len(pieces)))
        gain = gain * jnp.repeat(draws, dims[position] // blocks).reshape([-1 if axis == position else 1 for axis in range(len(dims))])
    return gain


def gaussian(key, extent, scale, reach, cuts=(), kind=jnp.bfloat16):
    entries = jax.random.normal(key, extent, jnp.float32) * scale
    if len(cuts) > 0:
        entries = block_scale(key, extent, cuts, -0.22, 0.18) * entries
    return jnp.clip(entries, min=-reach, max=reach).astype(kind)


def setup_inputs(seed: int = 0) -> dict:
    streams_of = jax.random.split(jax.random.key(seed), 6)
    mask_params = gaussian(streams_of[0], (NR, NC), 1.0, 6.0, ((0, 32), (1, 8)), jnp.float32)
    target_bits = place_ends(jax.random.randint(streams_of[1], (NR, NC // 30), 0, 2**30), jax.random.fold_in(streams_of[1], 1), 0, (2**30) - 1).astype(jnp.int32)
    kern_real = gaussian(streams_of[2], (KS, NK * KS), (KS * KS) ** -0.5, 0.09375, (), jnp.float32)
    kern_imag = gaussian(streams_of[3], (KS, NK * KS), (KS * KS) ** -0.5, 0.09375, (), jnp.float32)
    socs_weights = jnp.clip(jnp.exp(jax.random.uniform(streams_of[4], (NK,), jnp.float32, math.log(0.02), math.log(0.2))), 0.02, 0.2)
    return dict(mask_params=mask_params, target_bits=target_bits, kern_real=kern_real, kern_imag=kern_imag, socs_weights=socs_weights)


sharpness = 2.0
steepness = 4.0
threshold = 0.8
step_size = 1.0


def reference(mask_params, target_bits, kern_real, kern_imag, socs_weights):
    column = jnp.arange(NC, dtype=jnp.int32)
    packed = target_bits[:, column // 30]
    target = jnp.bitwise_and(jnp.right_shift(packed, column % 30), 1).astype(jnp.float32)
    taps_real = jnp.transpose(kern_real.reshape(KS, NK, KS), (1, 0, 2))
    taps_imag = jnp.transpose(kern_imag.reshape(KS, NK, KS), (1, 0, 2))
    shape_full = (NR + KS - 1, NC + KS - 1)
    forward_specs = []
    backward_specs = []
    for kernel_index in range(NK):
        kernel = lax.complex(taps_real[kernel_index], taps_imag[kernel_index])
        forward_specs.append(jnp.fft.fft2(kernel, s=shape_full))
        backward_specs.append(jnp.fft.fft2(jnp.flip(kernel, (0, 1)), s=shape_full))
    params = mask_params
    mask_grad = jnp.zeros((NR, NC), jnp.float32)
    intensity = jnp.zeros((NR, NC), jnp.float32)
    for iteration in range(ITERS):
        mask_field = jax.nn.sigmoid(sharpness * params)
        mask_spec = jnp.fft.fft2(mask_field, s=shape_full)
        intensity = jnp.zeros((NR, NC), jnp.float32)
        fields = []
        for kernel_index in range(NK):
            near_field = jnp.fft.ifft2(mask_spec * forward_specs[kernel_index])[H:H + NR, H:H + NC]
            real_part = jnp.real(near_field)
            imag_part = jnp.imag(near_field)
            fields.append((real_part, imag_part))
            intensity = intensity + socs_weights[kernel_index] * (real_part * real_part + imag_part * imag_part)
        resist = jax.nn.sigmoid(steepness * (intensity - threshold))
        cotangent = 2.0 * (resist - target) * steepness * resist * (1.0 - resist)
        adjoint_spec = None
        for kernel_index in range(NK):
            scaled = 2.0 * socs_weights[kernel_index] * cotangent
            source = lax.complex(scaled * fields[kernel_index][0], -scaled * fields[kernel_index][1])
            product_term = jnp.fft.fft2(source, s=shape_full) * backward_specs[kernel_index]
            adjoint_spec = product_term if adjoint_spec is None else adjoint_spec + product_term
        mask_grad = jnp.real(jnp.fft.ifft2(adjoint_spec))[H - 1:H - 1 + NR, H - 1:H - 1 + NC]
        if iteration + 1 < ITERS:
            params = params - step_size * sharpness * mask_field * (1.0 - mask_field) * mask_grad
    return mask_grad, intensity
```

```python
import functools
import math

import jax
import jax.numpy as jnp
import ml_dtypes
import numpy as np
from jax import lax
from jax.experimental import pallas as pl
from jax.experimental.pallas import tpu as pltpu
from jax.sharding import PartitionSpec as P

H = 32
KS = 64
ITERS = 3
ROWS = 128
sharpness = 2.0
steepness = 4.0
threshold = 0.8
step_size = 1.0
f32 = jnp.float32
bf16 = jnp.bfloat16


def up(value, unit):
    return -(-value // unit) * unit


def halves(table):
    table = table.astype(np.float32)
    high = table.astype(ml_dtypes.bfloat16)
    low = (table - high.astype(np.float32)).astype(ml_dtypes.bfloat16)
    return high, low


def angles(left, right, length):
    product = np.outer(left.astype(np.int64), right.astype(np.int64)) % length
    return product * (2.0 * math.pi / length)


def grown(table, rows, cols):
    return np.pad(table, [(0, rows - table.shape[0]), (0, cols - table.shape[1])])


def left_stack(table):
    high, low = halves(table)
    return np.concatenate([high, high, low], 1)


def right_stack(table):
    high, low = halves(table)
    return np.concatenate([high, high, low], 0)


class Geometry:
    def __init__(self, width):
        self.mask = width
        self.field = width - 2 * H
        self.grad = width - 4 * H
        self.length = width | 1
        self.freqs = (self.length + 1) // 2
        self.freqs_up = up(self.freqs, 16)
        self.mask_up = up(self.mask, 16)
        self.field_up = up(self.field, 16)
        self.grad_up = up(self.grad, 8)

    def tables(self):
        freq = np.arange(self.freqs)
        fu = self.freqs_up

        def forward(count, count_up):
            phase = angles(freq, np.arange(count), self.length)
            return np.concatenate(
                [grown(np.cos(phase), fu, count_up), grown(-np.sin(phase), fu, count_up)], 0
            )

        def inverse(places, count_up):
            phase = angles(places, freq, self.length)
            weight = np.where(freq == 0, 1.0, 2.0) / (self.length * ROWS)
            return np.concatenate(
                [
                    grown(np.cos(phase) * weight, count_up, fu),
                    grown(-np.sin(phase) * weight, count_up, fu),
                ],
                1,
            )

        taps = angles(freq, np.arange(KS) - H, self.length)
        return dict(
            mask_cols=left_stack(forward(self.mask, self.mask_up)),
            field_cols=left_stack(inverse(np.arange(self.field) + H, self.field_up)),
            source_cols=left_stack(forward(self.field, self.field_up)),
            grad_cols=left_stack(inverse(np.arange(self.grad) + H, self.grad_up)),
            tap_cols=left_stack(
                np.concatenate([grown(np.cos(taps), fu, KS), grown(np.sin(taps), fu, KS)], 1)
            ),
        )


def row_tables():
    freq = np.arange(ROWS)

    def complex_table(phase, sign):
        cos, sin = np.cos(phase), sign * np.sin(phase)
        return np.block([[cos, sin], [-sin, cos]])

    def side(table):
        high, low = halves(table)
        return np.concatenate([high, low], 1)

    places = np.arange(64) + H
    field = complex_table(angles(freq, places, ROWS), 1.0)
    field_swapped = np.concatenate([field[:, 64:], field[:, :64]], 1)
    source = complex_table(angles(np.arange(64), freq, ROWS), -1.0)
    source_swapped = np.concatenate([source[64:], source[:64]], 0)
    taps = angles(np.arange(KS) - H, freq, ROWS)
    tap = np.concatenate([np.cos(taps), -np.sin(taps)], 1)
    zero = np.zeros_like(tap)
    return dict(
        mask_rows=right_stack(complex_table(angles(freq, freq, ROWS), -1.0)),
        field_rows=side(field),
        field_rows_swapped=side(field_swapped),
        source_rows=right_stack(source),
        source_rows_swapped=right_stack(source_swapped),
        grad_rows=right_stack(complex_table(angles(freq, freq - H, ROWS), 1.0)),
        tap_rows=right_stack(np.block([[tap, zero], [zero, tap]])),
    )


def split(value):
    high = value.astype(bf16)
    return high, (value - high.astype(f32)).astype(bf16)


def dot(left, right):
    return lax.dot_general(
        left, right, (((1,), (0,)), ((), ())), preferred_element_type=f32
    )


def left_dot(table, value):
    high, low = split(value)
    return dot(table, jnp.concatenate([high, low, high], 0))


def right_dot(value, table):
    high, low = split(value)
    return dot(jnp.concatenate([high, low, high], 1), table)


def sigmoid(value):
    return 1.0 / (1.0 + jnp.exp(-value))


def swap_halves(value):
    return pltpu.roll(value, 64, 1)


def window(shape, first_col, first_row, whole_cols, whole_rows):
    col = lax.broadcasted_iota(jnp.int32, shape, 0) + first_col
    row = lax.broadcasted_iota(jnp.int32, shape, 1) + first_row
    return (col >= 0) & (col < whole_cols) & (row >= 0) & (row < whole_rows)


def setup_kernel(geos, kern_real, kern_imag, tap_rows, *rest):
    tables, outs, scratch = rest[: len(geos)], rest[len(geos) : -1], rest[-1]
    kernels = kern_real.shape[1] // KS
    both = jnp.concatenate([kern_real[...], kern_imag[...]], 0)
    for start in range(0, both.shape[1], 128):
        part = both[:, start : start + 128].T
        scratch[start : start + 128, :] = right_dot(part, tap_rows[...])
    for k in range(kernels):
        half = scratch[k * KS : (k + 1) * KS, :]
        turned = jnp.concatenate(
            [half[:, 128:256], -half[:, 0:128], half[:, 384:512], -half[:, 256:384]], 1
        )
        high, low = split(jnp.concatenate([half, turned], 0))
        stacked = jnp.concatenate([high, low, high], 0)
        for geo, table, out in zip(geos, tables, outs):
            spec = dot(table[...], stacked)
            count = geo.freqs_up
            out[2 * k * count : (2 * k + 1) * count, :] = spec[:, :256]
            out[(2 * k + 1) * count : (2 * k + 2) * count, :] = spec[:, 256:]


def one_step(geo, mask, target, inside, weights, spec, tabs, fields):
    count = geo.freqs_up
    kernels = weights.shape[0]
    lane = lax.broadcasted_iota(jnp.int32, (count, 128), 1) < 64
    across = left_dot(tabs["mask_cols"][...], mask)
    mask_spec = right_dot(
        jnp.concatenate([across[:count], across[count:]], 1), tabs["mask_rows"][...]
    )
    mask_re, mask_im = mask_spec[:, :128], mask_spec[:, 128:]

    def down(index, table):
        place = spec[index * count : (index + 1) * count, :]
        re, im = place[:, :128], place[:, 128:]
        product = jnp.concatenate(
            [re * mask_re - im * mask_im, re * mask_im + im * mask_re], 1
        )
        high, low = split(product)
        wide = dot(high, table[...])
        return wide[:, :128] + wide[:, 128:] + dot(low, table[:, :128])

    intensity = jnp.zeros((geo.field_up, 128), f32)
    for k in range(0, kernels, 2):
        parts = []
        for j in (k, k + 1):
            first = down(2 * j, tabs["field_rows"])
            second = down(2 * j + 1, tabs["field_rows_swapped"])
            parts.append(
                jnp.concatenate(
                    [
                        jnp.where(lane, first, second),
                        swap_halves(jnp.where(lane, second, first)),
                    ],
                    0,
                )
            )
        field = left_dot(tabs["field_cols"][...], jnp.concatenate(parts, 1))
        for j in (0, 1):
            own = field[:, j * 128 : (j + 1) * 128]
            fields[k + j] = own
            intensity = intensity + weights[k + j] * (own * own)
    intensity = intensity + swap_halves(intensity)
    resist = sigmoid(steepness * (intensity - threshold))
    cotangent = 2.0 * (resist - target) * steepness * resist * (1.0 - resist)
    cotangent = jnp.where(inside, cotangent, 0.0)
    total_re = jnp.zeros((count, 128), f32)
    total_im = jnp.zeros((count, 128), f32)
    for k in range(0, kernels, 2):
        source = jnp.concatenate(
            [(2.0 * weights[j] * cotangent) * fields[j] for j in (k, k + 1)], 1
        )
        across = left_dot(tabs["source_cols"][...], source)
        for j in (0, 1):
            re = across[:count, j * 128 : (j + 1) * 128]
            im = swap_halves(across[count:, j * 128 : (j + 1) * 128])
            for index, value, table in (
                (0, jnp.where(lane, re, im), tabs["source_rows"]),
                (1, jnp.where(lane, im, re), tabs["source_rows_swapped"]),
            ):
                got = right_dot(value, table[...])
                got_re, got_im = got[:, :128], got[:, 128:]
                start = (2 * (k + j) + index) * count
                place = spec[start : start + count, :]
                re_k, im_k = place[:, :128], place[:, 128:]
                total_re = total_re + (re_k * got_re + im_k * got_im)
                total_im = total_im + (re_k * got_im - im_k * got_re)
    back = right_dot(jnp.concatenate([total_re, total_im], 1), tabs["grad_rows"][...])
    grad = left_dot(
        tabs["grad_cols"][...], jnp.concatenate([back[:, :128], back[:, 128:]], 0)
    )
    return intensity, grad[: geo.grad]


STEP_TABLES = (
    "mask_cols",
    "mask_rows",
    "field_rows",
    "field_rows_swapped",
    "field_cols",
    "source_cols",
    "source_rows",
    "source_rows_swapped",
    "grad_rows",
    "grad_cols",
)


def prep_kernel(place, own, across, within, bits, params, target, to_left, to_right, tall):
    even = place[0] % 2 == 0
    cols = own.shape[1]
    tall[...] = jnp.zeros_like(tall)
    tall[0:32, :cols] = jnp.where(even, across[32:64, :], within[32:64, :])
    tall[32:96, :cols] = own[...]
    tall[96:128, :cols] = jnp.where(even, within[0:32, :], across[0:32, :])
    params[...] = tall[...].T[:cols]
    col = lax.broadcasted_iota(jnp.int32, (64, tall.shape[1]), 1)
    word = jnp.zeros_like(col)
    for index in range(bits.shape[1]):
        word = jnp.where(col // 30 == index, bits[:, index : index + 1], word)
    bit = jnp.bitwise_and(jnp.right_shift(word, col % 30), 1).astype(f32)
    target[...] = jnp.concatenate([bit, bit], 0).T[:cols]
    to_left[0:128, :] = params[0:128, :]
    to_left[128:224, :] = target[0:96, :]
    to_right[0:128, :] = params[cols - 128 : cols, :]
    to_right[128:224, :] = target[cols - 96 : cols, :]


def gathered(even, own, across, within):
    lane = lax.broadcasted_iota(jnp.int32, own.shape, 1) >= 64
    above = jnp.where(even, across[...], within[...])
    below = jnp.where(even, within[...], across[...])
    return own[...] + swap_halves(jnp.where(lane, above, below))


def stepped(params, grad):
    field = sigmoid(sharpness * params)
    return params - step_size * sharpness * field * (1.0 - field) * grad


def masked(geo, place, tile, whole, params, col_offset):
    first_col = place[1] * tile[1] + col_offset
    first_row = place[0] * tile[0] - H
    inside = window(params.shape, first_col, first_row, whole[1], whole[0])
    return jnp.where(inside, sigmoid(sharpness * params), 0.0)


def field_window(geo, place, tile, whole, col_offset):
    first_col = place[1] * tile[1] + col_offset + H
    return window((geo.field_up, 128), first_col, 0, whole[1], 1 << 30)


def first_kernel(
    geo, tile, whole, place, weights, own, target, left, right, spec, *rest
):
    tabs = dict(zip(STEP_TABLES, rest))
    spread, params_out, target_out, params, goal, fields = rest[len(STEP_TABLES) :]
    cols = own.shape[0]
    params[...] = jnp.zeros_like(params)
    params[0:128, :] = left[0:128, :]
    params[128 : 128 + cols, :] = own[...]
    params[128 + cols : 256 + cols, :] = right[0:128, :]
    goal[...] = jnp.zeros_like(goal)
    goal[0:96, :] = left[128:224, :]
    goal[96 : 96 + cols, :] = target[...]
    goal[96 + cols : 192 + cols, :] = right[128:224, :]
    mask = masked(geo, place, tile, whole, params[...], -128)
    inside = field_window(geo, place, tile, whole, -128)
    _, grad = one_step(geo, mask, goal[...], inside, weights, spec, tabs, fields)
    spread[...] = grad
    params_out[...] = params[64 : 64 + params_out.shape[0], :]
    target_out[...] = goal[64 : 64 + target_out.shape[0], :]


def second_kernel(
    geo, tile, whole, place, weights, own, across, within, old, target, spec, *rest
):
    tabs = dict(zip(STEP_TABLES, rest))
    spread, params_out, params, goal, fields = rest[len(STEP_TABLES) :]
    even = place[0] % 2 == 0
    width = own.shape[0]
    params[...] = jnp.zeros_like(params)
    params[0:width, :] = stepped(old[...], gathered(even, own, across, within))
    goal[...] = jnp.zeros_like(goal)
    goal[0 : target.shape[0], :] = target[...]
    mask = masked(geo, place, tile, whole, params[...], -64)
    inside = field_window(geo, place, tile, whole, -64)
    _, grad = one_step(geo, mask, goal[...], inside, weights, spec, tabs, fields)
    spread[...] = grad
    params_out[...] = params[64 : 64 + params_out.shape[0], :]


def update_kernel(place, own, across, within, old, params, to_left, to_right):
    even = place[0] % 2 == 0
    params[...] = stepped(old[...], gathered(even, own, across, within))
    cols = params.shape[0]
    to_left[...] = params[0:64, :]
    to_right[...] = params[cols - 64 : cols, :]


def third_kernel(
    geo, tile, whole, place, weights, own, left, right, target, spec, *rest
):
    tabs = dict(zip(STEP_TABLES, rest))
    spread, intensity_out, params, goal, fields = rest[len(STEP_TABLES) :]
    cols = own.shape[0]
    params[...] = jnp.zeros_like(params)
    params[0:64, :] = left[...]
    params[64 : 64 + cols, :] = own[...]
    params[64 + cols : 128 + cols, :] = right[...]
    goal[...] = jnp.zeros_like(goal)
    goal[0 : target.shape[0], :] = target[...]
    mask = masked(geo, place, tile, whole, params[...], -64)
    inside = field_window(geo, place, tile, whole, -64)
    aim = goal[0 : geo.field_up, :]
    intensity, grad = one_step(geo, mask, aim, inside, weights, spec, tabs, fields)
    spread[...] = grad
    goal[0 : geo.field_up, :] = intensity
    goal[0:256, :] = jnp.concatenate(
        [goal[H : H + cols, :], jnp.zeros((256 - cols, 128), f32)], 0
    )
    intensity_out[...] = goal[0:256, :].T[:64, :cols]


def final_kernel(place, own, across, within, out, wide):
    even = place[0] % 2 == 0
    cols = own.shape[0]
    wide[...] = jnp.zeros_like(wide)
    wide[0:cols, :] = gathered(even, own, across, within)
    out[...] = wide[...].T[H : H + 64, :cols]


def call(kernel, name, out_shapes, scratch, args, scalars):
    specs = [pl.BlockSpec(memory_space=pltpu.SMEM)] * scalars
    specs += [pl.BlockSpec(memory_space=pltpu.VMEM)] * (len(args) - scalars)
    return pl.pallas_call(
        kernel,
        name=name,
        out_shape=[jax.ShapeDtypeStruct(shape, f32) for shape in out_shapes],
        in_specs=specs,
        out_specs=[pl.BlockSpec(memory_space=pltpu.VMEM)] * len(out_shapes),
        scratch_shapes=[pltpu.VMEM(shape, f32) for shape in scratch],
        compiler_params=pltpu.CompilerParams(vmem_limit_bytes=56 * 1024 * 1024),
    )(*args)


def per_device(rows, cols, mask_params, target_bits, kern_real, kern_imag, socs_weights):
    tile = mask_params.shape
    whole = (tile[0] * rows, tile[1] * cols)
    kernels = kern_real.shape[1] // KS
    near = [(i, i ^ 1) for i in range(rows)]
    far = [(i, i + 1) for i in range(1, rows - 1, 2)]
    far = far + [(b, a) for a, b in far]
    right = [(i, i + 1) for i in range(cols - 1)]
    left = [(b, a) for a, b in right]
    place = jnp.stack([lax.axis_index("row"), lax.axis_index("col")]).astype(jnp.int32)

    def row_exchange(value):
        return lax.ppermute(value, "row", far), lax.ppermute(value, "row", near)

    def col_exchange(to_left, to_right):
        return lax.ppermute(to_right, "col", right), lax.ppermute(to_left, "col", left)

    wide, slim = Geometry(tile[1] + 8 * H), Geometry(tile[1] + 4 * H)
    shared = row_tables()
    wide_tabs, slim_tabs = {**wide.tables(), **shared}, {**slim.tables(), **shared}

    def tabs(table):
        return [jnp.asarray(table[name]) for name in STEP_TABLES]

    across, within = row_exchange(mask_params)
    n = tile[1]
    params, target, to_left, to_right = call(
        prep_kernel,
        "prep",
        [(n, 128), (n, 128), (224, 128), (224, 128)],
        [(128, 256)],
        [place, mask_params, across, within, target_bits],
        1,
    )
    from_left, from_right = col_exchange(to_left, to_right)
    wide_spec, slim_spec = call(
        functools.partial(setup_kernel, (wide, slim)),
        "spectra",
        [(2 * kernels * geo.freqs_up, 256) for geo in (wide, slim)],
        [(kernels * KS, 512)],
        [
            kern_real,
            kern_imag,
            jnp.asarray(shared["tap_rows"]),
            jnp.asarray(wide_tabs["tap_cols"]),
            jnp.asarray(slim_tabs["tap_cols"]),
        ],
        0,
    )

    def scratch(geo):
        return [(geo.mask_up, 128), (geo.field_up, 128), (kernels, geo.field_up, 128)]

    spread, params, target = call(
        functools.partial(first_kernel, wide, tile, whole),
        "first",
        [(wide.grad, 128), (slim.mask, 128), (slim.field, 128)],
        scratch(wide),
        [place, socs_weights, params, target, from_left, from_right, wide_spec, *tabs(wide_tabs)],
        2,
    )
    across, within = row_exchange(spread)
    spread, params = call(
        functools.partial(second_kernel, slim, tile, whole),
        "second",
        [(slim.grad, 128), (n, 128)],
        scratch(slim),
        [place, socs_weights, spread, across, within, params, target, slim_spec, *tabs(slim_tabs)],
        2,
    )
    across, within = row_exchange(spread)
    params, to_left, to_right = call(
        update_kernel,
        "update",
        [(n, 128), (64, 128), (64, 128)],
        [],
        [place, spread, across, within, params],
        1,
    )
    from_left, from_right = col_exchange(to_left, to_right)
    third_scratch = scratch(slim)
    third_scratch[1] = (max(256, slim.field_up), 128)
    spread, intensity = call(
        functools.partial(third_kernel, slim, tile, whole),
        "third",
        [(slim.grad, 128), tile],
        third_scratch,
        [place, socs_weights, params, from_left, from_right, target, slim_spec, *tabs(slim_tabs)],
        2,
    )
    across, within = row_exchange(spread)
    (mask_grad,) = call(
        final_kernel,
        "final",
        [tile],
        [(256, 128)],
        [place, spread, across, within],
        1,
    )
    return mask_grad, intensity


def solution(mesh):
    placed = (P("row", "col"), P("row", "col"), P(), P(), P())
    return jax.shard_map(
        functools.partial(per_device, mesh.shape["row"], mesh.shape["col"]),
        mesh=mesh,
        in_specs=placed,
        out_specs=(P("row", "col"), P("row", "col")),
        check_vma=False,
    )
```

```python
import functools
import math

import jax
import jax.numpy as jnp
import ml_dtypes
import numpy as np
from jax import lax
from jax.experimental import pallas as pl
from jax.experimental.pallas import tpu as pltpu
from jax.sharding import PartitionSpec as P

H = 32
KS = 64
ITERS = 3
ROWS = 128
sharpness = 2.0
steepness = 4.0
threshold = 0.8
step_size = 1.0
f32 = jnp.float32
bf16 = jnp.bfloat16


def up(value, unit):
    return -(-value // unit) * unit


def halves(table):
    table = table.astype(np.float32)
    high = table.astype(ml_dtypes.bfloat16)
    low = (table - high.astype(np.float32)).astype(ml_dtypes.bfloat16)
    return high, low


def angles(left, right, length):
    product = np.outer(left.astype(np.int64), right.astype(np.int64)) % length
    return product * (2.0 * math.pi / length)


def grown(table, rows, cols):
    return np.pad(table, [(0, rows - table.shape[0]), (0, cols - table.shape[1])])


def left_stack(table):
    high, low = halves(table)
    return np.concatenate([high, high, low], 1)


def right_stack(table):
    high, low = halves(table)
    return np.concatenate([high, high, low], 0)


class Geometry:
    def __init__(self, width):
        self.mask = width
        self.field = width - 2 * H
        self.grad = width - 4 * H
        self.length = width | 1
        self.freqs = (self.length + 1) // 2
        self.freqs_up = up(self.freqs, 16)
        self.mask_up = up(self.mask, 16)
        self.field_up = up(self.field, 16)
        self.grad_up = up(self.grad, 8)

    def tables(self):
        freq = np.arange(self.freqs)
        fu = self.freqs_up

        def forward(count, count_up):
            phase = angles(freq, np.arange(count), self.length)
            return np.concatenate(
                [grown(np.cos(phase), fu, count_up), grown(-np.sin(phase), fu, count_up)], 0
            )

        def inverse(places, count_up):
            phase = angles(places, freq, self.length)
            weight = np.where(freq == 0, 1.0, 2.0) / (self.length * ROWS)
            return np.concatenate(
                [
                    grown(np.cos(phase) * weight, count_up, fu),
                    grown(-np.sin(phase) * weight, count_up, fu),
                ],
                1,
            )

        taps = angles(freq, np.arange(KS) - H, self.length)
        return dict(
            mask_cols=left_stack(forward(self.mask, self.mask_up)),
            field_cols=left_stack(inverse(np.arange(self.field) + H, self.field_up)),
            source_cols=left_stack(forward(self.field, self.field_up)),
            grad_cols=left_stack(inverse(np.arange(self.grad) + H, self.grad_up)),
            tap_cols=left_stack(
                np.concatenate([grown(np.cos(taps), fu, KS), grown(np.sin(taps), fu, KS)], 1)
            ),
        )


def row_tables():
    freq = np.arange(ROWS)

    def complex_table(phase, sign):
        cos, sin = np.cos(phase), sign * np.sin(phase)
        return np.block([[cos, sin], [-sin, cos]])

    def side(table):
        high, low = halves(table)
        return np.concatenate([high, low], 1)

    places = np.arange(64) + H
    field = complex_table(angles(freq, places, ROWS), 1.0)
    field_swapped = np.concatenate([field[:, 64:], field[:, :64]], 1)
    source = complex_table(angles(np.arange(64), freq, ROWS), -1.0)
    source_swapped = np.concatenate([source[64:], source[:64]], 0)
    taps = angles(np.arange(KS) - H, freq, ROWS)
    tap = np.concatenate([np.cos(taps), -np.sin(taps)], 1)
    zero = np.zeros_like(tap)
    return dict(
        mask_rows=right_stack(complex_table(angles(freq, freq, ROWS), -1.0)),
        field_rows=side(field),
        field_rows_swapped=side(field_swapped),
        source_rows=right_stack(source),
        source_rows_swapped=right_stack(source_swapped),
        grad_rows=right_stack(complex_table(angles(freq, freq - H, ROWS), 1.0)),
        tap_rows=right_stack(np.block([[tap, zero], [zero, tap]])),
    )


def split(value):
    high = value.astype(bf16)
    return high, (value - high.astype(f32)).astype(bf16)


def dot(left, right):
    return lax.dot_general(
        left, right, (((1,), (0,)), ((), ())), preferred_element_type=f32
    )


def left_dot(table, value):
    high, low = split(value)
    return dot(table, jnp.concatenate([high, low, high], 0))


def right_dot(value, table):
    high, low = split(value)
    return dot(jnp.concatenate([high, low, high], 1), table)


def sigmoid(value):
    return 1.0 / (1.0 + jnp.exp(-value))


def swap_halves(value):
    return pltpu.roll(value, 64, 1)


def window(shape, first_col, first_row, whole_cols, whole_rows):
    col = lax.broadcasted_iota(jnp.int32, shape, 0) + first_col
    row = lax.broadcasted_iota(jnp.int32, shape, 1) + first_row
    return (col >= 0) & (col < whole_cols) & (row >= 0) & (row < whole_rows)


def setup_kernel(geos, held, kern_real, kern_imag, tap_rows, *rest):
    tables, rest = rest[: len(geos)], rest[len(geos) :]
    sources, rest = rest[:held], rest[held:]
    outs, rest = rest[: len(geos)], rest[len(geos) :]
    targets, (scratch, sems) = rest[:held], rest[held:]
    copies = [
        pltpu.make_async_copy(source, target, sems.at[index])
        for index, (source, target) in enumerate(zip(sources, targets))
    ]
    for copy in copies:
        copy.start()
    kernels = kern_real.shape[1] // KS
    both = jnp.concatenate([kern_real[...], kern_imag[...]], 0)
    for start in range(0, both.shape[1], 128):
        part = both[:, start : start + 128].T
        scratch[start : start + 128, :] = right_dot(part, tap_rows[...])
    for k in range(kernels):
        half = scratch[k * KS : (k + 1) * KS, :]
        turned = jnp.concatenate(
            [half[:, 128:256], -half[:, 0:128], half[:, 384:512], -half[:, 256:384]], 1
        )
        high, low = split(jnp.concatenate([half, turned], 0))
        stacked = jnp.concatenate([high, low, high], 0)
        for geo, table, out in zip(geos, tables, outs):
            spec = dot(table[...], stacked)
            count = geo.freqs_up
            out[2 * k * count : (2 * k + 1) * count, :] = spec[:, :256]
            out[(2 * k + 1) * count : (2 * k + 2) * count, :] = spec[:, 256:]
    for copy in copies:
        copy.wait()


def one_step(geo, mask, target, inside, weights, spec, tabs, fields):
    count = geo.freqs_up
    kernels = weights.shape[0]
    lane = lax.broadcasted_iota(jnp.int32, (count, 128), 1) < 64
    across = left_dot(tabs["mask_cols"][...], mask)
    mask_spec = right_dot(
        jnp.concatenate([across[:count], across[count:]], 1), tabs["mask_rows"][...]
    )
    mask_re, mask_im = mask_spec[:, :128], mask_spec[:, 128:]

    def down(index, table):
        place = spec[index * count : (index + 1) * count, :]
        re, im = place[:, :128], place[:, 128:]
        product = jnp.concatenate(
            [re * mask_re - im * mask_im, re * mask_im + im * mask_re], 1
        )
        high, low = split(product)
        wide = dot(high, table[...])
        return wide[:, :128] + wide[:, 128:] + dot(low, table[:, :128])

    intensity = jnp.zeros((geo.field_up, 128), f32)
    for k in range(0, kernels, 2):
        parts = []
        for j in (k, k + 1):
            first = down(2 * j, tabs["field_rows"])
            second = down(2 * j + 1, tabs["field_rows_swapped"])
            parts.append(
                jnp.concatenate(
                    [
                        jnp.where(lane, first, second),
                        swap_halves(jnp.where(lane, second, first)),
                    ],
                    0,
                )
            )
        field = left_dot(tabs["field_cols"][...], jnp.concatenate(parts, 1))
        for j in (0, 1):
            own = field[:, j * 128 : (j + 1) * 128]
            fields[k + j] = own
            intensity = intensity + weights[k + j] * (own * own)
    intensity = intensity + swap_halves(intensity)
    resist = sigmoid(steepness * (intensity - threshold))
    cotangent = 2.0 * (resist - target) * steepness * resist * (1.0 - resist)
    cotangent = jnp.where(inside, cotangent, 0.0)
    total_re = jnp.zeros((count, 128), f32)
    total_im = jnp.zeros((count, 128), f32)
    for k in range(0, kernels, 2):
        source = jnp.concatenate(
            [(2.0 * weights[j] * cotangent) * fields[j] for j in (k, k + 1)], 1
        )
        across = left_dot(tabs["source_cols"][...], source)
        for j in (0, 1):
            re = across[:count, j * 128 : (j + 1) * 128]
            im = swap_halves(across[count:, j * 128 : (j + 1) * 128])
            for index, value, table in (
                (0, jnp.where(lane, re, im), tabs["source_rows"]),
                (1, jnp.where(lane, im, re), tabs["source_rows_swapped"]),
            ):
                got = right_dot(value, table[...])
                got_re, got_im = got[:, :128], got[:, 128:]
                start = (2 * (k + j) + index) * count
                place = spec[start : start + count, :]
                re_k, im_k = place[:, :128], place[:, 128:]
                total_re = total_re + (re_k * got_re + im_k * got_im)
                total_im = total_im + (re_k * got_im - im_k * got_re)
    back = right_dot(jnp.concatenate([total_re, total_im], 1), tabs["grad_rows"][...])
    grad = left_dot(
        tabs["grad_cols"][...], jnp.concatenate([back[:, :128], back[:, 128:]], 0)
    )
    return intensity, grad[: geo.grad]


COLUMN_TABLES = ("mask_cols", "field_cols", "source_cols", "grad_cols")
ROW_TABLES = (
    "mask_rows",
    "field_rows",
    "field_rows_swapped",
    "source_rows",
    "source_rows_swapped",
    "grad_rows",
)
STEP_TABLES = COLUMN_TABLES + ROW_TABLES


def prep_kernel(place, own, across, within, bits, params, target, to_left, to_right, tall):
    even = place[0] % 2 == 0
    cols = own.shape[1]
    tall[...] = jnp.zeros_like(tall)
    tall[0:32, :cols] = jnp.where(even, across[32:64, :], within[32:64, :])
    tall[32:96, :cols] = own[...]
    tall[96:128, :cols] = jnp.where(even, within[0:32, :], across[0:32, :])
    params[...] = tall[...].T[:cols]
    col = lax.broadcasted_iota(jnp.int32, (64, tall.shape[1]), 1)
    word = jnp.zeros_like(col)
    for index in range(bits.shape[1]):
        word = jnp.where(col // 30 == index, bits[:, index : index + 1], word)
    bit = jnp.bitwise_and(jnp.right_shift(word, col % 30), 1).astype(f32)
    target[...] = jnp.concatenate([bit, bit], 0).T[:cols]
    to_left[0:128, :] = params[0:128, :]
    to_left[128:224, :] = target[0:96, :]
    to_right[0:128, :] = params[cols - 128 : cols, :]
    to_right[128:224, :] = target[cols - 96 : cols, :]


def gathered(even, own, across, within):
    lane = lax.broadcasted_iota(jnp.int32, own.shape, 1) >= 64
    above = jnp.where(even, across[...], within[...])
    below = jnp.where(even, within[...], across[...])
    return own[...] + swap_halves(jnp.where(lane, above, below))


def stepped(params, grad):
    field = sigmoid(sharpness * params)
    return params - step_size * sharpness * field * (1.0 - field) * grad


def masked(geo, place, tile, whole, params, col_offset):
    first_col = place[1] * tile[1] + col_offset
    first_row = place[0] * tile[0] - H
    inside = window(params.shape, first_col, first_row, whole[1], whole[0])
    return jnp.where(inside, sigmoid(sharpness * params), 0.0)


def field_window(geo, place, tile, whole, col_offset):
    first_col = place[1] * tile[1] + col_offset + H
    return window((geo.field_up, 128), first_col, 0, whole[1], 1 << 30)


def first_kernel(
    geo, tile, whole, place, weights, own, target, left, right, spec, *rest
):
    tabs = dict(zip(STEP_TABLES, rest))
    spread, params_out, target_out, params, goal, fields = rest[len(STEP_TABLES) :]
    cols = own.shape[0]
    params[...] = jnp.zeros_like(params)
    params[0:128, :] = left[0:128, :]
    params[128 : 128 + cols, :] = own[...]
    params[128 + cols : 256 + cols, :] = right[0:128, :]
    goal[...] = jnp.zeros_like(goal)
    goal[0:96, :] = left[128:224, :]
    goal[96 : 96 + cols, :] = target[...]
    goal[96 + cols : 192 + cols, :] = right[128:224, :]
    mask = masked(geo, place, tile, whole, params[...], -128)
    inside = field_window(geo, place, tile, whole, -128)
    _, grad = one_step(geo, mask, goal[...], inside, weights, spec, tabs, fields)
    spread[...] = grad
    params_out[...] = params[64 : 64 + params_out.shape[0], :]
    target_out[...] = goal[64 : 64 + target_out.shape[0], :]


def second_kernel(
    geo, tile, whole, place, weights, own, across, within, old, target, spec, *rest
):
    tabs = dict(zip(STEP_TABLES, rest))
    spread, params_out, params, goal, fields = rest[len(STEP_TABLES) :]
    even = place[0] % 2 == 0
    width = own.shape[0]
    params[...] = jnp.zeros_like(params)
    params[0:width, :] = stepped(old[...], gathered(even, own, across, within))
    goal[...] = jnp.zeros_like(goal)
    goal[0 : target.shape[0], :] = target[...]
    mask = masked(geo, place, tile, whole, params[...], -64)
    inside = field_window(geo, place, tile, whole, -64)
    _, grad = one_step(geo, mask, goal[...], inside, weights, spec, tabs, fields)
    spread[...] = grad
    params_out[...] = params[64 : 64 + params_out.shape[0], :]


def update_kernel(place, own, across, within, old, params, to_left, to_right):
    even = place[0] % 2 == 0
    params[...] = stepped(old[...], gathered(even, own, across, within))
    cols = params.shape[0]
    to_left[...] = params[0:64, :]
    to_right[...] = params[cols - 64 : cols, :]


def third_kernel(
    geo, tile, whole, place, weights, own, left, right, target, spec, *rest
):
    tabs = dict(zip(STEP_TABLES, rest))
    spread, intensity_out, params, goal, fields = rest[len(STEP_TABLES) :]
    cols = own.shape[0]
    params[...] = jnp.zeros_like(params)
    params[0:64, :] = left[...]
    params[64 : 64 + cols, :] = own[...]
    params[64 + cols : 128 + cols, :] = right[...]
    goal[...] = jnp.zeros_like(goal)
    goal[0 : target.shape[0], :] = target[...]
    mask = masked(geo, place, tile, whole, params[...], -64)
    inside = field_window(geo, place, tile, whole, -64)
    aim = goal[0 : geo.field_up, :]
    intensity, grad = one_step(geo, mask, aim, inside, weights, spec, tabs, fields)
    spread[...] = grad
    goal[0 : geo.field_up, :] = intensity
    goal[0:256, :] = jnp.concatenate(
        [goal[H : H + cols, :], jnp.zeros((256 - cols, 128), f32)], 0
    )
    intensity_out[...] = goal[0:256, :].T[:64, :cols]


def final_kernel(place, own, across, within, out, wide):
    even = place[0] % 2 == 0
    cols = own.shape[0]
    wide[...] = jnp.zeros_like(wide)
    wide[0:cols, :] = gathered(even, own, across, within)
    out[...] = wide[...].T[H : H + 64, :cols]


def call(kernel, name, out_shapes, scratch, args, scalars):
    args = args[:scalars] + [
        pltpu.with_memory_space_constraint(arg, pltpu.VMEM) for arg in args[scalars:]
    ]
    specs = [pl.BlockSpec(memory_space=pltpu.SMEM)] * scalars
    specs += [pl.BlockSpec(memory_space=pltpu.VMEM)] * (len(args) - scalars)
    return pl.pallas_call(
        kernel,
        name=name,
        out_shape=[
            shape if isinstance(shape, jax.ShapeDtypeStruct) else pltpu.VMEM(shape, f32)
            for shape in out_shapes
        ],
        in_specs=specs,
        out_specs=[pl.BlockSpec(memory_space=pltpu.VMEM)] * len(out_shapes),
        scratch_shapes=[pltpu.VMEM(shape, f32) for shape in scratch],
        compiler_params=pltpu.CompilerParams(vmem_limit_bytes=24 * 1024 * 1024),
    )(*args)


def per_device(rows, cols, mask_params, target_bits, kern_real, kern_imag, socs_weights):
    tile = mask_params.shape
    whole = (tile[0] * rows, tile[1] * cols)
    kernels = kern_real.shape[1] // KS
    near = [(i, i ^ 1) for i in range(rows)]
    far = [(i, i + 1) for i in range(1, rows - 1, 2)]
    far = far + [(b, a) for a, b in far]
    right = [(i, i + 1) for i in range(cols - 1)]
    left = [(b, a) for a, b in right]
    place = jnp.stack([lax.axis_index("row"), lax.axis_index("col")]).astype(jnp.int32)

    def row_exchange(value):
        return lax.ppermute(value, "row", far), lax.ppermute(value, "row", near)

    def col_exchange(to_left, to_right):
        return lax.ppermute(to_right, "col", right), lax.ppermute(to_left, "col", left)

    wide, slim = Geometry(tile[1] + 8 * H), Geometry(tile[1] + 4 * H)
    shared = row_tables()
    wide_tabs, slim_tabs = wide.tables(), slim.tables()

    across, within = row_exchange(mask_params)
    n = tile[1]
    params, target, to_left, to_right = call(
        prep_kernel,
        "prep",
        [(n, 128), (n, 128), (224, 128), (224, 128)],
        [(128, 256)],
        [place, mask_params, across, within, target_bits],
        1,
    )
    from_left, from_right = col_exchange(to_left, to_right)
    names = [(label, name) for label in ("wide", "slim") for name in COLUMN_TABLES]
    names += [("shared", name) for name in ROW_TABLES]
    made = {"wide": wide_tabs, "slim": slim_tabs, "shared": shared}
    tables = [jnp.asarray(made[label][name]) for label, name in names]
    inputs = [
        kern_real,
        kern_imag,
        jnp.asarray(shared["tap_rows"]),
        jnp.asarray(wide_tabs["tap_cols"]),
        jnp.asarray(slim_tabs["tap_cols"]),
    ]
    wide_spec, slim_spec, *held = pl.pallas_call(
        functools.partial(setup_kernel, (wide, slim), len(tables)),
        name="spectra",
        out_shape=[
            pltpu.VMEM((2 * kernels * geo.freqs_up, 256), f32) for geo in (wide, slim)
        ]
        + [pltpu.VMEM(table.shape, table.dtype) for table in tables],
        in_specs=[pl.BlockSpec(memory_space=pltpu.VMEM)] * len(inputs)
        + [pl.BlockSpec(memory_space=pltpu.HBM)] * len(tables),
        out_specs=[pl.BlockSpec(memory_space=pltpu.VMEM)] * (2 + len(tables)),
        scratch_shapes=[
            pltpu.VMEM((kernels * KS, 512), f32),
            pltpu.SemaphoreType.DMA((len(tables),)),
        ],
        compiler_params=pltpu.CompilerParams(vmem_limit_bytes=24 * 1024 * 1024),
    )(*[pltpu.with_memory_space_constraint(arg, pltpu.HBM) for arg in inputs + tables])
    place_of = {key: table for key, table in zip(names, held)}

    def tabs(label):
        return [place_of[label, name] for name in COLUMN_TABLES] + [
            place_of["shared", name] for name in ROW_TABLES
        ]

    def scratch(geo):
        return [(geo.mask_up, 128), (geo.field_up, 128), (kernels, geo.field_up, 128)]

    spread, params, target = call(
        functools.partial(first_kernel, wide, tile, whole),
        "first",
        [(wide.grad, 128), (slim.mask, 128), (slim.field, 128)],
        scratch(wide),
        [place, socs_weights, params, target, from_left, from_right, wide_spec, *tabs("wide")],
        2,
    )
    across, within = row_exchange(spread)
    spread, params = call(
        functools.partial(second_kernel, slim, tile, whole),
        "second",
        [(slim.grad, 128), (n, 128)],
        scratch(slim),
        [place, socs_weights, spread, across, within, params, target, slim_spec, *tabs("slim")],
        2,
    )
    across, within = row_exchange(spread)
    params, to_left, to_right = call(
        update_kernel,
        "update",
        [(n, 128), (64, 128), (64, 128)],
        [],
        [place, spread, across, within, params],
        1,
    )
    from_left, from_right = col_exchange(to_left, to_right)
    third_scratch = scratch(slim)
    third_scratch[1] = (max(256, slim.field_up), 128)
    spread, intensity = call(
        functools.partial(third_kernel, slim, tile, whole),
        "third",
        [(slim.grad, 128), jax.ShapeDtypeStruct(tile, f32)],
        third_scratch,
        [place, socs_weights, params, from_left, from_right, target, slim_spec, *tabs("slim")],
        2,
    )
    across, within = row_exchange(spread)
    (mask_grad,) = call(
        final_kernel,
        "final",
        [jax.ShapeDtypeStruct(tile, f32)],
        [(256, 128)],
        [place, spread, across, within],
        1,
    )
    return mask_grad, intensity


def solution(mesh):
    placed = (P("row", "col"), P("row", "col"), P(), P(), P())
    return jax.shard_map(
        functools.partial(per_device, mesh.shape["row"], mesh.shape["col"]),
        mesh=mesh,
        in_specs=placed,
        out_specs=(P("row", "col"), P("row", "col")),
        check_vma=False,
    )
```

```python
import functools
import math

import jax
import jax.numpy as jnp
import ml_dtypes
import numpy as np
from jax import lax
from jax.experimental import pallas as pl
from jax.experimental.pallas import tpu as pltpu
from jax.sharding import PartitionSpec as P

H = 32
KS = 64
ITERS = 3
ROWS = 128
sharpness = 2.0
steepness = 4.0
threshold = 0.8
step_size = 1.0
f32 = jnp.float32
bf16 = jnp.bfloat16
VMEM_LIMIT = 28 * 1024 * 1024


def up(value, unit):
    return -(-value // unit) * unit


def halves(table):
    table = table.astype(np.float32)
    high = table.astype(ml_dtypes.bfloat16)
    low = (table - high.astype(np.float32)).astype(ml_dtypes.bfloat16)
    return high, low


def angles(left, right, length):
    product = np.outer(left.astype(np.int64), right.astype(np.int64)) % length
    return product * (2.0 * math.pi / length)


def grown(table, rows, cols):
    return np.pad(table, [(0, rows - table.shape[0]), (0, cols - table.shape[1])])


def left_stack(table):
    high, low = halves(table)
    return np.concatenate([high, high, low], 1)


def right_stack(table):
    high, low = halves(table)
    return np.concatenate([high, high, low], 0)


class Geometry:
    def __init__(self, width):
        self.mask = width
        self.field = width - 2 * H
        self.grad = width - 4 * H
        self.length = width | 1
        self.freqs = (self.length + 1) // 2
        self.freqs_up = up(self.freqs, 16)
        self.mask_up = up(self.mask, 16)
        self.half = self.field // 2
        self.half_up = up(self.half, 16)
        self.grad_up = up(self.grad, 32)

    def tables(self):
        freq = np.arange(self.freqs)
        fu, hu = self.freqs_up, self.half_up
        middle = H + (self.field - 1) / 2.0
        weight = np.where(freq == 0, 1.0, 2.0) / (self.length * ROWS)

        def phases(places):
            return angles(freq, np.round(2 * places), 2 * self.length)

        def complex_table(phase, sign, rows, cols, axis):
            parts = [grown(np.cos(phase), rows, cols), grown(sign * np.sin(phase), rows, cols)]
            return np.concatenate(parts, axis)

        mask = phases(np.arange(self.mask) - middle)
        half = phases(np.arange(self.half) + 0.5)
        grad = phases(np.arange(self.grad) + 2 * H - middle)
        taps = phases(np.arange(KS) - H)
        grad_table = np.concatenate(
            [
                grown((np.cos(grad) * weight[:, None]).T, self.grad_up, fu),
                grown((-np.sin(grad) * weight[:, None]).T, self.grad_up, fu),
            ],
            1,
        )
        return dict(
            mask_cols=left_stack(complex_table(mask, -1.0, fu, self.mask_up, 0)),
            field_even=left_stack(grown((np.cos(half) * weight[:, None]).T, hu, fu)),
            field_odd=left_stack(grown((np.sin(half) * weight[:, None]).T, hu, fu)),
            source_even=left_stack(grown(np.cos(half), fu, hu)),
            source_odd=left_stack(grown(-np.sin(half), fu, hu)),
            grad_cols=left_stack(grad_table),
            tap_cols=left_stack(complex_table(taps, 1.0, fu, KS, 1)),
        )


def row_tables():
    freq = np.arange(ROWS)

    def complex_table(phase, sign):
        cos, sin = np.cos(phase), sign * np.sin(phase)
        return np.block([[cos, sin], [-sin, cos]])

    def side(table):
        high, low = halves(table)
        return np.concatenate([high, low], 1)

    places = np.arange(64) + H
    field = complex_table(angles(freq, places, ROWS), 1.0)
    field_swapped = np.concatenate([field[:, 64:], field[:, :64]], 1)
    source = complex_table(angles(np.arange(64), freq, ROWS), -1.0)
    source_swapped = np.concatenate([source[64:], source[:64]], 0)
    taps = angles(np.arange(KS) - H, freq, ROWS)
    tap = np.concatenate([np.cos(taps), -np.sin(taps)], 1)
    zero = np.zeros_like(tap)
    return dict(
        mask_rows=right_stack(complex_table(angles(freq, freq, ROWS), -1.0)),
        field_rows=side(field),
        field_rows_swapped=side(field_swapped),
        source_rows=right_stack(source),
        source_rows_swapped=right_stack(source_swapped),
        grad_rows=right_stack(complex_table(angles(freq, freq - H, ROWS), 1.0)),
        tap_rows=right_stack(np.block([[tap, zero], [zero, tap]])),
    )


def split(value):
    high = value.astype(bf16)
    return high, (value - high.astype(f32)).astype(bf16)


def dot(left, right):
    return lax.dot_general(
        left, right, (((1,), (0,)), ((), ())), preferred_element_type=f32
    )


def left_dot(table, value):
    high, low = split(value)
    return dot(table, jnp.concatenate([high, low, high], 0))


def right_dot(value, table):
    high, low = split(value)
    return dot(jnp.concatenate([high, low, high], 1), table)


def sigmoid(value):
    return 1.0 / (1.0 + jnp.exp(-value))


def swap_halves(value):
    return pltpu.roll(value, 64, 1)


def window(shape, first_col, first_row, whole_cols, whole_rows):
    col = lax.broadcasted_iota(jnp.int32, shape, 0) + first_col
    row = lax.broadcasted_iota(jnp.int32, shape, 1) + first_row
    return (col >= 0) & (col < whole_cols) & (row >= 0) & (row < whole_rows)


def setup_kernel(geos, held, kern_real, kern_imag, tap_rows, *rest):
    tables, rest = rest[: len(geos)], rest[len(geos) :]
    sources, rest = rest[:held], rest[held:]
    outs, rest = rest[: len(geos)], rest[len(geos) :]
    targets, (scratch, sems) = rest[:held], rest[held:]
    copies = [
        pltpu.make_async_copy(source, target, sems.at[index])
        for index, (source, target) in enumerate(zip(sources, targets))
    ]
    for copy in copies:
        copy.start()
    kernels = kern_real.shape[1] // KS
    both = jnp.concatenate([kern_real[...], kern_imag[...]], 0)
    for start in range(0, both.shape[1], 128):
        part = both[:, start : start + 128].T
        scratch[start : start + 128, :] = right_dot(part, tap_rows[...])
    for k in range(kernels):
        half = scratch[k * KS : (k + 1) * KS, :]
        turned = jnp.concatenate(
            [half[:, 128:256], -half[:, 0:128], half[:, 384:512], -half[:, 256:384]], 1
        )
        high, low = split(jnp.concatenate([half, turned], 0))
        stacked = jnp.concatenate([high, low, high], 0)
        for geo, table, out in zip(geos, tables, outs):
            spec = dot(table[...], stacked)
            count = geo.freqs_up
            out[2 * k * count : (2 * k + 1) * count, :] = spec[:, :256]
            out[(2 * k + 1) * count : (2 * k + 2) * count, :] = spec[:, 256:]
    for copy in copies:
        copy.wait()


def one_step(geo, mask, target, inside, weights, spec, tabs, fields):
    count = geo.freqs_up
    group = weights.shape[0]
    kernels = weights.shape[0]
    lane = lax.broadcasted_iota(jnp.int32, (count, 128), 1) < 64
    across = left_dot(tabs["mask_cols"][...], mask)
    mask_spec = right_dot(
        jnp.concatenate([across[:count], across[count:]], 1), tabs["mask_rows"][...]
    )
    mask_re, mask_im = mask_spec[:, :128], mask_spec[:, 128:]

    def product(index):
        place = spec[index * count : (index + 1) * count, :]
        re, im = place[:, :128], place[:, 128:]
        return jnp.concatenate(
            [re * mask_re - im * mask_im, re * mask_im + im * mask_re], 1
        )

    def down(indices, table):
        high, low = split(jnp.concatenate([product(i) for i in indices], 0))
        wide = dot(high, table[...])
        got = wide[:, :128] + wide[:, 128:] + dot(low, table[:, :128])
        return [got[i * count : (i + 1) * count] for i in range(len(indices))]

    zero = jnp.zeros((geo.half_up, 128), f32)
    intensity = [zero, zero]
    for k in range(0, kernels, group):
        ks = range(k, k + group)
        firsts = down([2 * j for j in ks], tabs["field_rows"])
        seconds = down([2 * j + 1 for j in ks], tabs["field_rows_swapped"])
        evens = [jnp.where(lane, a, b) for a, b in zip(firsts, seconds)]
        odds = [swap_halves(jnp.where(lane, b, a)) for a, b in zip(firsts, seconds)]
        even = left_dot(tabs["field_even"][...], jnp.concatenate(evens, 1))
        odd = left_dot(tabs["field_odd"][...], jnp.concatenate(odds, 1))
        for side, field in enumerate((even - odd, even + odd)):
            for j in range(group):
                own = field[:, j * 128 : (j + 1) * 128]
                fields[side, k + j] = own
                intensity[side] = intensity[side] + weights[k + j] * (own * own)
    cotangent = []
    for side in (0, 1):
        intensity[side] = intensity[side] + swap_halves(intensity[side])
        resist = sigmoid(steepness * (intensity[side] - threshold))
        slope = 2.0 * (resist - target[side]) * steepness * resist * (1.0 - resist)
        cotangent.append(jnp.where(inside[side], slope, 0.0))
    total_re = jnp.zeros((count, 128), f32)
    total_im = jnp.zeros((count, 128), f32)
    for k in range(0, kernels, group):
        ks = range(k, k + group)
        right, left = (
            jnp.concatenate(
                [(2.0 * weights[j] * cotangent[side]) * fields[side, j] for j in ks],
                1,
            )
            for side in (0, 1)
        )
        even = left_dot(tabs["source_even"][...], right + left)
        odd = left_dot(tabs["source_odd"][...], right - left)
        res = [even[:, j * 128 : (j + 1) * 128] for j in range(group)]
        ims = [swap_halves(odd[:, j * 128 : (j + 1) * 128]) for j in range(group)]
        for index, values, table in (
            (0, [jnp.where(lane, a, b) for a, b in zip(res, ims)], tabs["source_rows"]),
            (1, [jnp.where(lane, b, a) for a, b in zip(res, ims)], tabs["source_rows_swapped"]),
        ):
            got = right_dot(jnp.concatenate(values, 0), table[...])
            for j in range(group):
                got_re, got_im = (
                    got[j * count : (j + 1) * count, :128],
                    got[j * count : (j + 1) * count, 128:],
                )
                start = (2 * (k + j) + index) * count
                place = spec[start : start + count, :]
                re_k, im_k = place[:, :128], place[:, 128:]
                total_re = total_re + (re_k * got_re + im_k * got_im)
                total_im = total_im + (re_k * got_im - im_k * got_re)
    back = right_dot(jnp.concatenate([total_re, total_im], 1), tabs["grad_rows"][...])
    grad = left_dot(
        tabs["grad_cols"][...], jnp.concatenate([back[:, :128], back[:, 128:]], 0)
    )
    return intensity, grad


COLUMN_TABLES = (
    "mask_cols",
    "field_even",
    "field_odd",
    "source_even",
    "source_odd",
    "grad_cols",
)
ROW_TABLES = (
    "mask_rows",
    "field_rows",
    "field_rows_swapped",
    "source_rows",
    "source_rows_swapped",
    "grad_rows",
)
STEP_TABLES = COLUMN_TABLES + ROW_TABLES


def lanes(shape):
    return lax.broadcasted_iota(jnp.int32, shape, 1) < 64


def early_kernel(own, bits, params, target, tall):
    cols = own.shape[1]
    tall[...] = jnp.zeros_like(tall)
    tall[32:96, :cols] = own[...]
    params[...] = tall[...].T[:cols]
    col = lax.broadcasted_iota(jnp.int32, (64, tall.shape[1]), 1)
    word = jnp.zeros_like(col)
    for index in range(bits.shape[1]):
        word = jnp.where(col // 30 == index, bits[:, index : index + 1], word)
    bit = jnp.bitwise_and(jnp.right_shift(word, col % 30), 1).astype(f32)
    target[...] = jnp.concatenate([bit, bit], 0).T[:cols]


def prep_kernel(place, own, target, across, within, params, to_first, to_second, tall):
    even = place[0] % 2 == 0
    cols = own.shape[0]
    tall[...] = jnp.zeros_like(tall)
    tall[0:32, :cols] = jnp.where(even, across[32:64, :], within[32:64, :])
    tall[96:128, :cols] = jnp.where(even, within[0:32, :], across[0:32, :])
    params[...] = own[...] + tall[...].T[:cols]
    right = place[1] % 2 == 0
    left_lanes = lanes((48, 128))

    def packed(start):
        return jnp.where(left_lanes, target[start : start + 48], target[start + 48 : start + 96])

    to_left = jnp.concatenate([params[0:128, :], packed(0)], 0)
    to_right = jnp.concatenate([params[cols - 128 : cols, :], packed(cols - 96)], 0)
    to_first[...] = jnp.where(right, to_right, to_left)
    to_second[...] = jnp.where(right, to_left, to_right)


def spread_out(place, grad, spread, to_far, to_near):
    even = place[0] % 2 == 0
    half = to_far.shape[0]
    spread[...] = grad
    turned = swap_halves(grad)
    straight = jnp.where(even, grad, turned)
    crossed = jnp.where(even, turned, grad)
    left_lanes = lanes((half, 128))
    to_far[...] = jnp.where(left_lanes, straight[:half], crossed[half:])
    to_near[...] = jnp.where(left_lanes, crossed[:half], straight[half:])


def gathered(place, spread, far, near):
    even = place[0] % 2 == 0
    far, near = far[...], near[...]
    left_lanes = lanes(far.shape)
    far_turned, near_turned = swap_halves(far), swap_halves(near)
    straight = jnp.concatenate(
        [jnp.where(left_lanes, far, near_turned), jnp.where(left_lanes, far_turned, near)], 0
    )
    crossed = jnp.concatenate(
        [jnp.where(left_lanes, near, far_turned), jnp.where(left_lanes, near_turned, far)], 0
    )
    return spread[...] + jnp.where(even, straight, crossed)


def stepped(params, grad):
    field = sigmoid(sharpness * params)
    return params - step_size * sharpness * field * (1.0 - field) * grad


def masked(place, tile, whole, params, col_offset):
    first_col = place[1] * tile[1] + col_offset
    first_row = place[0] * tile[0] - H
    inside = window(params.shape, first_col, first_row, whole[1], whole[0])
    return jnp.where(inside, sigmoid(sharpness * params), 0.0)


def field_window(geo, place, tile, whole, col_offset):
    middle = place[1] * tile[1] + col_offset + H + geo.half
    step = lax.broadcasted_iota(jnp.int32, (geo.half_up, 128), 0)
    return [(col >= 0) & (col < whole[1]) for col in (middle + step, middle - 1 - step)]


def first_kernel(
    geo, tile, whole, place, weights, own, target, first, second, spec, mirror, *rest
):
    tabs = dict(zip(STEP_TABLES, rest))
    rest = rest[len(STEP_TABLES) :]
    spread, to_far, to_near, params_out, goal_out, params, goal, fields = rest
    cols = own.shape[0]
    right_first = place[1] % 2 == 0
    left = jnp.where(right_first, second[...], first[...])
    right = jnp.where(right_first, first[...], second[...])
    params[...] = jnp.zeros_like(params)
    params[0:128, :] = left[0:128, :]
    params[128 : 128 + cols, :] = own[...]
    params[128 + cols : 256 + cols, :] = right[0:128, :]
    left_lanes = lanes((48, 128))
    goal[...] = jnp.zeros_like(goal)
    for start, side in ((0, left), (96 + cols, right)):
        packed = side[128:176, :]
        turned = swap_halves(packed)
        goal[start : start + 48, :] = jnp.where(left_lanes, packed, turned)
        goal[start + 48 : start + 96, :] = jnp.where(left_lanes, turned, packed)
    goal[96 : 96 + cols, :] = target[...]
    goals = [
        goal[geo.half : geo.half + geo.half_up, :],
        dot(mirror[...], goal[0 : mirror.shape[1], :].astype(bf16)),
    ]
    for side in (0, 1):
        goal_out[side] = goals[side][: goal_out.shape[1]]
    params_out[...] = params[64 : 64 + params_out.shape[0], :]
    mask = masked(place, tile, whole, params[...], -128)
    inside = field_window(geo, place, tile, whole, -128)
    _, grad = one_step(geo, mask, goals, inside, weights, spec, tabs, fields)
    spread_out(place, grad, spread, to_far, to_near)


def second_kernel(geo, tile, whole, place, weights, own, far, near, old, goal, spec, *rest):
    tabs = dict(zip(STEP_TABLES, rest))
    spread, to_far, to_near, params_out, fields = rest[len(STEP_TABLES) :]
    params = stepped(old[...], gathered(place, own, far, near))
    params_out[...] = params[64 : 64 + params_out.shape[0], :]
    mask = masked(place, tile, whole, params, -64)
    inside = field_window(geo, place, tile, whole, -64)
    goals = [goal[0], goal[1]]
    _, grad = one_step(geo, mask, goals, inside, weights, spec, tabs, fields)
    spread_out(place, grad, spread, to_far, to_near)


def update_kernel(cols, place, own, far, near, old, params, to_first, to_second):
    params[...] = stepped(old[...], gathered(place, own, far, near))
    right = place[1] % 2 == 0
    to_left, to_right = params[0:64, :], params[cols - 64 : cols, :]
    to_first[...] = jnp.where(right, to_right, to_left)
    to_second[...] = jnp.where(right, to_left, to_right)


def third_kernel(
    geo, tile, whole, place, weights, own, first, second, goal, spec, mirror, *rest
):
    tabs = dict(zip(STEP_TABLES, rest))
    rest = rest[len(STEP_TABLES) :]
    spread, to_far, to_near, intensity_out, params, flat, fields = rest
    cols = tile[1]
    right_first = place[1] % 2 == 0
    params[...] = jnp.zeros_like(params)
    params[0:64, :] = jnp.where(right_first, second[...], first[...])
    params[64 : 64 + cols, :] = own[0:cols, :]
    params[64 + cols : 128 + cols, :] = jnp.where(right_first, first[...], second[...])
    mask = masked(place, tile, whole, params[...], -64)
    inside = field_window(geo, place, tile, whole, -64)
    goals = [goal[0], goal[1]]
    intensity, grad = one_step(geo, mask, goals, inside, weights, spec, tabs, fields)
    spread_out(place, grad, spread, to_far, to_near)
    high, low = split(intensity[1])
    rest = (intensity[1] - high.astype(f32) - low.astype(f32)).astype(bf16)
    turned = dot(mirror[...], high) + (dot(mirror[...], low) + dot(mirror[...], rest))
    flat[...] = jnp.zeros_like(flat)
    flat[0 : cols // 2, :] = turned[0 : cols // 2]
    flat[cols // 2 : cols, :] = intensity[0][0 : cols // 2]
    intensity_out[...] = flat[...].T[:64, :cols]


def final_kernel(cols, place, own, far, near, out, wide):
    wide[...] = jnp.zeros_like(wide)
    wide[0 : own.shape[0], :] = gathered(place, own, far, near)
    out[...] = wide[...].T[H : H + 64, :cols]


def mirror_table(rows, rows_up, cols_up):
    table = np.zeros((rows_up, cols_up), np.float32)
    table[np.arange(rows), rows - 1 - np.arange(rows)] = 1.0
    return table.astype(ml_dtypes.bfloat16)


def call(kernel, name, out_shapes, scratch, args, scalars):
    args = args[:scalars] + [
        pltpu.with_memory_space_constraint(arg, pltpu.VMEM) for arg in args[scalars:]
    ]
    specs = [pl.BlockSpec(memory_space=pltpu.SMEM)] * scalars
    specs += [pl.BlockSpec(memory_space=pltpu.VMEM)] * (len(args) - scalars)
    return pl.pallas_call(
        kernel,
        name=name,
        out_shape=[
            shape if isinstance(shape, jax.ShapeDtypeStruct) else pltpu.VMEM(shape, f32)
            for shape in out_shapes
        ],
        in_specs=specs,
        out_specs=[pl.BlockSpec(memory_space=pltpu.VMEM)] * len(out_shapes),
        scratch_shapes=[pltpu.VMEM(shape, f32) for shape in scratch],
        compiler_params=pltpu.CompilerParams(vmem_limit_bytes=VMEM_LIMIT),
    )(*args)


def per_device(rows, cols, mask_params, target_bits, kern_real, kern_imag, socs_weights):
    tile = mask_params.shape
    whole = (tile[0] * rows, tile[1] * cols)
    kernels = kern_real.shape[1] // KS
    place = jnp.stack([lax.axis_index("row"), lax.axis_index("col")]).astype(jnp.int32)

    def swaps(count, start):
        pairs = [(i, i + 1) for i in range(start, count - 1, 2)]
        return pairs + [(b, a) for a, b in pairs]

    def row_exchange(to_far, to_near):
        far = lax.ppermute(to_far, "row", swaps(rows, 1))
        return far, lax.ppermute(to_near, "row", swaps(rows, 0))

    def col_exchange(to_first, to_second):
        first = lax.ppermute(to_first, "col", swaps(cols, 0))
        return first, lax.ppermute(to_second, "col", swaps(cols, 1))

    wide, slim = Geometry(tile[1] + 8 * H), Geometry(tile[1] + 4 * H)
    shared = row_tables()
    shared["wide_mirror"] = mirror_table(wide.half, wide.half_up, wide.half_up)
    shared["slim_mirror"] = mirror_table(tile[1] // 2, up(tile[1] // 2, 16), slim.half_up)
    made = {"wide": wide.tables(), "slim": slim.tables(), "shared": shared}
    n = tile[1]
    far, near = row_exchange(mask_params, mask_params)
    params, target = call(
        early_kernel,
        "early",
        [(n, 128), (n, 128)],
        [(128, 256)],
        [mask_params, target_bits],
        0,
    )
    params, to_first, to_second = call(
        prep_kernel,
        "prep",
        [(n, 128), (176, 128), (176, 128)],
        [(128, 256)],
        [place, params, target, far, near],
        1,
    )
    first, second = col_exchange(to_first, to_second)
    names = [(label, name) for label in ("wide", "slim") for name in COLUMN_TABLES]
    names += [("shared", name) for name in ROW_TABLES + ("wide_mirror", "slim_mirror")]
    tables = [jnp.asarray(made[label][name]) for label, name in names]
    inputs = [
        kern_real,
        kern_imag,
        jnp.asarray(shared["tap_rows"]),
        jnp.asarray(made["wide"]["tap_cols"]),
        jnp.asarray(made["slim"]["tap_cols"]),
    ]
    wide_spec, slim_spec, *held = pl.pallas_call(
        functools.partial(setup_kernel, (wide, slim), len(tables)),
        name="spectra",
        out_shape=[
            pltpu.VMEM((2 * kernels * geo.freqs_up, 256), f32) for geo in (wide, slim)
        ]
        + [pltpu.VMEM(table.shape, table.dtype) for table in tables],
        in_specs=[pl.BlockSpec(memory_space=pltpu.VMEM)] * len(inputs)
        + [pl.BlockSpec(memory_space=pltpu.HBM)] * len(tables),
        out_specs=[pl.BlockSpec(memory_space=pltpu.VMEM)] * (2 + len(tables)),
        scratch_shapes=[
            pltpu.VMEM((kernels * KS, 512), f32),
            pltpu.SemaphoreType.DMA((len(tables),)),
        ],
        compiler_params=pltpu.CompilerParams(vmem_limit_bytes=VMEM_LIMIT),
    )(*[pltpu.with_memory_space_constraint(arg, pltpu.HBM) for arg in inputs + tables])
    place_of = {key: table for key, table in zip(names, held)}

    def tabs(label):
        return [place_of[label, name] for name in COLUMN_TABLES] + [
            place_of["shared", name] for name in ROW_TABLES
        ]

    def spreads(geo):
        return [(geo.grad_up, 128)] + [(geo.grad_up // 2, 128)] * 2

    def fields(geo):
        return (2, kernels, geo.half_up, 128)

    spread, to_far, to_near, params, goal = call(
        functools.partial(first_kernel, wide, tile, whole),
        "first",
        spreads(wide) + [(slim.mask_up, 128), (2, slim.half_up, 128)],
        [(wide.mask_up, 128), (wide.half + wide.half_up, 128), fields(wide)],
        [place, socs_weights, params, target, first, second, wide_spec]
        + [place_of["shared", "wide_mirror"], *tabs("wide")],
        2,
    )
    far, near = row_exchange(to_far, to_near)
    spread, to_far, to_near, params = call(
        functools.partial(second_kernel, slim, tile, whole),
        "second",
        spreads(slim) + [(slim.grad_up, 128)],
        [fields(slim)],
        [place, socs_weights, spread, far, near, params, goal, slim_spec, *tabs("slim")],
        2,
    )
    far, near = row_exchange(to_far, to_near)
    params, to_first, to_second = call(
        functools.partial(update_kernel, n),
        "update",
        [(slim.grad_up, 128), (64, 128), (64, 128)],
        [],
        [place, spread, far, near, params],
        1,
    )
    first, second = col_exchange(to_first, to_second)
    spread, to_far, to_near, intensity = call(
        functools.partial(third_kernel, slim, tile, whole),
        "third",
        spreads(slim) + [jax.ShapeDtypeStruct(tile, f32)],
        [(slim.mask_up, 128), (256, 128), fields(slim)],
        [place, socs_weights, params, first, second, goal, slim_spec]
        + [place_of["shared", "slim_mirror"], *tabs("slim")],
        2,
    )
    far, near = row_exchange(to_far, to_near)
    (mask_grad,) = call(
        functools.partial(final_kernel, n),
        "final",
        [jax.ShapeDtypeStruct(tile, f32)],
        [(256, 128)],
        [place, spread, far, near],
        1,
    )
    return mask_grad, intensity


def solution(mesh):
    placed = (P("row", "col"), P("row", "col"), P(), P(), P())
    return jax.shard_map(
        functools.partial(per_device, mesh.shape["row"], mesh.shape["col"]),
        mesh=mesh,
        in_specs=placed,
        out_specs=(P("row", "col"), P("row", "col")),
        check_vma=False,
    )
```

```python
import functools
import math

import jax
import jax.numpy as jnp
import ml_dtypes
import numpy as np
from jax import lax
from jax.experimental import pallas as pl
from jax.experimental.pallas import tpu as pltpu
from jax.sharding import PartitionSpec as P

H = 32
KS = 64
ITERS = 3
ROWS = 128
sharpness = 2.0
steepness = 4.0
threshold = 0.8
step_size = 1.0
f32 = jnp.float32
bf16 = jnp.bfloat16
VMEM_LIMIT = 28 * 1024 * 1024


def up(value, unit):
    return -(-value // unit) * unit


def halves(table):
    table = table.astype(np.float32)
    high = table.astype(ml_dtypes.bfloat16)
    low = (table - high.astype(np.float32)).astype(ml_dtypes.bfloat16)
    return high, low


def angles(left, right, length):
    product = np.outer(left.astype(np.int64), right.astype(np.int64)) % length
    return product * (2.0 * math.pi / length)


def grown(table, rows, cols):
    return np.pad(table, [(0, rows - table.shape[0]), (0, cols - table.shape[1])])


def left_stack(table):
    high, low = halves(table)
    return np.concatenate([high, high, low], 1)


def right_stack(table):
    high, low = halves(table)
    return np.concatenate([high, high, low], 0)


class Geometry:
    def __init__(self, width):
        self.mask = width
        self.field = width - 2 * H
        self.grad = width - 4 * H
        self.length = width | 1
        self.freqs = (self.length + 1) // 2
        self.freqs_up = up(self.freqs, 16)
        self.mask_up = up(self.mask, 16)
        self.half = self.field // 2
        self.half_up = up(self.half, 16)
        self.grad_up = up(self.grad, 32)

    def tables(self):
        freq = np.arange(self.freqs)
        fu, hu = self.freqs_up, self.half_up
        middle = H + (self.field - 1) / 2.0
        weight = np.where(freq == 0, 1.0, 2.0) / (self.length * ROWS)

        def phases(places):
            return angles(freq, np.round(2 * places), 2 * self.length)

        def complex_table(phase, sign, rows, cols, axis):
            parts = [grown(np.cos(phase), rows, cols), grown(sign * np.sin(phase), rows, cols)]
            return np.concatenate(parts, axis)

        mask = phases(np.arange(self.mask) - middle)
        half = phases(np.arange(self.half) + 0.5)
        grad = phases(np.arange(self.grad) + 2 * H - middle)
        taps = phases(np.arange(KS) - H)
        grad_table = np.concatenate(
            [
                grown((np.cos(grad) * weight[:, None]).T, self.grad_up, fu),
                grown((-np.sin(grad) * weight[:, None]).T, self.grad_up, fu),
            ],
            1,
        )
        return dict(
            mask_cols=left_stack(complex_table(mask, -1.0, fu, self.mask_up, 0)),
            field_even=left_stack(grown((np.cos(half) * weight[:, None]).T, hu, fu)),
            field_odd=left_stack(grown((np.sin(half) * weight[:, None]).T, hu, fu)),
            source_even=left_stack(grown(np.cos(half), fu, hu)),
            source_odd=left_stack(grown(-np.sin(half), fu, hu)),
            grad_cols=left_stack(grad_table),
            tap_cols=left_stack(complex_table(taps, 1.0, fu, KS, 1)),
        )


def row_tables():
    freq = np.arange(ROWS)

    def complex_table(phase, sign):
        cos, sin = np.cos(phase), sign * np.sin(phase)
        return np.block([[cos, sin], [-sin, cos]])

    def side(table):
        high, low = halves(table)
        return np.concatenate([high, low], 1)

    places = np.arange(64) + H
    field = complex_table(angles(freq, places, ROWS), 1.0)
    field_swapped = np.concatenate([field[:, 64:], field[:, :64]], 1)
    source = complex_table(angles(np.arange(64), freq, ROWS), -1.0)
    source_swapped = np.concatenate([source[64:], source[:64]], 0)
    taps = angles(np.arange(KS) - H, freq, ROWS)
    tap = np.concatenate([np.cos(taps), -np.sin(taps)], 1)
    zero = np.zeros_like(tap)
    return dict(
        mask_rows=right_stack(complex_table(angles(freq, freq, ROWS), -1.0)),
        field_rows=side(field),
        field_rows_swapped=side(field_swapped),
        source_rows=right_stack(source),
        source_rows_swapped=right_stack(source_swapped),
        grad_rows=right_stack(complex_table(angles(freq, freq - H, ROWS), 1.0)),
        tap_rows=right_stack(np.block([[tap, zero], [zero, tap]])),
    )


def split(value):
    high = value.astype(bf16)
    return high, (value - high.astype(f32)).astype(bf16)


def dot(left, right):
    return lax.dot_general(
        left, right, (((1,), (0,)), ((), ())), preferred_element_type=f32
    )


def left_dot(table, value):
    high, low = split(value)
    return dot(table, jnp.concatenate([high, low, high], 0))


def right_dot(value, table):
    high, low = split(value)
    return dot(jnp.concatenate([high, low, high], 1), table)


def sigmoid(value):
    return 1.0 / (1.0 + jnp.exp(-value))


def swap_halves(value):
    return pltpu.roll(value, 64, 1)


def is_even(place, axis, shape):
    return jnp.broadcast_to(place[axis : axis + 1, : shape[1]], shape) % 2 == 0


def window(shape, first_col, first_row, whole_cols, whole_rows):
    col = lax.broadcasted_iota(jnp.int32, shape, 0) + first_col
    row = lax.broadcasted_iota(jnp.int32, shape, 1) + first_row
    return (col >= 0) & (col < whole_cols) & (row >= 0) & (row < whole_rows)


def column_spectra(geo, half, table, out):
    count = geo.freqs_up
    for k in range(out.shape[0] // (2 * count)):
        part = half[k * KS : (k + 1) * KS, :]
        turned = jnp.concatenate(
            [part[:, 128:256], -part[:, 0:128], part[:, 384:512], -part[:, 256:384]], 1
        )
        spec = left_dot(table[...], jnp.concatenate([part, turned], 0))
        out[2 * k * count : (2 * k + 1) * count, :] = spec[:, :256]
        out[(2 * k + 1) * count : (2 * k + 2) * count, :] = spec[:, 256:]


def setup_kernel(geo, held, kern_real, kern_imag, tap_rows, tap_cols, *rest):
    sources, (out, half), rest = rest[:held], rest[held : held + 2], rest[held + 2 :]
    targets, sems = rest[:held], rest[held]
    copies = [
        pltpu.make_async_copy(source, target, sems.at[index])
        for index, (source, target) in enumerate(zip(sources, targets))
    ]
    for copy in copies:
        copy.start()
    both = jnp.concatenate([kern_real[...], kern_imag[...]], 0)
    for start in range(0, both.shape[1], 128):
        part = both[:, start : start + 128].T
        half[start : start + 128, :] = right_dot(part, tap_rows[...])
    column_spectra(geo, half, tap_cols, out)
    for copy in copies:
        copy.wait()


def slim_kernel(geo, half, tap_cols, out):
    column_spectra(geo, half, tap_cols, out)


def one_step(geo, mask, target, inside, weights, spec, tabs, fields):
    count = geo.freqs_up
    group = kernels = fields.shape[1]
    lane = lax.broadcasted_iota(jnp.int32, (count, 128), 1) < 64
    across = left_dot(tabs["mask_cols"][...], mask)
    mask_spec = right_dot(
        jnp.concatenate([across[:count], across[count:]], 1), tabs["mask_rows"][...]
    )
    mask_re, mask_im = mask_spec[:, :128], mask_spec[:, 128:]

    def product(index):
        place = spec[index * count : (index + 1) * count, :]
        re, im = place[:, :128], place[:, 128:]
        return jnp.concatenate(
            [re * mask_re - im * mask_im, re * mask_im + im * mask_re], 1
        )

    def down(indices, table):
        high, low = split(jnp.concatenate([product(i) for i in indices], 0))
        wide = dot(high, table[...])
        got = wide[:, :128] + wide[:, 128:] + dot(low, table[:, :128])
        return [got[i * count : (i + 1) * count] for i in range(len(indices))]

    zero = jnp.zeros((geo.half_up, 128), f32)
    intensity = [zero, zero]
    for k in range(0, kernels, group):
        ks = range(k, k + group)
        firsts = down([2 * j for j in ks], tabs["field_rows"])
        seconds = down([2 * j + 1 for j in ks], tabs["field_rows_swapped"])
        evens = [jnp.where(lane, a, b) for a, b in zip(firsts, seconds)]
        odds = [swap_halves(jnp.where(lane, b, a)) for a, b in zip(firsts, seconds)]
        even = left_dot(tabs["field_even"][...], jnp.concatenate(evens, 1))
        odd = left_dot(tabs["field_odd"][...], jnp.concatenate(odds, 1))
        for side, field in enumerate((even - odd, even + odd)):
            for j in range(group):
                own = field[:, j * 128 : (j + 1) * 128]
                fields[side, k + j] = own
                intensity[side] = intensity[side] + weights[k + j : k + j + 1, :] * (own * own)
    cotangent = []
    for side in (0, 1):
        intensity[side] = intensity[side] + swap_halves(intensity[side])
        resist = sigmoid(steepness * (intensity[side] - threshold))
        slope = 2.0 * (resist - target[side]) * steepness * resist * (1.0 - resist)
        cotangent.append(jnp.where(inside[side], slope, 0.0))
    total_re = jnp.zeros((count, 128), f32)
    total_im = jnp.zeros((count, 128), f32)
    for k in range(0, kernels, group):
        ks = range(k, k + group)
        right, left = (
            jnp.concatenate(
                [
                    (2.0 * weights[j : j + 1, :] * cotangent[side]) * fields[side, j]
                    for j in ks
                ],
                1,
            )
            for side in (0, 1)
        )
        even = left_dot(tabs["source_even"][...], right + left)
        odd = left_dot(tabs["source_odd"][...], right - left)
        res = [even[:, j * 128 : (j + 1) * 128] for j in range(group)]
        ims = [swap_halves(odd[:, j * 128 : (j + 1) * 128]) for j in range(group)]
        for index, values, table in (
            (0, [jnp.where(lane, a, b) for a, b in zip(res, ims)], tabs["source_rows"]),
            (1, [jnp.where(lane, b, a) for a, b in zip(res, ims)], tabs["source_rows_swapped"]),
        ):
            got = right_dot(jnp.concatenate(values, 0), table[...])
            for j in range(group):
                got_re, got_im = (
                    got[j * count : (j + 1) * count, :128],
                    got[j * count : (j + 1) * count, 128:],
                )
                start = (2 * (k + j) + index) * count
                place = spec[start : start + count, :]
                re_k, im_k = place[:, :128], place[:, 128:]
                total_re = total_re + (re_k * got_re + im_k * got_im)
                total_im = total_im + (re_k * got_im - im_k * got_re)
    back = right_dot(jnp.concatenate([total_re, total_im], 1), tabs["grad_rows"][...])
    grad = left_dot(
        tabs["grad_cols"][...], jnp.concatenate([back[:, :128], back[:, 128:]], 0)
    )
    return intensity, grad


COLUMN_TABLES = (
    "mask_cols",
    "field_even",
    "field_odd",
    "source_even",
    "source_odd",
    "grad_cols",
)
ROW_TABLES = (
    "mask_rows",
    "field_rows",
    "field_rows_swapped",
    "source_rows",
    "source_rows_swapped",
    "grad_rows",
)
STEP_TABLES = COLUMN_TABLES + ROW_TABLES


def lanes(shape):
    return lax.broadcasted_iota(jnp.int32, shape, 1) < 64


def early_kernel(own, bits, params, target, tall):
    cols = own.shape[1]
    tall[...] = jnp.zeros_like(tall)
    tall[32:96, :cols] = own[...]
    params[...] = tall[...].T[:cols]
    col = lax.broadcasted_iota(jnp.int32, (64, tall.shape[1]), 1)
    word = jnp.zeros_like(col)
    for index in range(bits.shape[1]):
        word = jnp.where(col // 30 == index, bits[:, index : index + 1], word)
    bit = jnp.bitwise_and(jnp.right_shift(word, col % 30), 1).astype(f32)
    target[...] = jnp.concatenate([bit, bit], 0).T[:cols]


def prep_kernel(place, own, target, across, within, params, to_first, to_second, tall):
    even = is_even(place, 0, (32, own.shape[0]))
    cols = own.shape[0]
    tall[...] = jnp.zeros_like(tall)
    tall[0:32, :cols] = jnp.where(even, across[32:64, :], within[32:64, :])
    tall[96:128, :cols] = jnp.where(even, within[0:32, :], across[0:32, :])
    params[...] = own[...] + tall[...].T[:cols]
    right = is_even(place, 1, (176, 128))
    left_lanes = lanes((48, 128))

    def packed(start):
        return jnp.where(left_lanes, target[start : start + 48], target[start + 48 : start + 96])

    to_left = jnp.concatenate([params[0:128, :], packed(0)], 0)
    to_right = jnp.concatenate([params[cols - 128 : cols, :], packed(cols - 96)], 0)
    to_first[...] = jnp.where(right, to_right, to_left)
    to_second[...] = jnp.where(right, to_left, to_right)


def spread_out(place, grad, spread, to_far, to_near):
    even = is_even(place, 0, grad.shape)
    half = to_far.shape[0]
    spread[...] = grad
    turned = swap_halves(grad)
    straight = jnp.where(even, grad, turned)
    crossed = jnp.where(even, turned, grad)
    left_lanes = lanes((half, 128))
    to_far[...] = jnp.where(left_lanes, straight[:half], crossed[half:])
    to_near[...] = jnp.where(left_lanes, crossed[:half], straight[half:])


def gathered(place, spread, far, near):
    even = is_even(place, 0, spread.shape)
    far, near = far[...], near[...]
    left_lanes = lanes(far.shape)
    far_turned, near_turned = swap_halves(far), swap_halves(near)
    straight = jnp.concatenate(
        [jnp.where(left_lanes, far, near_turned), jnp.where(left_lanes, far_turned, near)], 0
    )
    crossed = jnp.concatenate(
        [jnp.where(left_lanes, near, far_turned), jnp.where(left_lanes, near_turned, far)], 0
    )
    return spread[...] + jnp.where(even, straight, crossed)


def stepped(params, grad):
    field = sigmoid(sharpness * params)
    return params - step_size * sharpness * field * (1.0 - field) * grad


def masked(place, tile, whole, params, col_offset):
    first_col = place[1:2, :128] * tile[1] + col_offset
    first_row = place[0:1, :128] * tile[0] - H
    inside = window(params.shape, first_col, first_row, whole[1], whole[0])
    return jnp.where(inside, sigmoid(sharpness * params), 0.0)


def field_window(geo, place, tile, whole, col_offset):
    middle = place[1:2, :128] * tile[1] + col_offset + H + geo.half
    step = lax.broadcasted_iota(jnp.int32, (geo.half_up, 128), 0)
    return [(col >= 0) & (col < whole[1]) for col in (middle + step, middle - 1 - step)]


def first_kernel(
    geo, tile, whole, place, weights, own, target, first, second, spec, mirror, *rest
):
    tabs = dict(zip(STEP_TABLES, rest))
    rest = rest[len(STEP_TABLES) :]
    spread, to_far, to_near, params_out, goal_out, params, goal, fields = rest
    cols = own.shape[0]
    right_first = is_even(place, 1, first.shape)
    left = jnp.where(right_first, second[...], first[...])
    right = jnp.where(right_first, first[...], second[...])
    params[...] = jnp.zeros_like(params)
    params[0:128, :] = left[0:128, :]
    params[128 : 128 + cols, :] = own[...]
    params[128 + cols : 256 + cols, :] = right[0:128, :]
    left_lanes = lanes((48, 128))
    goal[...] = jnp.zeros_like(goal)
    for start, side in ((0, left), (96 + cols, right)):
        packed = side[128:176, :]
        turned = swap_halves(packed)
        goal[start : start + 48, :] = jnp.where(left_lanes, packed, turned)
        goal[start + 48 : start + 96, :] = jnp.where(left_lanes, turned, packed)
    goal[96 : 96 + cols, :] = target[...]
    goals = [
        goal[geo.half : geo.half + geo.half_up, :],
        dot(mirror[...], goal[0 : mirror.shape[1], :].astype(bf16)),
    ]
    for side in (0, 1):
        goal_out[side] = goals[side][: goal_out.shape[1]]
    params_out[...] = params[64 : 64 + params_out.shape[0], :]
    mask = masked(place, tile, whole, params[...], -128)
    inside = field_window(geo, place, tile, whole, -128)
    _, grad = one_step(geo, mask, goals, inside, weights, spec, tabs, fields)
    spread_out(place, grad, spread, to_far, to_near)


def second_kernel(geo, tile, whole, place, weights, own, far, near, old, goal, spec, *rest):
    tabs = dict(zip(STEP_TABLES, rest))
    spread, to_far, to_near, params_out, fields = rest[len(STEP_TABLES) :]
    params = stepped(old[...], gathered(place, own, far, near))
    params_out[...] = params[64 : 64 + params_out.shape[0], :]
    mask = masked(place, tile, whole, params, -64)
    inside = field_window(geo, place, tile, whole, -64)
    goals = [goal[0], goal[1]]
    _, grad = one_step(geo, mask, goals, inside, weights, spec, tabs, fields)
    spread_out(place, grad, spread, to_far, to_near)


def update_kernel(cols, place, own, far, near, old, params, to_first, to_second):
    params[...] = stepped(old[...], gathered(place, own, far, near))
    right = is_even(place, 1, (64, 128))
    to_left, to_right = params[0:64, :], params[cols - 64 : cols, :]
    to_first[...] = jnp.where(right, to_right, to_left)
    to_second[...] = jnp.where(right, to_left, to_right)


def third_kernel(
    geo, tile, whole, place, weights, own, first, second, goal, spec, *rest
):
    tabs = dict(zip(STEP_TABLES, rest))
    rest = rest[len(STEP_TABLES) :]
    spread, to_far, to_near, intensity_out, params, fields = rest
    cols = tile[1]
    right_first = is_even(place, 1, (64, 128))
    params[...] = jnp.zeros_like(params)
    params[0:64, :] = jnp.where(right_first, second[...], first[...])
    params[64 : 64 + cols, :] = own[0:cols, :]
    params[64 + cols : 128 + cols, :] = jnp.where(right_first, first[...], second[...])
    mask = masked(place, tile, whole, params[...], -64)
    inside = field_window(geo, place, tile, whole, -64)
    goals = [goal[0], goal[1]]
    intensity, grad = one_step(geo, mask, goals, inside, weights, spec, tabs, fields)
    spread_out(place, grad, spread, to_far, to_near)
    for side in (0, 1):
        intensity_out[side] = intensity[side]


def intensity_kernel(cols, intensity, mirror, out, flat):
    high, low = split(intensity[1])
    rest = (intensity[1] - high.astype(f32) - low.astype(f32)).astype(bf16)
    turned = dot(mirror[...], high) + (dot(mirror[...], low) + dot(mirror[...], rest))
    flat[...] = jnp.zeros_like(flat)
    flat[0 : cols // 2, :] = turned[0 : cols // 2]
    flat[cols // 2 : cols, :] = intensity[0][0 : cols // 2]
    out[...] = flat[...].T[:64, :cols]


def final_kernel(cols, place, own, far, near, out, wide):
    wide[...] = jnp.zeros_like(wide)
    wide[0 : own.shape[0], :] = gathered(place, own, far, near)
    out[...] = wide[...].T[H : H + 64, :cols]


def mirror_table(rows, rows_up, cols_up):
    table = np.zeros((rows_up, cols_up), np.float32)
    table[np.arange(rows), rows - 1 - np.arange(rows)] = 1.0
    return table.astype(ml_dtypes.bfloat16)


def call(kernel, name, out_shapes, scratch, args):
    return pl.pallas_call(
        kernel,
        name=name,
        out_shape=[
            shape if isinstance(shape, jax.ShapeDtypeStruct) else pltpu.VMEM(shape, f32)
            for shape in out_shapes
        ],
        in_specs=[pl.BlockSpec(memory_space=pltpu.VMEM)] * len(args),
        out_specs=[pl.BlockSpec(memory_space=pltpu.VMEM)] * len(out_shapes),
        scratch_shapes=[pltpu.VMEM(shape, f32) for shape in scratch],
        compiler_params=pltpu.CompilerParams(vmem_limit_bytes=VMEM_LIMIT),
    )(*[pltpu.with_memory_space_constraint(arg, pltpu.VMEM) for arg in args])


def per_device(rows, cols, mask_params, target_bits, kern_real, kern_imag, socs_weights):
    tile = mask_params.shape
    whole = (tile[0] * rows, tile[1] * cols)
    kernels = kern_real.shape[1] // KS
    axis = lax.broadcasted_iota(jnp.int32, (8, 256), 0)
    place = jnp.where(axis == 0, lax.axis_index("row"), lax.axis_index("col"))
    weights = jnp.broadcast_to(socs_weights[:, None], (kernels, 128))

    def swaps(count, start):
        pairs = [(i, i + 1) for i in range(start, count - 1, 2)]
        return pairs + [(b, a) for a, b in pairs]

    def row_exchange(to_far, to_near):
        far = lax.ppermute(to_far, "row", swaps(rows, 1))
        return far, lax.ppermute(to_near, "row", swaps(rows, 0))

    def col_exchange(to_first, to_second):
        first = lax.ppermute(to_first, "col", swaps(cols, 0))
        return first, lax.ppermute(to_second, "col", swaps(cols, 1))

    wide, slim = Geometry(tile[1] + 8 * H), Geometry(tile[1] + 4 * H)
    shared = row_tables()
    shared["wide_mirror"] = mirror_table(wide.half, wide.half_up, wide.half_up)
    shared["slim_mirror"] = mirror_table(tile[1] // 2, up(tile[1] // 2, 16), slim.half_up)
    made = {"wide": wide.tables(), "slim": slim.tables(), "shared": shared}
    n = tile[1]
    far, near = row_exchange(mask_params, mask_params)
    params, target = call(
        early_kernel,
        "early",
        [(n, 128), (n, 128)],
        [(128, 256)],
        [mask_params, target_bits],
    )
    params, to_first, to_second = call(
        prep_kernel,
        "prep",
        [(n, 128), (176, 128), (176, 128)],
        [(128, 256)],
        [place, params, target, far, near],
    )
    first, second = col_exchange(to_first, to_second)
    names = [(label, name) for label in ("wide", "slim") for name in COLUMN_TABLES]
    names += [("shared", name) for name in ROW_TABLES + ("wide_mirror", "slim_mirror")]
    names += [("slim", "tap_cols")]
    tables = [jnp.asarray(made[label][name]) for label, name in names]
    inputs = [
        kern_real,
        kern_imag,
        jnp.asarray(shared["tap_rows"]),
        jnp.asarray(made["wide"]["tap_cols"]),
    ]
    wide_spec, half_spec, *held = pl.pallas_call(
        functools.partial(setup_kernel, wide, len(tables)),
        name="spectra",
        out_shape=[
            pltpu.VMEM((2 * kernels * wide.freqs_up, 256), f32),
            pltpu.VMEM((kernels * KS, 512), f32),
        ]
        + [pltpu.VMEM(table.shape, table.dtype) for table in tables],
        in_specs=[pl.BlockSpec(memory_space=pltpu.VMEM)] * len(inputs)
        + [pl.BlockSpec(memory_space=pltpu.HBM)] * len(tables),
        out_specs=[pl.BlockSpec(memory_space=pltpu.VMEM)] * (2 + len(tables)),
        scratch_shapes=[pltpu.SemaphoreType.DMA((len(tables),))],
        compiler_params=pltpu.CompilerParams(vmem_limit_bytes=VMEM_LIMIT),
    )(*[pltpu.with_memory_space_constraint(arg, pltpu.HBM) for arg in inputs + tables])
    place_of = {key: table for key, table in zip(names, held)}

    def tabs(label):
        return [place_of[label, name] for name in COLUMN_TABLES] + [
            place_of["shared", name] for name in ROW_TABLES
        ]

    def spreads(geo):
        return [(geo.grad_up, 128)] + [(geo.grad_up // 2, 128)] * 2

    def fields(geo):
        return (2, kernels, geo.half_up, 128)

    spread, to_far, to_near, params, goal = call(
        functools.partial(first_kernel, wide, tile, whole),
        "first",
        spreads(wide) + [(slim.mask_up, 128), (2, slim.half_up, 128)],
        [(wide.mask_up, 128), (wide.half + wide.half_up, 128), fields(wide)],
        [place, weights, params, target, first, second, wide_spec]
        + [place_of["shared", "wide_mirror"], *tabs("wide")],
    )
    far, near = row_exchange(to_far, to_near)
    (slim_spec,) = call(
        functools.partial(slim_kernel, slim),
        "slim",
        [(2 * kernels * slim.freqs_up, 256)],
        [],
        [half_spec, place_of["slim", "tap_cols"]],
    )
    spread, to_far, to_near, params = call(
        functools.partial(second_kernel, slim, tile, whole),
        "second",
        spreads(slim) + [(slim.grad_up, 128)],
        [fields(slim)],
        [place, weights, spread, far, near, params, goal, slim_spec, *tabs("slim")],
    )
    far, near = row_exchange(to_far, to_near)
    params, to_first, to_second = call(
        functools.partial(update_kernel, n),
        "update",
        [(slim.grad_up, 128), (64, 128), (64, 128)],
        [],
        [place, spread, far, near, params],
    )
    first, second = col_exchange(to_first, to_second)
    spread, to_far, to_near, intensity = call(
        functools.partial(third_kernel, slim, tile, whole),
        "third",
        spreads(slim) + [(2, slim.half_up, 128)],
        [(slim.mask_up, 128), fields(slim)],
        [place, weights, params, first, second, goal, slim_spec, *tabs("slim")],
    )
    far, near = row_exchange(to_far, to_near)
    (intensity,) = call(
        functools.partial(intensity_kernel, n),
        "intensity",
        [jax.ShapeDtypeStruct(tile, f32)],
        [(256, 128)],
        [intensity, place_of["shared", "slim_mirror"]],
    )
    (mask_grad,) = call(
        functools.partial(final_kernel, n),
        "final",
        [jax.ShapeDtypeStruct(tile, f32)],
        [(256, 128)],
        [place, spread, far, near],
    )
    return mask_grad, intensity


def solution(mesh):
    placed = (P("row", "col"), P("row", "col"), P(), P(), P())
    return jax.shard_map(
        functools.partial(per_device, mesh.shape["row"], mesh.shape["col"]),
        mesh=mesh,
        in_specs=placed,
        out_specs=(P("row", "col"), P("row", "col")),
        check_vma=False,
    )
```

```python
import functools
import math

import jax
import jax.numpy as jnp
import ml_dtypes
import numpy as np
from jax import lax
from jax.experimental import pallas as pl
from jax.experimental.pallas import tpu as pltpu
from jax.sharding import PartitionSpec as P

H = 32
KS = 64
ITERS = 3
ROWS = 128
sharpness = 2.0
steepness = 4.0
threshold = 0.8
step_size = 1.0
f32 = jnp.float32
bf16 = jnp.bfloat16
VMEM_LIMIT = 28 * 1024 * 1024


def up(value, unit):
    return -(-value // unit) * unit


def halves(table):
    table = table.astype(np.float32)
    high = table.astype(ml_dtypes.bfloat16)
    low = (table - high.astype(np.float32)).astype(ml_dtypes.bfloat16)
    return high, low


def angles(left, right, length):
    product = np.outer(left.astype(np.int64), right.astype(np.int64)) % length
    return product * (2.0 * math.pi / length)


def grown(table, rows, cols):
    return np.pad(table, [(0, rows - table.shape[0]), (0, cols - table.shape[1])])


def left_stack(table):
    high, low = halves(table)
    return np.concatenate([high, high, low], 1)


def right_stack(table):
    high, low = halves(table)
    return np.concatenate([high, high, low], 0)


class Geometry:
    def __init__(self, width):
        self.mask = width
        self.field = width - 2 * H
        self.grad = width - 4 * H
        self.length = width | 1
        self.freqs = (self.length + 1) // 2
        self.freqs_up = up(self.freqs, 16)
        self.mask_up = up(self.mask, 16)
        self.half = self.field // 2
        self.half_up = up(self.half, 16)
        self.grad_up = up(self.grad, 32)

    def tables(self):
        freq = np.arange(self.freqs)
        fu, hu = self.freqs_up, self.half_up
        middle = H + (self.field - 1) / 2.0
        weight = np.where(freq == 0, 1.0, 2.0) / (self.length * ROWS)

        def phases(places):
            return angles(freq, np.round(2 * places), 2 * self.length)

        def complex_table(phase, sign, rows, cols, axis):
            parts = [grown(np.cos(phase), rows, cols), grown(sign * np.sin(phase), rows, cols)]
            return np.concatenate(parts, axis)

        mask = phases(np.arange(self.mask) - middle)
        half = phases(np.arange(self.half) + 0.5)
        grad = phases(np.arange(self.grad) + 2 * H - middle)
        taps = phases(np.arange(KS) - H)
        grad_table = np.concatenate(
            [
                grown((np.cos(grad) * weight[:, None]).T, self.grad_up, fu),
                grown((-np.sin(grad) * weight[:, None]).T, self.grad_up, fu),
            ],
            1,
        )
        return dict(
            mask_cols=left_stack(complex_table(mask, -1.0, fu, self.mask_up, 0)),
            field_even=left_stack(grown((np.cos(half) * weight[:, None]).T, hu, fu)),
            field_odd=left_stack(grown((np.sin(half) * weight[:, None]).T, hu, fu)),
            source_even=left_stack(grown(np.cos(half), fu, hu)),
            source_odd=left_stack(grown(-np.sin(half), fu, hu)),
            grad_cols=left_stack(grad_table),
            tap_cols=left_stack(complex_table(taps, 1.0, fu, KS, 1)),
        )


def row_tables():
    freq = np.arange(ROWS)

    def complex_table(phase, sign):
        cos, sin = np.cos(phase), sign * np.sin(phase)
        return np.block([[cos, sin], [-sin, cos]])

    def side(table):
        high, low = halves(table)
        return np.concatenate([high, low], 1)

    places = np.arange(64) + H
    field = complex_table(angles(freq, places, ROWS), 1.0)
    field_swapped = np.concatenate([field[:, 64:], field[:, :64]], 1)
    source = complex_table(angles(np.arange(64), freq, ROWS), -1.0)
    source_swapped = np.concatenate([source[64:], source[:64]], 0)
    taps = angles(np.arange(KS) - H, freq, ROWS)
    tap = np.concatenate([np.cos(taps), -np.sin(taps)], 1)
    zero = np.zeros_like(tap)
    return dict(
        mask_rows=right_stack(complex_table(angles(freq, freq, ROWS), -1.0)),
        field_rows=side(field),
        field_rows_swapped=side(field_swapped),
        source_rows=right_stack(source),
        source_rows_swapped=right_stack(source_swapped),
        grad_rows=right_stack(complex_table(angles(freq, freq - H, ROWS), 1.0)),
        tap_rows=right_stack(np.block([[tap, zero], [zero, tap]])),
    )


def split(value):
    high = value.astype(bf16)
    return high, (value - high.astype(f32)).astype(bf16)


def dot(left, right):
    return lax.dot_general(
        left, right, (((1,), (0,)), ((), ())), preferred_element_type=f32
    )


def chunks(count, parts):
    units = count // 16
    edges = [16 * (units * i // parts) for i in range(parts + 1)]
    return list(zip(edges[:-1], edges[1:]))


def left_dot(table, value, parts=1):
    high, low = split(value)
    stacked = jnp.concatenate([high, low, high], 0)
    rows = [table[a:b, :] for a, b in chunks(table.shape[0], parts)]
    return jnp.concatenate([dot(part, stacked) for part in rows], 0)


def right_dot(value, table, parts=1):
    high, low = split(value)
    stacked = jnp.concatenate([high, low, high], 1)
    rows = [stacked[a:b] for a, b in chunks(value.shape[0], parts)]
    return jnp.concatenate([dot(part, table) for part in rows], 0)


def sigmoid(value):
    return 1.0 / (1.0 + jnp.exp(-value))


def swap_halves(value):
    return pltpu.roll(value, 64, 1)


def is_even(place, axis, shape):
    return jnp.broadcast_to(place[axis : axis + 1, : shape[1]], shape) % 2 == 0


def window(shape, first_col, first_row, whole_cols, whole_rows):
    col = lax.broadcasted_iota(jnp.int32, shape, 0) + first_col
    row = lax.broadcasted_iota(jnp.int32, shape, 1) + first_row
    return (col >= 0) & (col < whole_cols) & (row >= 0) & (row < whole_rows)


def column_spectra(geo, half, table, out):
    count = geo.freqs_up
    for k in range(out.shape[0] // (2 * count)):
        part = half[k * KS : (k + 1) * KS, :]
        turned = jnp.concatenate(
            [part[:, 128:256], -part[:, 0:128], part[:, 384:512], -part[:, 256:384]], 1
        )
        spec = left_dot(table[...], jnp.concatenate([part, turned], 0))
        out[2 * k * count : (2 * k + 1) * count, :] = spec[:, :256]
        out[(2 * k + 1) * count : (2 * k + 2) * count, :] = spec[:, 256:]


def taps_kernel(kern_real, kern_imag, tap_rows, half):
    both = jnp.concatenate([kern_real[...], kern_imag[...]], 0)
    for start in range(0, both.shape[1], 128):
        part = both[:, start : start + 128].T
        half[start : start + 128, :] = right_dot(part, tap_rows[...])


def setup_kernel(geo, held, half, tap_cols, *rest):
    sources, out, rest = rest[:held], rest[held], rest[held + 1 :]
    targets, sems = rest[:held], rest[held]
    copies = [
        pltpu.make_async_copy(source, target, sems.at[index])
        for index, (source, target) in enumerate(zip(sources, targets))
    ]
    for copy in copies:
        copy.start()
    column_spectra(geo, half, tap_cols, out)
    for copy in copies:
        copy.wait()


def slim_kernel(geo, half, tap_cols, out):
    column_spectra(geo, half, tap_cols, out)


def one_step(geo, mask, target, inside, weights, spec, tabs, fields):
    count = geo.freqs_up
    kernels = fields.shape[1]
    across = left_dot(tabs["mask_cols"], mask, 2)
    mask_spec = right_dot(
        jnp.concatenate([across[:count], across[count:]], 1), tabs["mask_rows"][...], 2
    )

    def place(index, start, stop):
        value = spec[index * count + start : index * count + stop, :]
        return value[:, :128], value[:, 128:]

    evens, odds = [], []
    for start, stop in chunks(count, 1):
        size = stop - start
        lane = lanes((size, 128))
        mask_re, mask_im = mask_spec[start:stop, :128], mask_spec[start:stop, 128:]

        def down(indices, table):
            products = []
            for index in indices:
                re, im = place(index, start, stop)
                products.append(
                    jnp.concatenate(
                        [re * mask_re - im * mask_im, re * mask_im + im * mask_re], 1
                    )
                )
            high, low = split(jnp.concatenate(products, 0))
            wide = dot(high, table[...])
            got = wide[:, :128] + wide[:, 128:] + dot(low, table[:, :128])
            return [got[i * size : (i + 1) * size] for i in range(len(indices))]

        firsts = down(range(0, 2 * kernels, 2), tabs["field_rows"])
        seconds = down(range(1, 2 * kernels, 2), tabs["field_rows_swapped"])
        pairs = list(zip(firsts, seconds))
        evens.append(jnp.concatenate([jnp.where(lane, a, b) for a, b in pairs], 1))
        odds.append(
            jnp.concatenate([swap_halves(jnp.where(lane, b, a)) for a, b in pairs], 1)
        )
    even = left_dot(tabs["field_even"][...], jnp.concatenate(evens, 0))
    odd = left_dot(tabs["field_odd"][...], jnp.concatenate(odds, 0))
    zero = jnp.zeros((geo.half_up, 128), f32)
    intensity = [zero, zero]
    for side, field in enumerate((even - odd, even + odd)):
        for j in range(kernels):
            own = field[:, j * 128 : (j + 1) * 128]
            fields[side, j] = own
            intensity[side] = intensity[side] + weights[j : j + 1, :] * (own * own)
    cotangent = []
    for side in (0, 1):
        intensity[side] = intensity[side] + swap_halves(intensity[side])
        resist = sigmoid(steepness * (intensity[side] - threshold))
        slope = 2.0 * (resist - target[side]) * steepness * resist * (1.0 - resist)
        cotangent.append(jnp.where(inside[side], slope, 0.0))
    right, left = (
        jnp.concatenate(
            [
                (2.0 * weights[j : j + 1, :] * cotangent[side]) * fields[side, j]
                for j in range(kernels)
            ],
            1,
        )
        for side in (0, 1)
    )
    even = left_dot(tabs["source_even"][...], right + left)
    odd = left_dot(tabs["source_odd"][...], right - left)
    totals = []
    for start, stop in chunks(count, 2):
        size = stop - start
        lane = lanes((size, 128))
        res = [even[start:stop, j * 128 : (j + 1) * 128] for j in range(kernels)]
        ims = [swap_halves(odd[start:stop, j * 128 : (j + 1) * 128]) for j in range(kernels)]
        total_re = jnp.zeros((size, 128), f32)
        total_im = jnp.zeros((size, 128), f32)
        for index, values, table in (
            (0, [jnp.where(lane, a, b) for a, b in zip(res, ims)], tabs["source_rows"]),
            (1, [jnp.where(lane, b, a) for a, b in zip(res, ims)], tabs["source_rows_swapped"]),
        ):
            got = right_dot(jnp.concatenate(values, 0), table[...])
            for j in range(kernels):
                got_re = got[j * size : (j + 1) * size, :128]
                got_im = got[j * size : (j + 1) * size, 128:]
                re, im = place(2 * j + index, start, stop)
                total_re = total_re + (re * got_re + im * got_im)
                total_im = total_im + (re * got_im - im * got_re)
        totals.append(jnp.concatenate([total_re, total_im], 1))
    back = right_dot(jnp.concatenate(totals, 0), tabs["grad_rows"][...], 2)
    grad = left_dot(
        tabs["grad_cols"], jnp.concatenate([back[:, :128], back[:, 128:]], 0), 2
    )
    return intensity, grad


COLUMN_TABLES = (
    "mask_cols",
    "field_even",
    "field_odd",
    "source_even",
    "source_odd",
    "grad_cols",
)
ROW_TABLES = (
    "mask_rows",
    "field_rows",
    "field_rows_swapped",
    "source_rows",
    "source_rows_swapped",
    "grad_rows",
)
STEP_TABLES = COLUMN_TABLES + ROW_TABLES


def lanes(shape):
    return lax.broadcasted_iota(jnp.int32, shape, 1) < 64


def early_kernel(own, bits, params, target, tall):
    cols = own.shape[1]
    tall[...] = jnp.zeros_like(tall)
    tall[32:96, :cols] = own[...]
    params[...] = tall[...].T[:cols]
    words = bits.shape[0]
    width = cols // words
    shift = lax.broadcasted_iota(jnp.int32, (width, 128), 0)
    for index in range(words):
        word = bits[index : index + 1, :]
        word = jnp.broadcast_to(jnp.concatenate([word, word], 1), (width, 128))
        bit = jnp.bitwise_and(jnp.right_shift(word, shift), 1).astype(f32)
        target[index * width : (index + 1) * width, :] = bit


def prep_kernel(place, own, target, across, within, params, to_first, to_second, tall):
    even = is_even(place, 0, (32, own.shape[0]))
    cols = own.shape[0]
    tall[...] = jnp.zeros_like(tall)
    tall[0:32, :cols] = jnp.where(even, across[32:64, :], within[32:64, :])
    tall[96:128, :cols] = jnp.where(even, within[0:32, :], across[0:32, :])
    params[...] = own[...] + tall[...].T[:cols]
    right = is_even(place, 1, (176, 128))
    left_lanes = lanes((48, 128))

    def packed(start):
        return jnp.where(left_lanes, target[start : start + 48], target[start + 48 : start + 96])

    to_left = jnp.concatenate([params[0:128, :], packed(0)], 0)
    to_right = jnp.concatenate([params[cols - 128 : cols, :], packed(cols - 96)], 0)
    to_first[...] = jnp.where(right, to_right, to_left)
    to_second[...] = jnp.where(right, to_left, to_right)


def spread_out(place, grad, spread, to_far, to_near):
    even = is_even(place, 0, grad.shape)
    half = to_far.shape[0]
    spread[...] = grad
    turned = swap_halves(grad)
    straight = jnp.where(even, grad, turned)
    crossed = jnp.where(even, turned, grad)
    left_lanes = lanes((half, 128))
    to_far[...] = jnp.where(left_lanes, straight[:half], crossed[half:])
    to_near[...] = jnp.where(left_lanes, crossed[:half], straight[half:])


def gathered(place, spread, far, near):
    even = is_even(place, 0, spread.shape)
    far, near = far[...], near[...]
    left_lanes = lanes(far.shape)
    far_turned, near_turned = swap_halves(far), swap_halves(near)
    straight = jnp.concatenate(
        [jnp.where(left_lanes, far, near_turned), jnp.where(left_lanes, far_turned, near)], 0
    )
    crossed = jnp.concatenate(
        [jnp.where(left_lanes, near, far_turned), jnp.where(left_lanes, near_turned, far)], 0
    )
    return spread[...] + jnp.where(even, straight, crossed)


def stepped(params, grad):
    field = sigmoid(sharpness * params)
    return params - step_size * sharpness * field * (1.0 - field) * grad


def masked(place, tile, whole, params, col_offset):
    first_col = place[1:2, :128] * tile[1] + col_offset
    first_row = place[0:1, :128] * tile[0] - H
    inside = window(params.shape, first_col, first_row, whole[1], whole[0])
    return jnp.where(inside, sigmoid(sharpness * params), 0.0)


def field_window(geo, place, tile, whole, col_offset):
    middle = place[1:2, :128] * tile[1] + col_offset + H + geo.half
    step = lax.broadcasted_iota(jnp.int32, (geo.half_up, 128), 0)
    return [(col >= 0) & (col < whole[1]) for col in (middle + step, middle - 1 - step)]


def first_kernel(
    geo, tile, whole, place, weights, own, target, first, second, spec, mirror, *rest
):
    tabs = dict(zip(STEP_TABLES, rest))
    rest = rest[len(STEP_TABLES) :]
    spread, to_far, to_near, params_out, goal_out, params, goal, fields = rest
    cols = own.shape[0]
    right_first = is_even(place, 1, first.shape)
    left = jnp.where(right_first, second[...], first[...])
    right = jnp.where(right_first, first[...], second[...])
    params[...] = jnp.zeros_like(params)
    params[0:128, :] = left[0:128, :]
    params[128 : 128 + cols, :] = own[...]
    params[128 + cols : 256 + cols, :] = right[0:128, :]
    left_lanes = lanes((48, 128))
    goal[...] = jnp.zeros_like(goal)
    for start, side in ((0, left), (96 + cols, right)):
        packed = side[128:176, :]
        turned = swap_halves(packed)
        goal[start : start + 48, :] = jnp.where(left_lanes, packed, turned)
        goal[start + 48 : start + 96, :] = jnp.where(left_lanes, turned, packed)
    goal[96 : 96 + cols, :] = target[...]
    goals = [
        goal[geo.half : geo.half + geo.half_up, :],
        dot(mirror[...], goal[0 : mirror.shape[1], :].astype(bf16)),
    ]
    for side in (0, 1):
        goal_out[side] = goals[side][: goal_out.shape[1]]
    params_out[...] = params[64 : 64 + params_out.shape[0], :]
    mask = masked(place, tile, whole, params[...], -128)
    inside = field_window(geo, place, tile, whole, -128)
    _, grad = one_step(geo, mask, goals, inside, weights, spec, tabs, fields)
    spread_out(place, grad, spread, to_far, to_near)


def second_kernel(geo, tile, whole, place, weights, own, far, near, old, goal, spec, *rest):
    tabs = dict(zip(STEP_TABLES, rest))
    spread, to_far, to_near, params_out, fields = rest[len(STEP_TABLES) :]
    params = stepped(old[...], gathered(place, own, far, near))
    params_out[...] = params[64 : 64 + params_out.shape[0], :]
    mask = masked(place, tile, whole, params, -64)
    inside = field_window(geo, place, tile, whole, -64)
    goals = [goal[0], goal[1]]
    _, grad = one_step(geo, mask, goals, inside, weights, spec, tabs, fields)
    spread_out(place, grad, spread, to_far, to_near)


def update_kernel(cols, place, own, far, near, old, params, to_first, to_second):
    params[...] = stepped(old[...], gathered(place, own, far, near))
    right = is_even(place, 1, (64, 128))
    to_left, to_right = params[0:64, :], params[cols - 64 : cols, :]
    to_first[...] = jnp.where(right, to_right, to_left)
    to_second[...] = jnp.where(right, to_left, to_right)


def third_kernel(
    geo, tile, whole, place, weights, own, first, second, goal, spec, *rest
):
    tabs = dict(zip(STEP_TABLES, rest))
    rest = rest[len(STEP_TABLES) :]
    spread, to_far, to_near, intensity_out, params, fields = rest
    cols = tile[1]
    right_first = is_even(place, 1, (64, 128))
    params[...] = jnp.zeros_like(params)
    params[0:64, :] = jnp.where(right_first, second[...], first[...])
    params[64 : 64 + cols, :] = own[0:cols, :]
    params[64 + cols : 128 + cols, :] = jnp.where(right_first, first[...], second[...])
    mask = masked(place, tile, whole, params[...], -64)
    inside = field_window(geo, place, tile, whole, -64)
    goals = [goal[0], goal[1]]
    intensity, grad = one_step(geo, mask, goals, inside, weights, spec, tabs, fields)
    spread_out(place, grad, spread, to_far, to_near)
    for side in (0, 1):
        intensity_out[side] = intensity[side]


def intensity_kernel(cols, intensity, mirror, out, flat):
    high, low = split(intensity[1])
    rest = (intensity[1] - high.astype(f32) - low.astype(f32)).astype(bf16)
    turned = dot(mirror[...], high) + (dot(mirror[...], low) + dot(mirror[...], rest))
    flat[...] = jnp.zeros_like(flat)
    flat[0 : cols // 2, :] = turned[0 : cols // 2]
    flat[cols // 2 : cols, :] = intensity[0][0 : cols // 2]
    out[...] = flat[...].T[:64, :cols]


def final_kernel(cols, place, own, far, near, out, wide):
    wide[...] = jnp.zeros_like(wide)
    wide[0 : own.shape[0], :] = gathered(place, own, far, near)
    out[...] = wide[...].T[H : H + 64, :cols]


def mirror_table(rows, rows_up, cols_up):
    table = np.zeros((rows_up, cols_up), np.float32)
    table[np.arange(rows), rows - 1 - np.arange(rows)] = 1.0
    return table.astype(ml_dtypes.bfloat16)


def call(kernel, name, out_shapes, scratch, args, space=pltpu.VMEM):
    return pl.pallas_call(
        kernel,
        name=name,
        out_shape=[
            shape if isinstance(shape, jax.ShapeDtypeStruct) else pltpu.VMEM(shape, f32)
            for shape in out_shapes
        ],
        in_specs=[pl.BlockSpec(memory_space=pltpu.VMEM)] * len(args),
        out_specs=[pl.BlockSpec(memory_space=pltpu.VMEM)] * len(out_shapes),
        scratch_shapes=[pltpu.VMEM(shape, f32) for shape in scratch],
        compiler_params=pltpu.CompilerParams(vmem_limit_bytes=VMEM_LIMIT),
    )(*[pltpu.with_memory_space_constraint(arg, space) for arg in args])


def per_device(rows, cols, mask_params, target_bits, kern_real, kern_imag, socs_weights):
    tile = mask_params.shape
    whole = (tile[0] * rows, tile[1] * cols)
    kernels = kern_real.shape[1] // KS
    axis = lax.broadcasted_iota(jnp.int32, (8, 256), 0)
    place = jnp.where(axis == 0, lax.axis_index("row"), lax.axis_index("col"))
    weights = jnp.broadcast_to(socs_weights[:, None], (kernels, 128))

    def swaps(count, start):
        pairs = [(i, i + 1) for i in range(start, count - 1, 2)]
        return pairs + [(b, a) for a, b in pairs]

    def row_exchange(to_far, to_near):
        far = lax.ppermute(to_far, "row", swaps(rows, 1))
        return far, lax.ppermute(to_near, "row", swaps(rows, 0))

    def col_exchange(to_first, to_second):
        first = lax.ppermute(to_first, "col", swaps(cols, 0))
        return first, lax.ppermute(to_second, "col", swaps(cols, 1))

    wide, slim = Geometry(tile[1] + 8 * H), Geometry(tile[1] + 4 * H)
    shared = row_tables()
    shared["wide_mirror"] = mirror_table(wide.half, wide.half_up, wide.half_up)
    shared["slim_mirror"] = mirror_table(tile[1] // 2, up(tile[1] // 2, 16), slim.half_up)
    made = {"wide": wide.tables(), "slim": slim.tables(), "shared": shared}
    n = tile[1]
    far, near = row_exchange(mask_params, mask_params)
    params, target = call(
        early_kernel,
        "early",
        [(n, 128), (n, 128)],
        [(128, 256)],
        [mask_params, target_bits.T],
        pltpu.HBM,
    )
    (half_spec,) = call(
        taps_kernel,
        "taps",
        [(kernels * KS, 512)],
        [],
        [kern_real, kern_imag, jnp.asarray(shared["tap_rows"])],
        pltpu.HBM,
    )
    near, half_spec = lax.optimization_barrier((near, half_spec))
    params, to_first, to_second = call(
        prep_kernel,
        "prep",
        [(n, 128), (176, 128), (176, 128)],
        [(128, 256)],
        [place, params, target, far, near],
    )
    first, second = col_exchange(to_first, to_second)
    names = [(label, name) for label in ("wide", "slim") for name in COLUMN_TABLES]
    names += [("shared", name) for name in ROW_TABLES + ("wide_mirror", "slim_mirror")]
    names += [("slim", "tap_cols")]
    tables = [jnp.asarray(made[label][name]) for label, name in names]
    arrays = [half_spec, jnp.asarray(made["wide"]["tap_cols"])] + tables
    spaces = [pltpu.VMEM] + [pltpu.HBM] * (1 + len(tables))
    wide_spec, *held = pl.pallas_call(
        functools.partial(setup_kernel, wide, len(tables)),
        name="spectra",
        out_shape=[pltpu.VMEM((2 * kernels * wide.freqs_up, 256), f32)]
        + [pltpu.VMEM(table.shape, table.dtype) for table in tables],
        in_specs=[pl.BlockSpec(memory_space=pltpu.VMEM)] * 2
        + [pl.BlockSpec(memory_space=pltpu.HBM)] * len(tables),
        out_specs=[pl.BlockSpec(memory_space=pltpu.VMEM)] * (1 + len(tables)),
        scratch_shapes=[pltpu.SemaphoreType.DMA((len(tables),))],
        compiler_params=pltpu.CompilerParams(vmem_limit_bytes=VMEM_LIMIT),
    )(*[pltpu.with_memory_space_constraint(*pair) for pair in zip(arrays, spaces)])
    place_of = {key: table for key, table in zip(names, held)}

    def tabs(label):
        return [place_of[label, name] for name in COLUMN_TABLES] + [
            place_of["shared", name] for name in ROW_TABLES
        ]

    def spreads(geo):
        return [(geo.grad_up, 128)] + [(geo.grad_up // 2, 128)] * 2

    def fields(geo):
        return (2, kernels, geo.half_up, 128)

    spread, to_far, to_near, params, goal = call(
        functools.partial(first_kernel, wide, tile, whole),
        "first",
        spreads(wide) + [(slim.mask_up, 128), (2, slim.half_up, 128)],
        [(wide.mask_up, 128), (wide.half + wide.half_up, 128), fields(wide)],
        [place, weights, params, target, first, second, wide_spec]
        + [place_of["shared", "wide_mirror"], *tabs("wide")],
    )
    far, near = row_exchange(to_far, to_near)
    (slim_spec,) = call(
        functools.partial(slim_kernel, slim),
        "slim",
        [(2 * kernels * slim.freqs_up, 256)],
        [],
        [half_spec, place_of["slim", "tap_cols"]],
    )
    spread, to_far, to_near, params = call(
        functools.partial(second_kernel, slim, tile, whole),
        "second",
        spreads(slim) + [(slim.grad_up, 128)],
        [fields(slim)],
        [place, weights, spread, far, near, params, goal, slim_spec, *tabs("slim")],
    )
    far, near = row_exchange(to_far, to_near)
    params, to_first, to_second = call(
        functools.partial(update_kernel, n),
        "update",
        [(slim.grad_up, 128), (64, 128), (64, 128)],
        [],
        [place, spread, far, near, params],
    )
    first, second = col_exchange(to_first, to_second)
    spread, to_far, to_near, intensity = call(
        functools.partial(third_kernel, slim, tile, whole),
        "third",
        spreads(slim) + [(2, slim.half_up, 128)],
        [(slim.mask_up, 128), fields(slim)],
        [place, weights, params, first, second, goal, slim_spec, *tabs("slim")],
    )
    far, near = row_exchange(to_far, to_near)
    (intensity,) = call(
        functools.partial(intensity_kernel, n),
        "intensity",
        [jax.ShapeDtypeStruct(tile, f32)],
        [(256, 128)],
        [intensity, place_of["shared", "slim_mirror"]],
    )
    (mask_grad,) = call(
        functools.partial(final_kernel, n),
        "final",
        [jax.ShapeDtypeStruct(tile, f32)],
        [(256, 128)],
        [place, spread, far, near],
    )
    return mask_grad, intensity


def solution(mesh):
    placed = (P("row", "col"), P("row", "col"), P(), P(), P())
    return jax.shard_map(
        functools.partial(per_device, mesh.shape["row"], mesh.shape["col"]),
        mesh=mesh,
        in_specs=placed,
        out_specs=(P("row", "col"), P("row", "col")),
        check_vma=False,
    )
```

```python
import functools
import math

import jax
import jax.numpy as jnp
import ml_dtypes
import numpy as np
from jax import lax
from jax.experimental import pallas as pl
from jax.experimental.pallas import tpu as pltpu
from jax.sharding import PartitionSpec as P

H = 32
KS = 64
ITERS = 3
ROWS = 128
sharpness = 2.0
steepness = 4.0
threshold = 0.8
step_size = 1.0
f32 = jnp.float32
bf16 = jnp.bfloat16
VMEM_LIMIT = 28 * 1024 * 1024


def up(value, unit):
    return -(-value // unit) * unit


def halves(table):
    table = table.astype(np.float32)
    high = table.astype(ml_dtypes.bfloat16)
    low = (table - high.astype(np.float32)).astype(ml_dtypes.bfloat16)
    return high, low


def angles(left, right, length):
    product = np.outer(left.astype(np.int64), right.astype(np.int64)) % length
    return product * (2.0 * math.pi / length)


def grown(table, rows, cols):
    return np.pad(table, [(0, rows - table.shape[0]), (0, cols - table.shape[1])])


def left_stack(table):
    high, low = halves(table)
    return np.concatenate([high, high, low], 1)


def right_stack(table):
    high, low = halves(table)
    return np.concatenate([high, high, low], 0)


class Geometry:
    def __init__(self, width, trim):
        self.mask = width
        self.centre = width // 2 - H
        self.half = self.centre - trim
        self.grad = width - 4 * H
        self.length = width | 1
        self.freqs = (self.length + 1) // 2
        self.freqs_up = up(self.freqs, 16)
        self.mask_up = up(self.mask, 16)
        self.half_up = up(self.half, 16)
        self.grad_up = up(self.grad, 32)

    def dense(self):
        return 3 * self.half <= 512 < 3 * self.half_up

    def source_stack(self, table):
        table = grown(table, self.freqs_up, self.half_up)
        if not self.dense():
            return left_stack(table)
        high, low = halves(table)
        first, second = high.copy(), high.copy()
        fit = 512 - 2 * self.half_up
        spare = self.half_up - self.half
        rest = self.half - fit
        first[:, self.half :] = low[:, fit : fit + spare]
        second[:, self.half : self.half + rest - spare] = low[:, fit + spare : self.half]
        return np.concatenate([first, second, low[:, :fit]], 1)

    def tables(self):
        freq = np.arange(self.freqs)
        fu, hu = self.freqs_up, self.half_up
        middle = H + self.centre - 0.5
        weight = np.where(freq == 0, 1.0, 2.0) / (self.length * ROWS)

        def phases(places):
            return angles(freq, np.round(2 * places), 2 * self.length)

        def complex_table(phase, sign, rows, cols, axis):
            parts = [grown(np.cos(phase), rows, cols), grown(sign * np.sin(phase), rows, cols)]
            return np.concatenate(parts, axis)

        mask = phases(np.arange(self.mask) - middle)
        half = phases(np.arange(self.half) + 0.5)
        grad = phases(np.arange(self.grad) + 2 * H - middle)
        taps = phases(np.arange(KS) - H)
        grad_table = np.concatenate(
            [
                grown((np.cos(grad) * weight[:, None]).T, self.grad_up, fu),
                grown((-np.sin(grad) * weight[:, None]).T, self.grad_up, fu),
            ],
            1,
        )
        return dict(
            mask_cols=left_stack(complex_table(mask, -1.0, fu, self.mask_up, 0)),
            field_even=left_stack(grown((np.cos(half) * weight[:, None]).T, hu, fu)),
            field_odd=left_stack(grown((np.sin(half) * weight[:, None]).T, hu, fu)),
            source_even=self.source_stack(np.cos(half)),
            source_odd=self.source_stack(-np.sin(half)),
            grad_cols=left_stack(grad_table),
            tap_cols=left_stack(complex_table(taps, 1.0, fu, KS, 1)),
        )


def row_tables():
    freq = np.arange(ROWS)

    def complex_table(phase, sign):
        cos, sin = np.cos(phase), sign * np.sin(phase)
        return np.block([[cos, sin], [-sin, cos]])

    def side(table):
        high, low = halves(table)
        return np.concatenate([high, low], 1)

    places = np.arange(64) + H
    field = complex_table(angles(freq, places, ROWS), 1.0)
    field_swapped = np.concatenate([field[:, 64:], field[:, :64]], 1)
    source = complex_table(angles(np.arange(64), freq, ROWS), -1.0)
    source_swapped = np.concatenate([source[64:], source[:64]], 0)
    taps = angles(np.arange(KS) - H, freq, ROWS)
    tap = np.concatenate([np.cos(taps), -np.sin(taps)], 1)
    zero = np.zeros_like(tap)
    return dict(
        mask_rows=right_stack(complex_table(angles(freq, freq, ROWS), -1.0)),
        field_rows=side(field),
        field_rows_swapped=side(field_swapped),
        source_rows=right_stack(source),
        source_rows_swapped=right_stack(source_swapped),
        grad_rows=right_stack(complex_table(angles(freq, freq - H, ROWS), 1.0)),
        tap_rows=right_stack(np.block([[tap, zero], [zero, tap]])),
    )


def split(value):
    high = value.astype(bf16)
    return high, (value - high.astype(f32)).astype(bf16)


def dot(left, right):
    return lax.dot_general(
        left, right, (((1,), (0,)), ((), ())), preferred_element_type=f32
    )


def chunks(count, parts):
    units = count // 16
    edges = [16 * (units * i // parts) for i in range(parts + 1)]
    return list(zip(edges[:-1], edges[1:]))


def left_dot(table, value, parts=1):
    high, low = split(value)
    stacked = jnp.concatenate([high, low, high], 0)
    rows = [table[a:b, :] for a, b in chunks(table.shape[0], parts)]
    return jnp.concatenate([dot(part, stacked) for part in rows], 0)


def source_dot(geo, table, value):
    if not geo.dense():
        return left_dot(table[...], value)
    fit = 512 - 2 * geo.half_up
    spare = geo.half_up - geo.half
    high, low = split(value)
    tail_high, tail_low = high[fit:].astype(f32)[: geo.half - fit], low[fit:].astype(f32)
    first = jnp.concatenate([tail_high, tail_high[:spare]], 0).astype(bf16)
    rest = tail_high[spare:]
    blank = jnp.zeros((spare - rest.shape[0], value.shape[1]), f32)
    second = jnp.concatenate([tail_low[: geo.half - fit], rest, blank], 0).astype(bf16)
    stacked = jnp.concatenate([high[:fit], first, low[:fit], second, high[:fit]], 0)
    return dot(table[...], stacked)


def right_dot(value, table, parts=1):
    high, low = split(value)
    stacked = jnp.concatenate([high, low, high], 1)
    rows = [stacked[a:b] for a, b in chunks(value.shape[0], parts)]
    return jnp.concatenate([dot(part, table) for part in rows], 0)


def sigmoid(value):
    return 1.0 / (1.0 + jnp.exp(-value))


def swap_halves(value):
    return pltpu.roll(value, 64, 1)


def is_even(place, axis, shape):
    return jnp.broadcast_to(place[axis : axis + 1, : shape[1]], shape) % 2 == 0


def window(shape, first_col, first_row, whole_cols, whole_rows):
    col = lax.broadcasted_iota(jnp.int32, shape, 0) + first_col
    row = lax.broadcasted_iota(jnp.int32, shape, 1) + first_row
    return (col >= 0) & (col < whole_cols) & (row >= 0) & (row < whole_rows)


def column_spectra(geo, half, table, out):
    count = geo.freqs_up
    for k in range(out.shape[0] // (2 * count)):
        part = half[k * KS : (k + 1) * KS, :]
        turned = jnp.concatenate(
            [part[:, 128:256], -part[:, 0:128], part[:, 384:512], -part[:, 256:384]], 1
        )
        spec = left_dot(table[...], jnp.concatenate([part, turned], 0))
        out[2 * k * count : (2 * k + 1) * count, :] = spec[:, :256]
        out[(2 * k + 1) * count : (2 * k + 2) * count, :] = spec[:, 256:]


def bring(sources, targets, sems):
    copies = [
        pltpu.make_async_copy(source, target, sems.at[index])
        for index, (source, target) in enumerate(zip(sources, targets))
    ]
    for copy in copies:
        copy.start()
    return copies


def setup_kernel(geo, held, kern_real, kern_imag, tap_rows, tap_cols, *rest):
    sources, (half, out), rest = rest[:held], rest[held : held + 2], rest[held + 2 :]
    copies = bring(sources, rest[:held], rest[held])
    both = jnp.concatenate([kern_real[...], kern_imag[...]], 0)
    for start in range(0, both.shape[1], 128):
        part = both[:, start : start + 128].T
        half[start : start + 128, :] = right_dot(part, tap_rows[...])
    column_spectra(geo, half, tap_cols, out)
    for copy in copies:
        copy.wait()


def slim_kernel(geo, held, half, tap_cols, *rest):
    sources, out, rest = rest[:held], rest[held], rest[held + 1 :]
    copies = bring(sources, rest[:held], rest[held])
    column_spectra(geo, half, tap_cols, out)
    for copy in copies:
        copy.wait()


def one_step(geo, mask, target, inside, weights, spec, tabs, fields):
    count = geo.freqs_up
    kernels = fields.shape[1]
    across = left_dot(tabs["mask_cols"], mask, 2)
    mask_spec = right_dot(
        jnp.concatenate([across[:count], across[count:]], 1), tabs["mask_rows"][...], 2
    )

    def place(index, start, stop):
        value = spec[index * count + start : index * count + stop, :]
        return value[:, :128], value[:, 128:]

    evens, odds = [], []
    for start, stop in chunks(count, 1):
        size = stop - start
        lane = lanes((size, 128))
        mask_re, mask_im = mask_spec[start:stop, :128], mask_spec[start:stop, 128:]

        def down(indices, table):
            products = []
            for index in indices:
                re, im = place(index, start, stop)
                products.append(
                    jnp.concatenate(
                        [re * mask_re - im * mask_im, re * mask_im + im * mask_re], 1
                    )
                )
            high, low = split(jnp.concatenate(products, 0))
            wide = dot(high, table[...])
            got = wide[:, :128] + wide[:, 128:] + dot(low, table[:, :128])
            return [got[i * size : (i + 1) * size] for i in range(len(indices))]

        firsts = down(range(0, 2 * kernels, 2), tabs["field_rows"])
        seconds = down(range(1, 2 * kernels, 2), tabs["field_rows_swapped"])
        pairs = list(zip(firsts, seconds))
        evens.append(jnp.concatenate([jnp.where(lane, a, b) for a, b in pairs], 1))
        odds.append(
            jnp.concatenate([swap_halves(jnp.where(lane, b, a)) for a, b in pairs], 1)
        )
    even = left_dot(tabs["field_even"][...], jnp.concatenate(evens, 0))
    odd = left_dot(tabs["field_odd"][...], jnp.concatenate(odds, 0))
    zero = jnp.zeros((geo.half_up, 128), f32)
    intensity = [zero, zero]
    for side, field in enumerate((even - odd, even + odd)):
        for j in range(kernels):
            own = field[:, j * 128 : (j + 1) * 128]
            fields[side, j] = own
            intensity[side] = intensity[side] + weights[j : j + 1, :] * (own * own)
    cotangent = []
    for side in (0, 1):
        intensity[side] = intensity[side] + swap_halves(intensity[side])
        resist = sigmoid(steepness * (intensity[side] - threshold))
        slope = 2.0 * (resist - target[side]) * steepness * resist * (1.0 - resist)
        cotangent.append(jnp.where(inside[side], slope, 0.0))
    right, left = (
        jnp.concatenate(
            [
                (2.0 * weights[j : j + 1, :] * cotangent[side]) * fields[side, j]
                for j in range(kernels)
            ],
            1,
        )
        for side in (0, 1)
    )
    even = source_dot(geo, tabs["source_even"], right + left)
    odd = source_dot(geo, tabs["source_odd"], right - left)
    totals = []
    for start, stop in chunks(count, 2):
        size = stop - start
        lane = lanes((size, 128))
        res = [even[start:stop, j * 128 : (j + 1) * 128] for j in range(kernels)]
        ims = [swap_halves(odd[start:stop, j * 128 : (j + 1) * 128]) for j in range(kernels)]
        total_re = jnp.zeros((size, 128), f32)
        total_im = jnp.zeros((size, 128), f32)
        for index, values, table in (
            (0, [jnp.where(lane, a, b) for a, b in zip(res, ims)], tabs["source_rows"]),
            (1, [jnp.where(lane, b, a) for a, b in zip(res, ims)], tabs["source_rows_swapped"]),
        ):
            got = right_dot(jnp.concatenate(values, 0), table[...])
            for j in range(kernels):
                got_re = got[j * size : (j + 1) * size, :128]
                got_im = got[j * size : (j + 1) * size, 128:]
                re, im = place(2 * j + index, start, stop)
                total_re = total_re + (re * got_re + im * got_im)
                total_im = total_im + (re * got_im - im * got_re)
        totals.append(jnp.concatenate([total_re, total_im], 1))
    back = right_dot(jnp.concatenate(totals, 0), tabs["grad_rows"][...], 2)
    grad = left_dot(
        tabs["grad_cols"], jnp.concatenate([back[:, :128], back[:, 128:]], 0), 2
    )
    return intensity, grad


COLUMN_TABLES = (
    "mask_cols",
    "field_even",
    "field_odd",
    "source_even",
    "source_odd",
    "grad_cols",
)
ROW_TABLES = (
    "mask_rows",
    "field_rows",
    "field_rows_swapped",
    "source_rows",
    "source_rows_swapped",
    "grad_rows",
)
STEP_TABLES = COLUMN_TABLES + ROW_TABLES


def lanes(shape):
    return lax.broadcasted_iota(jnp.int32, shape, 1) < 64


def early_kernel(own, bits, params, target, tall):
    cols = own.shape[1]
    tall[...] = jnp.zeros_like(tall)
    tall[32:96, :cols] = own[...]
    params[...] = tall[...].T[:cols]
    words = bits.shape[0]
    width = cols // words
    shift = lax.broadcasted_iota(jnp.int32, (width, 128), 0)
    for index in range(words):
        word = bits[index : index + 1, :]
        word = jnp.broadcast_to(jnp.concatenate([word, word], 1), (width, 128))
        bit = jnp.bitwise_and(jnp.right_shift(word, shift), 1).astype(f32)
        target[index * width : (index + 1) * width, :] = bit


def prep_kernel(place, own, target, across, within, params, to_first, to_second, tall):
    even = is_even(place, 0, (32, own.shape[0]))
    cols = own.shape[0]
    tall[...] = jnp.zeros_like(tall)
    tall[0:32, :cols] = jnp.where(even, across[32:64, :], within[32:64, :])
    tall[96:128, :cols] = jnp.where(even, within[0:32, :], across[0:32, :])
    params[...] = own[...] + tall[...].T[:cols]
    right = is_even(place, 1, (176, 128))
    left_lanes = lanes((48, 128))

    def packed(start):
        return jnp.where(left_lanes, target[start : start + 48], target[start + 48 : start + 96])

    to_left = jnp.concatenate([params[0:128, :], packed(0)], 0)
    to_right = jnp.concatenate([params[cols - 128 : cols, :], packed(cols - 96)], 0)
    to_first[...] = jnp.where(right, to_right, to_left)
    to_second[...] = jnp.where(right, to_left, to_right)


def spread_out(place, grad, spread, to_far, to_near):
    even = is_even(place, 0, grad.shape)
    half = to_far.shape[0]
    spread[...] = grad
    turned = swap_halves(grad)
    straight = jnp.where(even, grad, turned)
    crossed = jnp.where(even, turned, grad)
    left_lanes = lanes((half, 128))
    to_far[...] = jnp.where(left_lanes, straight[:half], crossed[half:])
    to_near[...] = jnp.where(left_lanes, crossed[:half], straight[half:])


def gathered(place, spread, far, near):
    even = is_even(place, 0, spread.shape)
    far, near = far[...], near[...]
    left_lanes = lanes(far.shape)
    far_turned, near_turned = swap_halves(far), swap_halves(near)
    straight = jnp.concatenate(
        [jnp.where(left_lanes, far, near_turned), jnp.where(left_lanes, far_turned, near)], 0
    )
    crossed = jnp.concatenate(
        [jnp.where(left_lanes, near, far_turned), jnp.where(left_lanes, near_turned, far)], 0
    )
    return spread[...] + jnp.where(even, straight, crossed)


def stepped(params, grad):
    field = sigmoid(sharpness * params)
    return params - step_size * sharpness * field * (1.0 - field) * grad


def masked(place, tile, whole, params, col_offset):
    first_col = place[1:2, :128] * tile[1] + col_offset
    first_row = place[0:1, :128] * tile[0] - H
    inside = window(params.shape, first_col, first_row, whole[1], whole[0])
    return jnp.where(inside, sigmoid(sharpness * params), 0.0)


def field_window(geo, place, tile, whole, col_offset):
    middle = place[1:2, :128] * tile[1] + col_offset + H + geo.centre
    step = lax.broadcasted_iota(jnp.int32, (geo.half_up, 128), 0)
    return [(col >= 0) & (col < whole[1]) for col in (middle + step, middle - 1 - step)]


def first_kernel(
    geo, tile, whole, place, weights, own, target, first, second, spec, mirror, *rest
):
    tabs = dict(zip(STEP_TABLES, rest))
    rest = rest[len(STEP_TABLES) :]
    spread, to_far, to_near, params_out, goal_out, params, goal, fields = rest
    cols = own.shape[0]
    right_first = is_even(place, 1, first.shape)
    left = jnp.where(right_first, second[...], first[...])
    right = jnp.where(right_first, first[...], second[...])
    params[...] = jnp.zeros_like(params)
    params[0:128, :] = left[0:128, :]
    params[128 : 128 + cols, :] = own[...]
    params[128 + cols : 256 + cols, :] = right[0:128, :]
    left_lanes = lanes((48, 128))
    goal[...] = jnp.zeros_like(goal)
    for start, side in ((0, left), (96 + cols, right)):
        packed = side[128:176, :]
        turned = swap_halves(packed)
        goal[start : start + 48, :] = jnp.where(left_lanes, packed, turned)
        goal[start + 48 : start + 96, :] = jnp.where(left_lanes, turned, packed)
    goal[96 : 96 + cols, :] = target[...]
    goals = [
        goal[geo.centre : geo.centre + geo.half_up, :],
        dot(mirror[...], goal[0 : mirror.shape[1], :].astype(bf16)),
    ]
    for side in (0, 1):
        goal_out[side] = goals[side][: goal_out.shape[1]]
    params_out[...] = params[64 : 64 + params_out.shape[0], :]
    mask = masked(place, tile, whole, params[...], -128)
    inside = field_window(geo, place, tile, whole, -128)
    _, grad = one_step(geo, mask, goals, inside, weights, spec, tabs, fields)
    spread_out(place, grad, spread, to_far, to_near)


def second_kernel(geo, tile, whole, place, weights, own, far, near, old, goal, spec, *rest):
    tabs = dict(zip(STEP_TABLES, rest))
    spread, to_far, to_near, params_out, fields = rest[len(STEP_TABLES) :]
    params = stepped(old[...], gathered(place, own, far, near))
    params_out[...] = params[64 : 64 + params_out.shape[0], :]
    mask = masked(place, tile, whole, params, -64)
    inside = field_window(geo, place, tile, whole, -64)
    goals = [goal[0], goal[1]]
    _, grad = one_step(geo, mask, goals, inside, weights, spec, tabs, fields)
    spread_out(place, grad, spread, to_far, to_near)


def update_kernel(cols, place, own, far, near, old, params, to_first, to_second):
    params[...] = stepped(old[...], gathered(place, own, far, near))
    right = is_even(place, 1, (64, 128))
    to_left, to_right = params[0:64, :], params[cols - 64 : cols, :]
    to_first[...] = jnp.where(right, to_right, to_left)
    to_second[...] = jnp.where(right, to_left, to_right)


def third_kernel(
    geo, tile, whole, place, weights, own, first, second, goal, spec, *rest
):
    tabs = dict(zip(STEP_TABLES, rest))
    rest = rest[len(STEP_TABLES) :]
    spread, to_far, to_near, intensity_out, params, fields = rest
    cols = tile[1]
    right_first = is_even(place, 1, (64, 128))
    params[...] = jnp.zeros_like(params)
    params[0:64, :] = jnp.where(right_first, second[...], first[...])
    params[64 : 64 + cols, :] = own[0:cols, :]
    params[64 + cols : 128 + cols, :] = jnp.where(right_first, first[...], second[...])
    mask = masked(place, tile, whole, params[...], -64)
    inside = field_window(geo, place, tile, whole, -64)
    goals = [goal[0], goal[1]]
    intensity, grad = one_step(geo, mask, goals, inside, weights, spec, tabs, fields)
    spread_out(place, grad, spread, to_far, to_near)
    for side in (0, 1):
        intensity_out[side] = intensity[side]


def intensity_kernel(cols, intensity, mirror, out, flat):
    high, low = split(intensity[1])
    rest = (intensity[1] - high.astype(f32) - low.astype(f32)).astype(bf16)
    turned = dot(mirror[...], high) + (dot(mirror[...], low) + dot(mirror[...], rest))
    flat[...] = jnp.zeros_like(flat)
    flat[0 : cols // 2, :] = turned[0 : cols // 2]
    flat[cols // 2 : cols, :] = intensity[0][0 : cols // 2]
    out[...] = flat[...].T[:64, :cols]


def final_kernel(cols, place, own, far, near, out, wide):
    wide[...] = jnp.zeros_like(wide)
    wide[0 : own.shape[0], :] = gathered(place, own, far, near)
    out[...] = wide[...].T[H : H + 64, :cols]


def mirror_table(rows, rows_up, cols_up):
    table = np.zeros((rows_up, cols_up), np.float32)
    table[np.arange(rows), rows - 1 - np.arange(rows)] = 1.0
    return table.astype(ml_dtypes.bfloat16)


def call(kernel, name, out_shapes, scratch, args, space=pltpu.VMEM):
    return pl.pallas_call(
        kernel,
        name=name,
        out_shape=[
            shape if isinstance(shape, jax.ShapeDtypeStruct) else pltpu.VMEM(shape, f32)
            for shape in out_shapes
        ],
        in_specs=[pl.BlockSpec(memory_space=pltpu.VMEM)] * len(args),
        out_specs=[pl.BlockSpec(memory_space=pltpu.VMEM)] * len(out_shapes),
        scratch_shapes=[pltpu.VMEM(shape, f32) for shape in scratch],
        compiler_params=pltpu.CompilerParams(vmem_limit_bytes=VMEM_LIMIT),
    )(*[pltpu.with_memory_space_constraint(arg, space) for arg in args])


def per_device(rows, cols, mask_params, target_bits, kern_real, kern_imag, socs_weights):
    tile = mask_params.shape
    whole = (tile[0] * rows, tile[1] * cols)
    kernels = kern_real.shape[1] // KS
    axis = lax.broadcasted_iota(jnp.int32, (8, 256), 0)
    place = jnp.where(axis == 0, lax.axis_index("row"), lax.axis_index("col"))
    weights = jnp.broadcast_to(socs_weights[:, None], (kernels, 128))

    def swaps(count, start):
        pairs = [(i, i + 1) for i in range(start, count - 1, 2)]
        return pairs + [(b, a) for a, b in pairs]

    def row_exchange(to_far, to_near):
        far = lax.ppermute(to_far, "row", swaps(rows, 1))
        return far, lax.ppermute(to_near, "row", swaps(rows, 0))

    def col_exchange(to_first, to_second):
        first = lax.ppermute(to_first, "col", swaps(cols, 0))
        return first, lax.ppermute(to_second, "col", swaps(cols, 1))

    wide, slim = Geometry(tile[1] + 8 * H, 1), Geometry(tile[1] + 4 * H, 0)
    shared = row_tables()
    shared["wide_mirror"] = mirror_table(wide.centre, wide.half_up, wide.half_up)
    shared["slim_mirror"] = mirror_table(tile[1] // 2, up(tile[1] // 2, 16), slim.half_up)
    n = tile[1]
    far, near = row_exchange(mask_params, mask_params)
    params, target = call(
        early_kernel,
        "early",
        [(n, 128), (n, 128)],
        [(128, 256)],
        [mask_params, target_bits.T],
        pltpu.HBM,
    )
    params, to_first, to_second = call(
        prep_kernel,
        "prep",
        [(n, 128), (176, 128), (176, 128)],
        [(128, 256)],
        [place, params, target, far, near],
    )
    first, second = col_exchange(to_first, to_second)
    made = {"wide": wide.tables(), "slim": slim.tables(), "shared": shared}
    place_of = {}

    def loader(kernel, name, geo, out_shapes, inputs, spaces, names):
        tables = [jnp.asarray(made[label][part]) for label, part in names]
        arrays = list(zip(inputs + tables, spaces + [pltpu.HBM] * len(tables)))
        outs = pl.pallas_call(
            functools.partial(kernel, geo, len(tables)),
            name=name,
            out_shape=[pltpu.VMEM(shape, f32) for shape in out_shapes]
            + [pltpu.VMEM(table.shape, table.dtype) for table in tables],
            in_specs=[pl.BlockSpec(memory_space=pltpu.VMEM)] * len(inputs)
            + [pl.BlockSpec(memory_space=pltpu.HBM)] * len(tables),
            out_specs=[pl.BlockSpec(memory_space=pltpu.VMEM)]
            * (len(out_shapes) + len(tables)),
            scratch_shapes=[pltpu.SemaphoreType.DMA((len(tables),))],
            compiler_params=pltpu.CompilerParams(vmem_limit_bytes=VMEM_LIMIT),
        )(*[pltpu.with_memory_space_constraint(*pair) for pair in arrays])
        place_of.update(zip(names, outs[len(out_shapes) :]))
        return outs[: len(out_shapes)]

    half_spec, wide_spec = loader(
        setup_kernel,
        "spectra",
        wide,
        [(kernels * KS, 512), (2 * kernels * wide.freqs_up, 256)],
        [
            kern_real,
            kern_imag,
            jnp.asarray(shared["tap_rows"]),
            jnp.asarray(made["wide"]["tap_cols"]),
        ],
        [pltpu.HBM] * 4,
        [("wide", part) for part in COLUMN_TABLES]
        + [("shared", part) for part in ROW_TABLES + ("wide_mirror",)],
    )

    def tabs(label):
        return [place_of[label, name] for name in COLUMN_TABLES] + [
            place_of["shared", name] for name in ROW_TABLES
        ]

    def spreads(geo):
        return [(geo.grad_up, 128)] + [(geo.grad_up // 2, 128)] * 2

    def fields(geo):
        return (2, kernels, geo.half_up, 128)

    spread, to_far, to_near, params, goal = call(
        functools.partial(first_kernel, wide, tile, whole),
        "first",
        spreads(wide) + [(slim.mask_up, 128), (2, slim.half_up, 128)],
        [(wide.mask_up, 128), (wide.centre + wide.half_up, 128), fields(wide)],
        [place, weights, params, target, first, second, wide_spec]
        + [place_of["shared", "wide_mirror"], *tabs("wide")],
    )
    far, near = row_exchange(to_far, to_near)
    (slim_spec,) = loader(
        slim_kernel,
        "slim",
        slim,
        [(2 * kernels * slim.freqs_up, 256)],
        [half_spec, jnp.asarray(made["slim"]["tap_cols"])],
        [pltpu.VMEM, pltpu.HBM],
        [("slim", part) for part in COLUMN_TABLES] + [("shared", "slim_mirror")],
    )
    spread, to_far, to_near, params = call(
        functools.partial(second_kernel, slim, tile, whole),
        "second",
        spreads(slim) + [(slim.grad_up, 128)],
        [fields(slim)],
        [place, weights, spread, far, near, params, goal, slim_spec, *tabs("slim")],
    )
    far, near = row_exchange(to_far, to_near)
    params, to_first, to_second = call(
        functools.partial(update_kernel, n),
        "update",
        [(slim.grad_up, 128), (64, 128), (64, 128)],
        [],
        [place, spread, far, near, params],
    )
    first, second = col_exchange(to_first, to_second)
    spread, to_far, to_near, intensity = call(
        functools.partial(third_kernel, slim, tile, whole),
        "third",
        spreads(slim) + [(2, slim.half_up, 128)],
        [(slim.mask_up, 128), fields(slim)],
        [place, weights, params, first, second, goal, slim_spec, *tabs("slim")],
    )
    far, near = row_exchange(to_far, to_near)
    (intensity,) = call(
        functools.partial(intensity_kernel, n),
        "intensity",
        [jax.ShapeDtypeStruct(tile, f32)],
        [(256, 128)],
        [intensity, place_of["shared", "slim_mirror"]],
    )
    (mask_grad,) = call(
        functools.partial(final_kernel, n),
        "final",
        [jax.ShapeDtypeStruct(tile, f32)],
        [(256, 128)],
        [place, spread, far, near],
    )
    return mask_grad, intensity


def solution(mesh):
    placed = (P("row", "col"), P("row", "col"), P(), P(), P())
    return jax.shard_map(
        functools.partial(per_device, mesh.shape["row"], mesh.shape["col"]),
        mesh=mesh,
        in_specs=placed,
        out_specs=(P("row", "col"), P("row", "col")),
        check_vma=False,
    )
```

```python
import functools
import math

import jax
import jax.numpy as jnp
import ml_dtypes
import numpy as np
from jax import lax
from jax.experimental import pallas as pl
from jax.experimental.pallas import tpu as pltpu
from jax.sharding import PartitionSpec as P

H = 32
KS = 64
ITERS = 3
ROWS = 128
sharpness = 2.0
steepness = 4.0
threshold = 0.8
step_size = 1.0
f32 = jnp.float32
bf16 = jnp.bfloat16
VMEM_LIMIT = 28 * 1024 * 1024


def up(value, unit):
    return -(-value // unit) * unit


def halves(table):
    table = table.astype(np.float32)
    high = table.astype(ml_dtypes.bfloat16)
    low = (table - high.astype(np.float32)).astype(ml_dtypes.bfloat16)
    return high, low


def angles(left, right, length):
    product = np.outer(left.astype(np.int64), right.astype(np.int64)) % length
    return product * (2.0 * math.pi / length)


def grown(table, rows, cols):
    return np.pad(table, [(0, rows - table.shape[0]), (0, cols - table.shape[1])])


def left_stack(table):
    high, low = halves(table)
    return np.concatenate([high, high, low], 1)


def right_stack(table):
    high, low = halves(table)
    return np.concatenate([high, high, low], 0)


class Geometry:
    def __init__(self, width, trim):
        self.mask = width
        self.centre = width // 2 - H
        self.half = self.centre - trim
        self.grad = width - 4 * H
        self.length = width | 1
        self.freqs = (self.length + 1) // 2
        self.freqs_up = up(self.freqs, 16)
        self.mask_up = up(self.mask, 16)
        self.half_up = up(self.half, 16)
        self.grad_up = up(self.grad, 32)

    def dense(self):
        return 3 * self.half <= 512 < 3 * self.half_up

    def source_stack(self, table):
        table = grown(table, self.freqs_up, self.half_up)
        if not self.dense():
            return left_stack(table)
        high, low = halves(table)
        first, second = high.copy(), high.copy()
        fit = 512 - 2 * self.half_up
        spare = self.half_up - self.half
        rest = self.half - fit
        first[:, self.half :] = low[:, fit : fit + spare]
        second[:, self.half : self.half + rest - spare] = low[:, fit + spare : self.half]
        return np.concatenate([first, second, low[:, :fit]], 1)

    def tables(self):
        freq = np.arange(self.freqs)
        fu, hu = self.freqs_up, self.half_up
        middle = H + self.centre - 0.5
        weight = np.where(freq == 0, 1.0, 2.0) / (self.length * ROWS)

        def phases(places):
            return angles(freq, np.round(2 * places), 2 * self.length)

        def complex_table(phase, sign, rows, cols, axis):
            parts = [grown(np.cos(phase), rows, cols), grown(sign * np.sin(phase), rows, cols)]
            return np.concatenate(parts, axis)

        mask = phases(np.arange(self.mask) - middle)
        half = phases(np.arange(self.half) + 0.5)
        grad = phases(np.arange(self.grad) + 2 * H - middle)
        taps = phases(np.arange(KS) - H)
        grad_table = np.concatenate(
            [
                grown((np.cos(grad) * weight[:, None]).T, self.grad_up, fu),
                grown((-np.sin(grad) * weight[:, None]).T, self.grad_up, fu),
            ],
            1,
        )
        return dict(
            mask_cols=left_stack(complex_table(mask, -1.0, fu, self.mask_up, 0)),
            field_even=left_stack(grown((np.cos(half) * weight[:, None]).T, hu, fu)),
            field_odd=left_stack(grown((np.sin(half) * weight[:, None]).T, hu, fu)),
            source_even=self.source_stack(np.cos(half)),
            source_odd=self.source_stack(-np.sin(half)),
            grad_cols=left_stack(grad_table),
            tap_cols=left_stack(complex_table(taps, 1.0, fu, KS, 1)),
        )


def row_tables():
    freq = np.arange(ROWS)

    def complex_table(phase, sign):
        cos, sin = np.cos(phase), sign * np.sin(phase)
        return np.block([[cos, sin], [-sin, cos]])

    def side(table):
        high, low = halves(table)
        return np.concatenate([high, low], 1)

    places = np.arange(64) + H
    field = complex_table(angles(freq, places, ROWS), 1.0)
    field_swapped = np.concatenate([field[:, 64:], field[:, :64]], 1)
    source = complex_table(angles(np.arange(64), freq, ROWS), -1.0)
    source_swapped = np.concatenate([source[64:], source[:64]], 0)
    taps = angles(np.arange(KS) - H, freq, ROWS)
    tap = np.concatenate([np.cos(taps), -np.sin(taps)], 1)
    zero = np.zeros_like(tap)
    return dict(
        mask_rows=right_stack(complex_table(angles(freq, freq, ROWS), -1.0)),
        field_rows=side(field),
        field_rows_swapped=side(field_swapped),
        source_rows=right_stack(source),
        source_rows_swapped=right_stack(source_swapped),
        grad_rows=right_stack(complex_table(angles(freq, freq - H, ROWS), 1.0)),
        tap_rows=right_stack(np.block([[tap, zero], [zero, tap]])),
    )


def split(value):
    high = value.astype(bf16)
    return high, (value - high.astype(f32)).astype(bf16)


def dot(left, right):
    return lax.dot_general(
        left, right, (((1,), (0,)), ((), ())), preferred_element_type=f32
    )


def chunks(count, parts):
    units = count // 16
    edges = [16 * (units * i // parts) for i in range(parts + 1)]
    return list(zip(edges[:-1], edges[1:]))


def left_dot(table, value, parts=1):
    high, low = split(value)
    stacked = jnp.concatenate([high, low, high], 0)
    rows = [table[a:b, :] for a, b in chunks(table.shape[0], parts)]
    return jnp.concatenate([dot(part, stacked) for part in rows], 0)


def source_dot(geo, table, value):
    if not geo.dense():
        return left_dot(table[...], value)
    fit = 512 - 2 * geo.half_up
    spare = geo.half_up - geo.half
    high, low = split(value)
    tail_high, tail_low = high[fit:].astype(f32)[: geo.half - fit], low[fit:].astype(f32)
    first = jnp.concatenate([tail_high, tail_high[:spare]], 0).astype(bf16)
    rest = tail_high[spare:]
    blank = jnp.zeros((spare - rest.shape[0], value.shape[1]), f32)
    second = jnp.concatenate([tail_low[: geo.half - fit], rest, blank], 0).astype(bf16)
    stacked = jnp.concatenate([high[:fit], first, low[:fit], second, high[:fit]], 0)
    return dot(table[...], stacked)


def right_dot(value, table, parts=1):
    high, low = split(value)
    stacked = jnp.concatenate([high, low, high], 1)
    rows = [stacked[a:b] for a, b in chunks(value.shape[0], parts)]
    return jnp.concatenate([dot(part, table) for part in rows], 0)


def sigmoid(value):
    return 1.0 / (1.0 + jnp.exp(-value))


def swap_halves(value):
    return pltpu.roll(value, 64, 1)


def is_even(place, axis, shape):
    return jnp.broadcast_to(place[axis : axis + 1, : shape[1]], shape) % 2 == 0


def window(shape, first_col, first_row, whole_cols, whole_rows):
    col = lax.broadcasted_iota(jnp.int32, shape, 0) + first_col
    row = lax.broadcasted_iota(jnp.int32, shape, 1) + first_row
    return (col >= 0) & (col < whole_cols) & (row >= 0) & (row < whole_rows)


def column_spectra(geo, half, table, out):
    count = geo.freqs_up
    for k in range(out.shape[0] // (2 * count)):
        part = half[k * KS : (k + 1) * KS, :]
        turned = jnp.concatenate(
            [part[:, 128:256], -part[:, 0:128], part[:, 384:512], -part[:, 256:384]], 1
        )
        spec = left_dot(table[...], jnp.concatenate([part, turned], 0))
        out[2 * k * count : (2 * k + 1) * count, :] = spec[:, :256]
        out[(2 * k + 1) * count : (2 * k + 2) * count, :] = spec[:, 256:]


def bring(sources, targets, sems):
    copies = [
        pltpu.make_async_copy(source, target, sems.at[index])
        for index, (source, target) in enumerate(zip(sources, targets))
    ]
    for copy in copies:
        copy.start()
    return copies


def setup_kernel(geo, held, kern_real, kern_imag, tap_rows, tap_cols, *rest):
    sources, (half, out), rest = rest[:held], rest[held : held + 2], rest[held + 2 :]
    copies = bring(sources, rest[:held], rest[held])
    both = jnp.concatenate([kern_real[...], kern_imag[...]], 0)
    for start in range(0, both.shape[1], 128):
        part = both[:, start : start + 128].T
        half[start : start + 128, :] = right_dot(part, tap_rows[...])
    column_spectra(geo, half, tap_cols, out)
    for copy in copies:
        copy.wait()


def slim_kernel(geo, held, half, tap_cols, *rest):
    sources, out, rest = rest[:held], rest[held], rest[held + 1 :]
    copies = bring(sources, rest[:held], rest[held])
    column_spectra(geo, half, tap_cols, out)
    for copy in copies:
        copy.wait()


def one_step(geo, mask, target, inside, weights, spec, tabs, fields):
    count = geo.freqs_up
    kernels = fields.shape[1]
    across = left_dot(tabs["mask_cols"], mask, 2)
    mask_spec = right_dot(
        jnp.concatenate([across[:count], across[count:]], 1), tabs["mask_rows"][...], 2
    )

    def place(index, start, stop):
        value = spec[index * count + start : index * count + stop, :]
        return value[:, :128], value[:, 128:]

    evens, odds = [], []
    for start, stop in chunks(count, 1):
        size = stop - start
        lane = lanes((size, 128))
        mask_re, mask_im = mask_spec[start:stop, :128], mask_spec[start:stop, 128:]

        def down(indices, table):
            products = []
            for index in indices:
                re, im = place(index, start, stop)
                products.append(
                    jnp.concatenate(
                        [re * mask_re - im * mask_im, re * mask_im + im * mask_re], 1
                    )
                )
            high, low = split(jnp.concatenate(products, 0))
            wide = dot(high, table[...])
            got = wide[:, :128] + wide[:, 128:] + dot(low, table[:, :128])
            return [got[i * size : (i + 1) * size] for i in range(len(indices))]

        firsts = down(range(0, 2 * kernels, 2), tabs["field_rows"])
        seconds = down(range(1, 2 * kernels, 2), tabs["field_rows_swapped"])
        pairs = list(zip(firsts, seconds))
        evens.append(jnp.concatenate([jnp.where(lane, a, b) for a, b in pairs], 1))
        odds.append(
            jnp.concatenate([swap_halves(jnp.where(lane, b, a)) for a, b in pairs], 1)
        )
    even = left_dot(tabs["field_even"][...], jnp.concatenate(evens, 0))
    odd = left_dot(tabs["field_odd"][...], jnp.concatenate(odds, 0))
    zero = jnp.zeros((geo.half_up, 128), f32)
    intensity = [zero, zero]
    for side, field in enumerate((even - odd, even + odd)):
        for j in range(kernels):
            own = field[:, j * 128 : (j + 1) * 128]
            fields[side, j] = own
            intensity[side] = intensity[side] + weights[j : j + 1, :] * (own * own)
    cotangent = []
    for side in (0, 1):
        intensity[side] = intensity[side] + swap_halves(intensity[side])
        resist = sigmoid(steepness * (intensity[side] - threshold))
        slope = 2.0 * (resist - target[side]) * steepness * resist * (1.0 - resist)
        cotangent.append(jnp.where(inside[side], slope, 0.0))
    right, left = (
        jnp.concatenate(
            [
                (2.0 * weights[j : j + 1, :] * cotangent[side]) * fields[side, j]
                for j in range(kernels)
            ],
            1,
        )
        for side in (0, 1)
    )
    even = source_dot(geo, tabs["source_even"], right + left)
    odd = source_dot(geo, tabs["source_odd"], right - left)
    totals = []
    for start, stop in chunks(count, 2):
        size = stop - start
        lane = lanes((size, 128))
        res = [even[start:stop, j * 128 : (j + 1) * 128] for j in range(kernels)]
        ims = [swap_halves(odd[start:stop, j * 128 : (j + 1) * 128]) for j in range(kernels)]
        total_re = jnp.zeros((size, 128), f32)
        total_im = jnp.zeros((size, 128), f32)
        for index, values, table in (
            (0, [jnp.where(lane, a, b) for a, b in zip(res, ims)], tabs["source_rows"]),
            (1, [jnp.where(lane, b, a) for a, b in zip(res, ims)], tabs["source_rows_swapped"]),
        ):
            got = right_dot(jnp.concatenate(values, 0), table[...])
            for j in range(kernels):
                got_re = got[j * size : (j + 1) * size, :128]
                got_im = got[j * size : (j + 1) * size, 128:]
                re, im = place(2 * j + index, start, stop)
                total_re = total_re + (re * got_re + im * got_im)
                total_im = total_im + (re * got_im - im * got_re)
        totals.append(jnp.concatenate([total_re, total_im], 1))
    back = right_dot(jnp.concatenate(totals, 0), tabs["grad_rows"][...], 2)
    grad = left_dot(
        tabs["grad_cols"], jnp.concatenate([back[:, :128], back[:, 128:]], 0), 2
    )
    return intensity, grad


COLUMN_TABLES = (
    "mask_cols",
    "field_even",
    "field_odd",
    "source_even",
    "source_odd",
    "grad_cols",
)
ROW_TABLES = (
    "mask_rows",
    "field_rows",
    "field_rows_swapped",
    "source_rows",
    "source_rows_swapped",
    "grad_rows",
)
STEP_TABLES = COLUMN_TABLES + ROW_TABLES


def lanes(shape):
    return lax.broadcasted_iota(jnp.int32, shape, 1) < 64


def early_kernel(own, bits, params, target, tall):
    cols = own.shape[1]
    tall[...] = jnp.zeros_like(tall)
    tall[32:96, :cols] = own[...]
    params[...] = tall[...].T[:cols]
    words = bits.shape[0]
    width = cols // words
    shift = lax.broadcasted_iota(jnp.int32, (width, 128), 0)
    for index in range(words):
        word = bits[index : index + 1, :]
        word = jnp.broadcast_to(jnp.concatenate([word, word], 1), (width, 128))
        bit = jnp.bitwise_and(jnp.right_shift(word, shift), 1).astype(f32)
        target[index * width : (index + 1) * width, :] = bit


def prep_kernel(place, own, target, across, within, params, to_first, to_second, tall):
    even = is_even(place, 0, (32, own.shape[0]))
    cols = own.shape[0]
    tall[...] = jnp.zeros_like(tall)
    tall[0:32, :cols] = jnp.where(even, across[32:64, :], within[32:64, :])
    tall[96:128, :cols] = jnp.where(even, within[0:32, :], across[0:32, :])
    params[...] = own[...] + tall[...].T[:cols]
    right = is_even(place, 1, (176, 128))
    left_lanes = lanes((48, 128))

    def packed(start):
        return jnp.where(left_lanes, target[start : start + 48], target[start + 48 : start + 96])

    to_left = jnp.concatenate([params[0:128, :], packed(0)], 0)
    to_right = jnp.concatenate([params[cols - 128 : cols, :], packed(cols - 96)], 0)
    to_first[...] = jnp.where(right, to_right, to_left)
    to_second[...] = jnp.where(right, to_left, to_right)


def spread_out(place, grad, spread, to_far, to_near):
    even = is_even(place, 0, grad.shape)
    half = to_far.shape[0]
    spread[...] = grad
    turned = swap_halves(grad)
    straight = jnp.where(even, grad, turned)
    crossed = jnp.where(even, turned, grad)
    left_lanes = lanes((half, 128))
    to_far[...] = jnp.where(left_lanes, straight[:half], crossed[half:])
    to_near[...] = jnp.where(left_lanes, crossed[:half], straight[half:])


def gathered(place, spread, far, near):
    even = is_even(place, 0, spread.shape)
    far, near = far[...], near[...]
    left_lanes = lanes(far.shape)
    far_turned, near_turned = swap_halves(far), swap_halves(near)
    straight = jnp.concatenate(
        [jnp.where(left_lanes, far, near_turned), jnp.where(left_lanes, far_turned, near)], 0
    )
    crossed = jnp.concatenate(
        [jnp.where(left_lanes, near, far_turned), jnp.where(left_lanes, near_turned, far)], 0
    )
    return spread[...] + jnp.where(even, straight, crossed)


def stepped(params, grad):
    field = sigmoid(sharpness * params)
    return params - step_size * sharpness * field * (1.0 - field) * grad


def masked(place, tile, whole, params, col_offset):
    first_col = place[1:2, :128] * tile[1] + col_offset
    first_row = place[0:1, :128] * tile[0] - H
    inside = window(params.shape, first_col, first_row, whole[1], whole[0])
    return jnp.where(inside, sigmoid(sharpness * params), 0.0)


def field_window(geo, place, tile, whole, col_offset):
    middle = place[1:2, :128] * tile[1] + col_offset + H + geo.centre
    step = lax.broadcasted_iota(jnp.int32, (geo.half_up, 128), 0)
    return [(col >= 0) & (col < whole[1]) for col in (middle + step, middle - 1 - step)]


def first_kernel(
    geo, tile, whole, place, weights, own, target, first, second, spec, mirror, *rest
):
    tabs = dict(zip(STEP_TABLES, rest))
    rest = rest[len(STEP_TABLES) :]
    spread, to_far, to_near, params_out, goal_out, params, goal, fields = rest
    cols = own.shape[0]
    right_first = is_even(place, 1, first.shape)
    left = jnp.where(right_first, second[...], first[...])
    right = jnp.where(right_first, first[...], second[...])
    params[...] = jnp.zeros_like(params)
    params[0:128, :] = left[0:128, :]
    params[128 : 128 + cols, :] = own[...]
    params[128 + cols : 256 + cols, :] = right[0:128, :]
    left_lanes = lanes((48, 128))
    goal[...] = jnp.zeros_like(goal)
    for start, side in ((0, left), (96 + cols, right)):
        packed = side[128:176, :]
        turned = swap_halves(packed)
        goal[start : start + 48, :] = jnp.where(left_lanes, packed, turned)
        goal[start + 48 : start + 96, :] = jnp.where(left_lanes, turned, packed)
    goal[96 : 96 + cols, :] = target[...]
    goals = [
        goal[geo.centre : geo.centre + geo.half_up, :],
        dot(mirror[...], goal[0 : mirror.shape[1], :].astype(bf16)),
    ]
    for side in (0, 1):
        goal_out[side] = goals[side][: goal_out.shape[1]]
    params_out[...] = params[64 : 64 + params_out.shape[0], :]
    mask = masked(place, tile, whole, params[...], -128)
    inside = field_window(geo, place, tile, whole, -128)
    _, grad = one_step(geo, mask, goals, inside, weights, spec, tabs, fields)
    spread_out(place, grad, spread, to_far, to_near)


def second_kernel(geo, tile, whole, place, weights, own, far, near, old, goal, spec, *rest):
    tabs = dict(zip(STEP_TABLES, rest))
    spread, to_far, to_near, params_out, fields = rest[len(STEP_TABLES) :]
    params = stepped(old[...], gathered(place, own, far, near))
    params_out[...] = params[64 : 64 + params_out.shape[0], :]
    mask = masked(place, tile, whole, params, -64)
    inside = field_window(geo, place, tile, whole, -64)
    goals = [goal[0], goal[1]]
    _, grad = one_step(geo, mask, goals, inside, weights, spec, tabs, fields)
    spread_out(place, grad, spread, to_far, to_near)


def update_kernel(cols, place, own, far, near, old, params, to_first, to_second):
    params[...] = stepped(old[...], gathered(place, own, far, near))
    right = is_even(place, 1, (64, 128))
    to_left, to_right = params[0:64, :], params[cols - 64 : cols, :]
    to_first[...] = jnp.where(right, to_right, to_left)
    to_second[...] = jnp.where(right, to_left, to_right)


def third_kernel(
    geo, tile, whole, place, weights, own, first, second, goal, spec, *rest
):
    tabs = dict(zip(STEP_TABLES, rest))
    rest = rest[len(STEP_TABLES) :]
    spread, to_far, to_near, intensity_out, params, fields = rest
    cols = tile[1]
    right_first = is_even(place, 1, (64, 128))
    params[...] = jnp.zeros_like(params)
    params[0:64, :] = jnp.where(right_first, second[...], first[...])
    params[64 : 64 + cols, :] = own[0:cols, :]
    params[64 + cols : 128 + cols, :] = jnp.where(right_first, first[...], second[...])
    mask = masked(place, tile, whole, params[...], -64)
    inside = field_window(geo, place, tile, whole, -64)
    goals = [goal[0], goal[1]]
    intensity, grad = one_step(geo, mask, goals, inside, weights, spec, tabs, fields)
    spread_out(place, grad, spread, to_far, to_near)
    for side in (0, 1):
        intensity_out[side] = intensity[side]


def intensity_kernel(cols, intensity, mirror, out, flat):
    high, low = split(intensity[1])
    rest = (intensity[1] - high.astype(f32) - low.astype(f32)).astype(bf16)
    turned = dot(mirror[...], high) + (dot(mirror[...], low) + dot(mirror[...], rest))
    flat[...] = jnp.zeros_like(flat)
    flat[0 : cols // 2, :] = turned[0 : cols // 2]
    flat[cols // 2 : cols, :] = intensity[0][0 : cols // 2]
    out[...] = flat[...].T[:64, :cols]


def final_kernel(cols, place, own, far, near, out, wide):
    wide[...] = jnp.zeros_like(wide)
    wide[0 : own.shape[0], :] = gathered(place, own, far, near)
    out[...] = wide[...].T[H : H + 64, :cols]


def mirror_table(rows, rows_up, cols_up):
    table = np.zeros((rows_up, cols_up), np.float32)
    table[np.arange(rows), rows - 1 - np.arange(rows)] = 1.0
    return table.astype(ml_dtypes.bfloat16)


def call(kernel, name, out_shapes, scratch, args, space=pltpu.VMEM):
    return pl.pallas_call(
        kernel,
        name=name,
        out_shape=[
            shape if isinstance(shape, jax.ShapeDtypeStruct) else pltpu.VMEM(shape, f32)
            for shape in out_shapes
        ],
        in_specs=[pl.BlockSpec(memory_space=pltpu.VMEM)] * len(args),
        out_specs=[pl.BlockSpec(memory_space=pltpu.VMEM)] * len(out_shapes),
        scratch_shapes=[pltpu.VMEM(shape, f32) for shape in scratch],
        compiler_params=pltpu.CompilerParams(vmem_limit_bytes=VMEM_LIMIT),
    )(*[pltpu.with_memory_space_constraint(arg, space) for arg in args])


def per_device(rows, cols, mask_params, target_bits, kern_real, kern_imag, socs_weights):
    tile = mask_params.shape
    whole = (tile[0] * rows, tile[1] * cols)
    kernels = kern_real.shape[1] // KS
    axis = lax.broadcasted_iota(jnp.int32, (8, 256), 0)
    place = jnp.where(axis == 0, lax.axis_index("row"), lax.axis_index("col"))
    weights = jnp.broadcast_to(socs_weights[:, None], (kernels, 128))

    def swaps(count, start):
        pairs = [(i, i + 1) for i in range(start, count - 1, 2)]
        return pairs + [(b, a) for a, b in pairs]

    def row_exchange(to_far, to_near):
        far = lax.ppermute(to_far, "row", swaps(rows, 1))
        return far, lax.ppermute(to_near, "row", swaps(rows, 0))

    def col_exchange(to_first, to_second):
        first = lax.ppermute(to_first, "col", swaps(cols, 0))
        return first, lax.ppermute(to_second, "col", swaps(cols, 1))

    wide, slim = Geometry(tile[1] + 8 * H, 1), Geometry(tile[1] + 4 * H, 0)
    shared = row_tables()
    shared["wide_mirror"] = mirror_table(wide.centre, wide.half_up, wide.half_up)
    shared["slim_mirror"] = mirror_table(tile[1] // 2, up(tile[1] // 2, 16), slim.half_up)
    n = tile[1]
    far, near = row_exchange(mask_params, mask_params)
    params, target = call(
        early_kernel,
        "early",
        [(n, 128), (n, 128)],
        [(128, 256)],
        [mask_params, target_bits.T],
        pltpu.HBM,
    )
    near, place, weights = lax.optimization_barrier((near, place, weights))
    params, to_first, to_second = call(
        prep_kernel,
        "prep",
        [(n, 128), (176, 128), (176, 128)],
        [(128, 256)],
        [place, params, target, far, near],
    )
    first, second = col_exchange(to_first, to_second)
    made = {"wide": wide.tables(), "slim": slim.tables(), "shared": shared}
    place_of = {}

    def loader(kernel, name, geo, out_shapes, inputs, spaces, names):
        tables = [jnp.asarray(made[label][part]) for label, part in names]
        arrays = list(zip(inputs + tables, spaces + [pltpu.HBM] * len(tables)))
        outs = pl.pallas_call(
            functools.partial(kernel, geo, len(tables)),
            name=name,
            out_shape=[pltpu.VMEM(shape, f32) for shape in out_shapes]
            + [pltpu.VMEM(table.shape, table.dtype) for table in tables],
            in_specs=[pl.BlockSpec(memory_space=pltpu.VMEM)] * len(inputs)
            + [pl.BlockSpec(memory_space=pltpu.HBM)] * len(tables),
            out_specs=[pl.BlockSpec(memory_space=pltpu.VMEM)]
            * (len(out_shapes) + len(tables)),
            scratch_shapes=[pltpu.SemaphoreType.DMA((len(tables),))],
            compiler_params=pltpu.CompilerParams(vmem_limit_bytes=VMEM_LIMIT),
        )(*[pltpu.with_memory_space_constraint(*pair) for pair in arrays])
        place_of.update(zip(names, outs[len(out_shapes) :]))
        return outs[: len(out_shapes)]

    half_spec, wide_spec = loader(
        setup_kernel,
        "spectra",
        wide,
        [(kernels * KS, 512), (2 * kernels * wide.freqs_up, 256)],
        [
            kern_real,
            kern_imag,
            jnp.asarray(shared["tap_rows"]),
            jnp.asarray(made["wide"]["tap_cols"]),
        ],
        [pltpu.HBM] * 4,
        [("wide", part) for part in COLUMN_TABLES]
        + [("shared", part) for part in ROW_TABLES + ("wide_mirror",)],
    )

    def tabs(label):
        return [place_of[label, name] for name in COLUMN_TABLES] + [
            place_of["shared", name] for name in ROW_TABLES
        ]

    def spreads(geo):
        return [(geo.grad_up, 128)] + [(geo.grad_up // 2, 128)] * 2

    def fields(geo):
        return (2, kernels, geo.half_up, 128)

    spread, to_far, to_near, params, goal = call(
        functools.partial(first_kernel, wide, tile, whole),
        "first",
        spreads(wide) + [(slim.mask_up, 128), (2, slim.half_up, 128)],
        [(wide.mask_up, 128), (wide.centre + wide.half_up, 128), fields(wide)],
        [place, weights, params, target, first, second, wide_spec]
        + [place_of["shared", "wide_mirror"], *tabs("wide")],
    )
    far, near = row_exchange(to_far, to_near)
    (slim_spec,) = loader(
        slim_kernel,
        "slim",
        slim,
        [(2 * kernels * slim.freqs_up, 256)],
        [half_spec, jnp.asarray(made["slim"]["tap_cols"])],
        [pltpu.VMEM, pltpu.HBM],
        [("slim", part) for part in COLUMN_TABLES] + [("shared", "slim_mirror")],
    )
    spread, to_far, to_near, params = call(
        functools.partial(second_kernel, slim, tile, whole),
        "second",
        spreads(slim) + [(slim.grad_up, 128)],
        [fields(slim)],
        [place, weights, spread, far, near, params, goal, slim_spec, *tabs("slim")],
    )
    far, near = row_exchange(to_far, to_near)
    params, to_first, to_second = call(
        functools.partial(update_kernel, n),
        "update",
        [(slim.grad_up, 128), (64, 128), (64, 128)],
        [],
        [place, spread, far, near, params],
    )
    first, second = col_exchange(to_first, to_second)
    spread, to_far, to_near, intensity = call(
        functools.partial(third_kernel, slim, tile, whole),
        "third",
        spreads(slim) + [(2, slim.half_up, 128)],
        [(slim.mask_up, 128), fields(slim)],
        [place, weights, params, first, second, goal, slim_spec, *tabs("slim")],
    )
    far, near = row_exchange(to_far, to_near)
    (intensity,) = call(
        functools.partial(intensity_kernel, n),
        "intensity",
        [jax.ShapeDtypeStruct(tile, f32)],
        [(256, 128)],
        [intensity, place_of["shared", "slim_mirror"]],
    )
    (mask_grad,) = call(
        functools.partial(final_kernel, n),
        "final",
        [jax.ShapeDtypeStruct(tile, f32)],
        [(256, 128)],
        [place, spread, far, near],
    )
    return mask_grad, intensity


def solution(mesh):
    placed = (P("row", "col"), P("row", "col"), P(), P(), P())
    return jax.shard_map(
        functools.partial(per_device, mesh.shape["row"], mesh.shape["col"]),
        mesh=mesh,
        in_specs=placed,
        out_specs=(P("row", "col"), P("row", "col")),
        check_vma=False,
    )
```

```python
import functools
import math

import jax
import jax.numpy as jnp
import ml_dtypes
import numpy as np
from jax import lax
from jax.experimental import pallas as pl
from jax.experimental.pallas import tpu as pltpu
from jax.sharding import PartitionSpec as P

H = 32
KS = 64
ITERS = 3
ROWS = 128
sharpness = 2.0
steepness = 4.0
threshold = 0.8
step_size = 1.0
f32 = jnp.float32
bf16 = jnp.bfloat16
VMEM_LIMIT = 28 * 1024 * 1024


def up(value, unit):
    return -(-value // unit) * unit


def halves(table):
    table = table.astype(np.float32)
    high = table.astype(ml_dtypes.bfloat16)
    low = (table - high.astype(np.float32)).astype(ml_dtypes.bfloat16)
    return high, low


def angles(left, right, length):
    product = np.outer(left.astype(np.int64), right.astype(np.int64)) % length
    return product * (2.0 * math.pi / length)


def grown(table, rows, cols):
    return np.pad(table, [(0, rows - table.shape[0]), (0, cols - table.shape[1])])


def left_stack(table):
    high, low = halves(table)
    return np.concatenate([high, high, low], 1)


def right_stack(table):
    high, low = halves(table)
    return np.concatenate([high, high, low], 0)


class Geometry:
    def __init__(self, width, trim):
        self.mask = width
        self.centre = width // 2 - H
        self.half = self.centre - trim
        self.grad = width - 4 * H
        self.length = width | 1
        self.freqs = (self.length + 1) // 2
        self.freqs_up = up(self.freqs, 16)
        self.mask_up = up(self.mask, 16)
        self.half_up = up(self.half, 16)
        self.grad_up = up(self.grad, 32)

    def dense(self):
        return 3 * self.half <= 512 < 3 * self.half_up

    def source_stack(self, table):
        table = grown(table, self.freqs_up, self.half_up)
        if not self.dense():
            return left_stack(table)
        high, low = halves(table)
        first, second = high.copy(), high.copy()
        fit = 512 - 2 * self.half_up
        spare = self.half_up - self.half
        rest = self.half - fit
        first[:, self.half :] = low[:, fit : fit + spare]
        second[:, self.half : self.half + rest - spare] = low[:, fit + spare : self.half]
        return np.concatenate([first, second, low[:, :fit]], 1)

    def tables(self):
        freq = np.arange(self.freqs)
        fu, hu = self.freqs_up, self.half_up
        middle = H + self.centre - 0.5
        weight = np.where(freq == 0, 1.0, 2.0) / (self.length * ROWS)

        def phases(places):
            return angles(freq, np.round(2 * places), 2 * self.length)

        def complex_table(phase, sign, rows, cols, axis):
            parts = [grown(np.cos(phase), rows, cols), grown(sign * np.sin(phase), rows, cols)]
            return np.concatenate(parts, axis)

        mask = phases(np.arange(self.mask) - middle)
        half = phases(np.arange(self.half) + 0.5)
        grad = phases(np.arange(self.grad) + 2 * H - middle)
        taps = phases(np.arange(KS) - H)
        grad_table = np.concatenate(
            [
                grown((np.cos(grad) * weight[:, None]).T, self.grad_up, fu),
                grown((-np.sin(grad) * weight[:, None]).T, self.grad_up, fu),
            ],
            1,
        )
        return dict(
            mask_cols=left_stack(complex_table(mask, -1.0, fu, self.mask_up, 0)),
            field_even=left_stack(grown((np.cos(half) * weight[:, None]).T, hu, fu)),
            field_odd=left_stack(grown((np.sin(half) * weight[:, None]).T, hu, fu)),
            source_even=self.source_stack(np.cos(half)),
            source_odd=self.source_stack(-np.sin(half)),
            grad_cols=left_stack(grad_table),
            tap_cols=left_stack(complex_table(taps, 1.0, fu, KS, 1)),
        )


def row_tables():
    freq = np.arange(ROWS)

    def complex_table(phase, sign):
        cos, sin = np.cos(phase), sign * np.sin(phase)
        return np.block([[cos, sin], [-sin, cos]])

    def side(table):
        high, low = halves(table)
        return np.concatenate([high, low], 1)

    places = np.arange(64) + H
    field = complex_table(angles(freq, places, ROWS), 1.0)
    field_swapped = np.concatenate([field[:, 64:], field[:, :64]], 1)
    source = complex_table(angles(np.arange(64), freq, ROWS), -1.0)
    source_swapped = np.concatenate([source[64:], source[:64]], 0)
    taps = angles(np.arange(KS) - H, freq, ROWS)
    tap = np.concatenate([np.cos(taps), -np.sin(taps)], 1)
    zero = np.zeros_like(tap)
    return dict(
        mask_rows=right_stack(complex_table(angles(freq, freq, ROWS), -1.0)),
        field_rows=side(field),
        field_rows_swapped=side(field_swapped),
        source_rows=right_stack(source),
        source_rows_swapped=right_stack(source_swapped),
        grad_rows=right_stack(complex_table(angles(freq, freq - H, ROWS), 1.0)),
        tap_rows=right_stack(np.block([[tap, zero], [zero, tap]])),
    )


def split(value):
    high = value.astype(bf16)
    return high, (value - high.astype(f32)).astype(bf16)


def dot(left, right):
    return lax.dot_general(
        left, right, (((1,), (0,)), ((), ())), preferred_element_type=f32
    )


def chunks(count, parts):
    units = count // 16
    edges = [16 * (units * i // parts) for i in range(parts + 1)]
    return list(zip(edges[:-1], edges[1:]))


def left_dot(table, value, parts=1):
    high, low = split(value)
    stacked = jnp.concatenate([high, low, high], 0)
    rows = [table[a:b, :] for a, b in chunks(table.shape[0], parts)]
    return jnp.concatenate([dot(part, stacked) for part in rows], 0)


def source_dot(geo, table, value):
    if not geo.dense():
        return left_dot(table[...], value)
    fit = 512 - 2 * geo.half_up
    spare = geo.half_up - geo.half
    high, low = split(value)
    tail_high, tail_low = high[fit:].astype(f32)[: geo.half - fit], low[fit:].astype(f32)
    first = jnp.concatenate([tail_high, tail_high[:spare]], 0).astype(bf16)
    rest = tail_high[spare:]
    blank = jnp.zeros((spare - rest.shape[0], value.shape[1]), f32)
    second = jnp.concatenate([tail_low[: geo.half - fit], rest, blank], 0).astype(bf16)
    stacked = jnp.concatenate([high[:fit], first, low[:fit], second, high[:fit]], 0)
    return dot(table[...], stacked)


def right_dot(value, table, parts=1):
    high, low = split(value)
    stacked = jnp.concatenate([high, low, high], 1)
    rows = [stacked[a:b] for a, b in chunks(value.shape[0], parts)]
    return jnp.concatenate([dot(part, table) for part in rows], 0)


def sigmoid(value):
    return 1.0 / (1.0 + jnp.exp(-value))


def swap_halves(value):
    return pltpu.roll(value, 64, 1)


def is_even(place, axis, shape):
    return jnp.broadcast_to(place[axis : axis + 1, : shape[1]], shape) % 2 == 0


def window(shape, first_col, first_row, whole_cols, whole_rows):
    col = lax.broadcasted_iota(jnp.int32, shape, 0) + first_col
    row = lax.broadcasted_iota(jnp.int32, shape, 1) + first_row
    return (col >= 0) & (col < whole_cols) & (row >= 0) & (row < whole_rows)


def column_spectra(geo, half, table, out):
    count = geo.freqs_up
    for k in range(out.shape[0] // (2 * count)):
        part = half[k * KS : (k + 1) * KS, :]
        turned = jnp.concatenate(
            [part[:, 128:256], -part[:, 0:128], part[:, 384:512], -part[:, 256:384]], 1
        )
        spec = left_dot(table[...], jnp.concatenate([part, turned], 0))
        out[2 * k * count : (2 * k + 1) * count, :] = spec[:, :256]
        out[(2 * k + 1) * count : (2 * k + 2) * count, :] = spec[:, 256:]


def bring(sources, targets, sems):
    copies = [
        pltpu.make_async_copy(source, target, sems.at[index])
        for index, (source, target) in enumerate(zip(sources, targets))
    ]
    for copy in copies:
        copy.start()
    return copies


def setup_kernel(geo, held, kern_real, kern_imag, tap_rows, tap_cols, *rest):
    sources, (half, out), rest = rest[:held], rest[held : held + 2], rest[held + 2 :]
    copies = bring(sources, rest[:held], rest[held])
    both = jnp.concatenate([kern_real[...], kern_imag[...]], 0)
    for start in range(0, both.shape[1], 128):
        part = both[:, start : start + 128].T
        half[start : start + 128, :] = right_dot(part, tap_rows[...])
    column_spectra(geo, half, tap_cols, out)
    for copy in copies:
        copy.wait()


def slim_kernel(geo, held, half, tap_cols, *rest):
    sources, out, rest = rest[:held], rest[held], rest[held + 1 :]
    copies = bring(sources, rest[:held], rest[held])
    column_spectra(geo, half, tap_cols, out)
    for copy in copies:
        copy.wait()


def one_step(geo, mask, target, inside, weights, spec, tabs, fields):
    count = geo.freqs_up
    kernels = fields.shape[1]
    across = left_dot(tabs["mask_cols"], mask, 2)
    mask_spec = right_dot(
        jnp.concatenate([across[:count], across[count:]], 1), tabs["mask_rows"][...], 2
    )

    def place(index, start, stop):
        value = spec[index * count + start : index * count + stop, :]
        return value[:, :128], value[:, 128:]

    evens, odds = [], []
    for start, stop in chunks(count, 1):
        size = stop - start
        lane = lanes((size, 128))
        mask_re, mask_im = mask_spec[start:stop, :128], mask_spec[start:stop, 128:]

        def down(indices, table):
            products = []
            for index in indices:
                re, im = place(index, start, stop)
                products.append(
                    jnp.concatenate(
                        [re * mask_re - im * mask_im, re * mask_im + im * mask_re], 1
                    )
                )
            high, low = split(jnp.concatenate(products, 0))
            wide = dot(high, table[...])
            got = wide[:, :128] + wide[:, 128:] + dot(low, table[:, :128])
            return [got[i * size : (i + 1) * size] for i in range(len(indices))]

        firsts = down(range(0, 2 * kernels, 2), tabs["field_rows"])
        seconds = down(range(1, 2 * kernels, 2), tabs["field_rows_swapped"])
        pairs = list(zip(firsts, seconds))
        evens.append(jnp.concatenate([jnp.where(lane, a, b) for a, b in pairs], 1))
        odds.append(
            jnp.concatenate([swap_halves(jnp.where(lane, b, a)) for a, b in pairs], 1)
        )
    even = left_dot(tabs["field_even"][...], jnp.concatenate(evens, 0))
    odd = left_dot(tabs["field_odd"][...], jnp.concatenate(odds, 0))
    zero = jnp.zeros((geo.half_up, 128), f32)
    intensity = [zero, zero]
    for side, field in enumerate((even - odd, even + odd)):
        for j in range(kernels):
            own = field[:, j * 128 : (j + 1) * 128]
            fields[side, j] = own
            intensity[side] = intensity[side] + weights[j : j + 1, :] * (own * own)
    cotangent = []
    for side in (0, 1):
        intensity[side] = intensity[side] + swap_halves(intensity[side])
        resist = sigmoid(steepness * (intensity[side] - threshold))
        slope = 2.0 * (resist - target[side]) * steepness * resist * (1.0 - resist)
        cotangent.append(jnp.where(inside[side], slope, 0.0))
    right, left = (
        jnp.concatenate(
            [
                (2.0 * weights[j : j + 1, :] * cotangent[side]) * fields[side, j]
                for j in range(kernels)
            ],
            1,
        )
        for side in (0, 1)
    )
    even = source_dot(geo, tabs["source_even"], right + left)
    odd = source_dot(geo, tabs["source_odd"], right - left)
    totals = []
    for start, stop in chunks(count, 2):
        size = stop - start
        lane = lanes((size, 128))
        res = [even[start:stop, j * 128 : (j + 1) * 128] for j in range(kernels)]
        ims = [swap_halves(odd[start:stop, j * 128 : (j + 1) * 128]) for j in range(kernels)]
        total_re = jnp.zeros((size, 128), f32)
        total_im = jnp.zeros((size, 128), f32)
        for index, values, table in (
            (0, [jnp.where(lane, a, b) for a, b in zip(res, ims)], tabs["source_rows"]),
            (1, [jnp.where(lane, b, a) for a, b in zip(res, ims)], tabs["source_rows_swapped"]),
        ):
            got = right_dot(jnp.concatenate(values, 0), table[...])
            for j in range(kernels):
                got_re = got[j * size : (j + 1) * size, :128]
                got_im = got[j * size : (j + 1) * size, 128:]
                re, im = place(2 * j + index, start, stop)
                total_re = total_re + (re * got_re + im * got_im)
                total_im = total_im + (re * got_im - im * got_re)
        totals.append(jnp.concatenate([total_re, total_im], 1))
    back = right_dot(jnp.concatenate(totals, 0), tabs["grad_rows"][...], 2)
    grad = left_dot(
        tabs["grad_cols"], jnp.concatenate([back[:, :128], back[:, 128:]], 0), 2
    )
    return intensity, grad


COLUMN_TABLES = (
    "mask_cols",
    "field_even",
    "field_odd",
    "source_even",
    "source_odd",
    "grad_cols",
)
ROW_TABLES = (
    "mask_rows",
    "field_rows",
    "field_rows_swapped",
    "source_rows",
    "source_rows_swapped",
    "grad_rows",
)
STEP_TABLES = COLUMN_TABLES + ROW_TABLES


def lanes(shape):
    return lax.broadcasted_iota(jnp.int32, shape, 1) < 64


def early_kernel(own, bits, params, target, tall):
    cols = own.shape[1]
    tall[...] = jnp.zeros_like(tall)
    tall[32:96, :cols] = own[...]
    params[...] = tall[...].T[:cols]
    words = bits.shape[0]
    width = cols // words
    shift = lax.broadcasted_iota(jnp.int32, (width, 128), 0)
    for index in range(words):
        word = bits[index : index + 1, :]
        word = jnp.broadcast_to(jnp.concatenate([word, word], 1), (width, 128))
        bit = jnp.bitwise_and(jnp.right_shift(word, shift), 1).astype(f32)
        target[index * width : (index + 1) * width, :] = bit


def prep_kernel(place, own, target, across, within, params, to_first, to_second, tall):
    even = is_even(place, 0, (32, own.shape[0]))
    cols = own.shape[0]
    tall[...] = jnp.zeros_like(tall)
    tall[0:32, :cols] = jnp.where(even, across[32:64, :], within[32:64, :])
    tall[96:128, :cols] = jnp.where(even, within[0:32, :], across[0:32, :])
    params[...] = own[...] + tall[...].T[:cols]
    right = is_even(place, 1, (176, 128))
    left_lanes = lanes((48, 128))

    def packed(start):
        return jnp.where(left_lanes, target[start : start + 48], target[start + 48 : start + 96])

    to_left = jnp.concatenate([params[0:128, :], packed(0)], 0)
    to_right = jnp.concatenate([params[cols - 128 : cols, :], packed(cols - 96)], 0)
    to_first[...] = jnp.where(right, to_right, to_left)
    to_second[...] = jnp.where(right, to_left, to_right)


def spread_out(place, grad, spread, to_far, to_near):
    even = is_even(place, 0, grad.shape)
    half = to_far.shape[0]
    spread[...] = grad
    turned = swap_halves(grad)
    straight = jnp.where(even, grad, turned)
    crossed = jnp.where(even, turned, grad)
    left_lanes = lanes((half, 128))
    to_far[...] = jnp.where(left_lanes, straight[:half], crossed[half:])
    to_near[...] = jnp.where(left_lanes, crossed[:half], straight[half:])


def last_spread_out(place, grad, spread, to_far, to_near):
    size = to_far.shape[0]
    quarter = lax.broadcasted_iota(jnp.int32, (size, 128), 1) // 32
    spread[...] = grad
    top = bottom = jnp.zeros((size, 128), f32)
    for index in range(4):
        part = grad[index * size : (index + 1) * size]
        here = quarter == index
        top = jnp.where(here, pltpu.roll(part, 32 * index, 1), top)
        bottom = jnp.where(here, pltpu.roll(part, (32 * index + 32) % 128, 1), bottom)
    even = is_even(place, 0, (size, 128))
    to_far[...] = jnp.where(even, top, bottom)
    to_near[...] = jnp.where(even, bottom, top)


def last_gathered(place, spread, far, near):
    size = far.shape[0]
    even = is_even(place, 0, far.shape)
    above = jnp.where(even, far[...], near[...])
    below = jnp.where(even, near[...], far[...])
    upper = lanes(far.shape)
    parts = [
        jnp.where(
            upper,
            pltpu.roll(above, (160 - 32 * index) % 128, 1),
            pltpu.roll(below, (192 - 32 * index) % 128, 1),
        )
        for index in range(4)
    ]
    return spread[...] + jnp.concatenate(parts, 0)


def gathered(place, spread, far, near):
    even = is_even(place, 0, spread.shape)
    far, near = far[...], near[...]
    left_lanes = lanes(far.shape)
    far_turned, near_turned = swap_halves(far), swap_halves(near)
    straight = jnp.concatenate(
        [jnp.where(left_lanes, far, near_turned), jnp.where(left_lanes, far_turned, near)], 0
    )
    crossed = jnp.concatenate(
        [jnp.where(left_lanes, near, far_turned), jnp.where(left_lanes, near_turned, far)], 0
    )
    return spread[...] + jnp.where(even, straight, crossed)


def stepped(params, grad):
    field = sigmoid(sharpness * params)
    return params - step_size * sharpness * field * (1.0 - field) * grad


def masked(place, tile, whole, params, col_offset):
    first_col = place[1:2, :128] * tile[1] + col_offset
    first_row = place[0:1, :128] * tile[0] - H
    inside = window(params.shape, first_col, first_row, whole[1], whole[0])
    return jnp.where(inside, sigmoid(sharpness * params), 0.0)


def field_window(geo, place, tile, whole, col_offset):
    middle = place[1:2, :128] * tile[1] + col_offset + H + geo.centre
    step = lax.broadcasted_iota(jnp.int32, (geo.half_up, 128), 0)
    return [(col >= 0) & (col < whole[1]) for col in (middle + step, middle - 1 - step)]


def first_kernel(
    geo, tile, whole, place, weights, own, target, first, second, spec, mirror, *rest
):
    tabs = dict(zip(STEP_TABLES, rest))
    rest = rest[len(STEP_TABLES) :]
    spread, to_far, to_near, params_out, goal_out, params, goal, fields = rest
    cols = own.shape[0]
    right_first = is_even(place, 1, first.shape)
    left = jnp.where(right_first, second[...], first[...])
    right = jnp.where(right_first, first[...], second[...])
    params[...] = jnp.zeros_like(params)
    params[0:128, :] = left[0:128, :]
    params[128 : 128 + cols, :] = own[...]
    params[128 + cols : 256 + cols, :] = right[0:128, :]
    left_lanes = lanes((48, 128))
    goal[...] = jnp.zeros_like(goal)
    for start, side in ((0, left), (96 + cols, right)):
        packed = side[128:176, :]
        turned = swap_halves(packed)
        goal[start : start + 48, :] = jnp.where(left_lanes, packed, turned)
        goal[start + 48 : start + 96, :] = jnp.where(left_lanes, turned, packed)
    goal[96 : 96 + cols, :] = target[...]
    goals = [
        goal[geo.centre : geo.centre + geo.half_up, :],
        dot(mirror[...], goal[0 : mirror.shape[1], :].astype(bf16)),
    ]
    for side in (0, 1):
        goal_out[side] = goals[side][: goal_out.shape[1]]
    params_out[...] = params[64 : 64 + params_out.shape[0], :]
    mask = masked(place, tile, whole, params[...], -128)
    inside = field_window(geo, place, tile, whole, -128)
    _, grad = one_step(geo, mask, goals, inside, weights, spec, tabs, fields)
    spread_out(place, grad, spread, to_far, to_near)


def second_kernel(geo, tile, whole, place, weights, own, far, near, old, goal, spec, *rest):
    tabs = dict(zip(STEP_TABLES, rest))
    spread, to_far, to_near, params_out, fields = rest[len(STEP_TABLES) :]
    params = stepped(old[...], gathered(place, own, far, near))
    params_out[...] = params[64 : 64 + params_out.shape[0], :]
    mask = masked(place, tile, whole, params, -64)
    inside = field_window(geo, place, tile, whole, -64)
    goals = [goal[0], goal[1]]
    _, grad = one_step(geo, mask, goals, inside, weights, spec, tabs, fields)
    spread_out(place, grad, spread, to_far, to_near)


def update_kernel(cols, place, own, far, near, old, params, to_first, to_second):
    params[...] = stepped(old[...], gathered(place, own, far, near))
    right = is_even(place, 1, (64, 128))
    to_left, to_right = params[0:64, :], params[cols - 64 : cols, :]
    to_first[...] = jnp.where(right, to_right, to_left)
    to_second[...] = jnp.where(right, to_left, to_right)


def third_kernel(
    geo, tile, whole, place, weights, own, first, second, goal, spec, *rest
):
    tabs = dict(zip(STEP_TABLES, rest))
    rest = rest[len(STEP_TABLES) :]
    spread, to_far, to_near, intensity_out, params, fields = rest
    cols = tile[1]
    right_first = is_even(place, 1, (64, 128))
    params[...] = jnp.zeros_like(params)
    params[0:64, :] = jnp.where(right_first, second[...], first[...])
    params[64 : 64 + cols, :] = own[0:cols, :]
    params[64 + cols : 128 + cols, :] = jnp.where(right_first, first[...], second[...])
    mask = masked(place, tile, whole, params[...], -64)
    inside = field_window(geo, place, tile, whole, -64)
    goals = [goal[0], goal[1]]
    intensity, grad = one_step(geo, mask, goals, inside, weights, spec, tabs, fields)
    last_spread_out(place, grad, spread, to_far, to_near)
    for side in (0, 1):
        intensity_out[side] = intensity[side]


def intensity_kernel(cols, intensity, mirror, out, flat):
    high, low = split(intensity[1])
    rest = (intensity[1] - high.astype(f32) - low.astype(f32)).astype(bf16)
    turned = dot(mirror[...], high) + (dot(mirror[...], low) + dot(mirror[...], rest))
    flat[...] = jnp.zeros_like(flat)
    flat[0 : cols // 2, :] = turned[0 : cols // 2]
    flat[cols // 2 : cols, :] = intensity[0][0 : cols // 2]
    out[...] = flat[...].T[:64, :cols]


def final_kernel(cols, place, own, far, near, out, wide):
    wide[...] = jnp.zeros_like(wide)
    wide[0 : own.shape[0], :] = last_gathered(place, own, far, near)
    out[...] = wide[...].T[H : H + 64, :cols]


def mirror_table(rows, rows_up, cols_up):
    table = np.zeros((rows_up, cols_up), np.float32)
    table[np.arange(rows), rows - 1 - np.arange(rows)] = 1.0
    return table.astype(ml_dtypes.bfloat16)


def call(kernel, name, out_shapes, scratch, args, space=pltpu.VMEM):
    return pl.pallas_call(
        kernel,
        name=name,
        out_shape=[
            shape if isinstance(shape, jax.ShapeDtypeStruct) else pltpu.VMEM(shape, f32)
            for shape in out_shapes
        ],
        in_specs=[pl.BlockSpec(memory_space=pltpu.VMEM)] * len(args),
        out_specs=[pl.BlockSpec(memory_space=pltpu.VMEM)] * len(out_shapes),
        scratch_shapes=[pltpu.VMEM(shape, f32) for shape in scratch],
        compiler_params=pltpu.CompilerParams(vmem_limit_bytes=VMEM_LIMIT),
    )(*[pltpu.with_memory_space_constraint(arg, space) for arg in args])


def per_device(rows, cols, mask_params, target_bits, kern_real, kern_imag, socs_weights):
    tile = mask_params.shape
    whole = (tile[0] * rows, tile[1] * cols)
    kernels = kern_real.shape[1] // KS
    axis = lax.broadcasted_iota(jnp.int32, (8, 256), 0)
    place = jnp.where(axis == 0, lax.axis_index("row"), lax.axis_index("col"))
    weights = jnp.broadcast_to(socs_weights[:, None], (kernels, 128))

    def swaps(count, start):
        pairs = [(i, i + 1) for i in range(start, count - 1, 2)]
        return pairs + [(b, a) for a, b in pairs]

    def row_exchange(to_far, to_near):
        far = lax.ppermute(to_far, "row", swaps(rows, 1))
        return far, lax.ppermute(to_near, "row", swaps(rows, 0))

    def col_exchange(to_first, to_second):
        first = lax.ppermute(to_first, "col", swaps(cols, 0))
        return first, lax.ppermute(to_second, "col", swaps(cols, 1))

    wide, slim = Geometry(tile[1] + 8 * H, 1), Geometry(tile[1] + 4 * H, 0)
    shared = row_tables()
    shared["wide_mirror"] = mirror_table(wide.centre, wide.half_up, wide.half_up)
    shared["slim_mirror"] = mirror_table(tile[1] // 2, up(tile[1] // 2, 16), slim.half_up)
    n = tile[1]
    far, near = row_exchange(mask_params, mask_params)
    params, target = call(
        early_kernel,
        "early",
        [(n, 128), (n, 128)],
        [(128, 256)],
        [mask_params, target_bits.T],
        pltpu.HBM,
    )
    near, place, weights = lax.optimization_barrier((near, place, weights))
    params, to_first, to_second = call(
        prep_kernel,
        "prep",
        [(n, 128), (176, 128), (176, 128)],
        [(128, 256)],
        [place, params, target, far, near],
    )
    first, second = col_exchange(to_first, to_second)
    made = {"wide": wide.tables(), "slim": slim.tables(), "shared": shared}
    place_of = {}

    def loader(kernel, name, geo, out_shapes, inputs, spaces, names):
        tables = [jnp.asarray(made[label][part]) for label, part in names]
        arrays = list(zip(inputs + tables, spaces + [pltpu.HBM] * len(tables)))
        outs = pl.pallas_call(
            functools.partial(kernel, geo, len(tables)),
            name=name,
            out_shape=[pltpu.VMEM(shape, f32) for shape in out_shapes]
            + [pltpu.VMEM(table.shape, table.dtype) for table in tables],
            in_specs=[pl.BlockSpec(memory_space=pltpu.VMEM)] * len(inputs)
            + [pl.BlockSpec(memory_space=pltpu.HBM)] * len(tables),
            out_specs=[pl.BlockSpec(memory_space=pltpu.VMEM)]
            * (len(out_shapes) + len(tables)),
            scratch_shapes=[pltpu.SemaphoreType.DMA((len(tables),))],
            compiler_params=pltpu.CompilerParams(vmem_limit_bytes=VMEM_LIMIT),
        )(*[pltpu.with_memory_space_constraint(*pair) for pair in arrays])
        place_of.update(zip(names, outs[len(out_shapes) :]))
        return outs[: len(out_shapes)]

    half_spec, wide_spec = loader(
        setup_kernel,
        "spectra",
        wide,
        [(kernels * KS, 512), (2 * kernels * wide.freqs_up, 256)],
        [
            kern_real,
            kern_imag,
            jnp.asarray(shared["tap_rows"]),
            jnp.asarray(made["wide"]["tap_cols"]),
        ],
        [pltpu.HBM] * 4,
        [("wide", part) for part in COLUMN_TABLES]
        + [("shared", part) for part in ROW_TABLES + ("wide_mirror",)],
    )

    def tabs(label):
        return [place_of[label, name] for name in COLUMN_TABLES] + [
            place_of["shared", name] for name in ROW_TABLES
        ]

    def spreads(geo):
        return [(geo.grad_up, 128)] + [(geo.grad_up // 2, 128)] * 2

    def fields(geo):
        return (2, kernels, geo.half_up, 128)

    spread, to_far, to_near, params, goal = call(
        functools.partial(first_kernel, wide, tile, whole),
        "first",
        spreads(wide) + [(slim.mask_up, 128), (2, slim.half_up, 128)],
        [(wide.mask_up, 128), (wide.centre + wide.half_up, 128), fields(wide)],
        [place, weights, params, target, first, second, wide_spec]
        + [place_of["shared", "wide_mirror"], *tabs("wide")],
    )
    far, near = row_exchange(to_far, to_near)
    (slim_spec,) = loader(
        slim_kernel,
        "slim",
        slim,
        [(2 * kernels * slim.freqs_up, 256)],
        [half_spec, jnp.asarray(made["slim"]["tap_cols"])],
        [pltpu.VMEM, pltpu.HBM],
        [("slim", part) for part in COLUMN_TABLES] + [("shared", "slim_mirror")],
    )
    spread, to_far, to_near, params = call(
        functools.partial(second_kernel, slim, tile, whole),
        "second",
        spreads(slim) + [(slim.grad_up, 128)],
        [fields(slim)],
        [place, weights, spread, far, near, params, goal, slim_spec, *tabs("slim")],
    )
    far, near = row_exchange(to_far, to_near)
    params, to_first, to_second = call(
        functools.partial(update_kernel, n),
        "update",
        [(slim.grad_up, 128), (64, 128), (64, 128)],
        [],
        [place, spread, far, near, params],
    )
    first, second = col_exchange(to_first, to_second)
    spread, to_far, to_near, intensity = call(
        functools.partial(third_kernel, slim, tile, whole),
        "third",
        spreads(slim)[:1] + [(slim.grad_up // 4, 128)] * 2 + [(2, slim.half_up, 128)],
        [(slim.mask_up, 128), fields(slim)],
        [place, weights, params, first, second, goal, slim_spec, *tabs("slim")],
    )
    far, near = row_exchange(to_far, to_near)
    (intensity,) = call(
        functools.partial(intensity_kernel, n),
        "intensity",
        [jax.ShapeDtypeStruct(tile, f32)],
        [(256, 128)],
        [intensity, place_of["shared", "slim_mirror"]],
    )
    (mask_grad,) = call(
        functools.partial(final_kernel, n),
        "final",
        [jax.ShapeDtypeStruct(tile, f32)],
        [(256, 128)],
        [place, spread, far, near],
    )
    return mask_grad, intensity


def solution(mesh):
    placed = (P("row", "col"), P("row", "col"), P(), P(), P())
    return jax.shard_map(
        functools.partial(per_device, mesh.shape["row"], mesh.shape["col"]),
        mesh=mesh,
        in_specs=placed,
        out_specs=(P("row", "col"), P("row", "col")),
        check_vma=False,
    )
```

```python
import functools
import math

import jax
import jax.numpy as jnp
import ml_dtypes
import numpy as np
from jax import lax
from jax.experimental import pallas as pl
from jax.experimental.pallas import tpu as pltpu
from jax.sharding import PartitionSpec as P

H = 32
KS = 64
ITERS = 3
ROWS = 128
sharpness = 2.0
steepness = 4.0
threshold = 0.8
step_size = 1.0
f32 = jnp.float32
bf16 = jnp.bfloat16
VMEM_LIMIT = 28 * 1024 * 1024


def up(value, unit):
    return -(-value // unit) * unit


def halves(table):
    table = table.astype(np.float32)
    high = table.astype(ml_dtypes.bfloat16)
    low = (table - high.astype(np.float32)).astype(ml_dtypes.bfloat16)
    return high, low


def angles(left, right, length):
    product = np.outer(left.astype(np.int64), right.astype(np.int64)) % length
    return product * (2.0 * math.pi / length)


def grown(table, rows, cols):
    return np.pad(table, [(0, rows - table.shape[0]), (0, cols - table.shape[1])])


def left_stack(table):
    high, low = halves(table)
    return np.concatenate([high, high, low], 1)


def right_stack(table):
    high, low = halves(table)
    return np.concatenate([high, high, low], 0)


class Geometry:
    def __init__(self, width, trim):
        self.mask = width
        self.centre = width // 2 - H
        self.half = self.centre - trim
        self.grad = width - 4 * H
        self.length = width | 1
        self.freqs = (self.length + 1) // 2
        self.freqs_up = up(self.freqs, 16)
        self.mask_up = up(self.mask, 16)
        self.half_up = up(self.half, 16)
        self.grad_up = up(self.grad, 32)

    def dense(self):
        return 3 * self.half <= 512 < 3 * self.half_up

    def source_stack(self, table):
        table = grown(table, self.freqs_up, self.half_up)
        if not self.dense():
            return left_stack(table)
        high, low = halves(table)
        first, second = high.copy(), high.copy()
        fit = 512 - 2 * self.half_up
        spare = self.half_up - self.half
        rest = self.half - fit
        first[:, self.half :] = low[:, fit : fit + spare]
        second[:, self.half : self.half + rest - spare] = low[:, fit + spare : self.half]
        return np.concatenate([first, second, low[:, :fit]], 1)

    def tables(self):
        freq = np.arange(self.freqs)
        fu, hu = self.freqs_up, self.half_up
        middle = H + self.centre - 0.5
        weight = np.where(freq == 0, 1.0, 2.0) / (self.length * ROWS)

        def phases(places):
            return angles(freq, np.round(2 * places), 2 * self.length)

        def complex_table(phase, sign, rows, cols, axis):
            parts = [grown(np.cos(phase), rows, cols), grown(sign * np.sin(phase), rows, cols)]
            return np.concatenate(parts, axis)

        mask = phases(np.arange(self.mask) - middle)
        half = phases(np.arange(self.half) + 0.5)
        grad = phases(np.arange(self.grad) + 2 * H - middle)
        taps = phases(np.arange(KS) - H)
        grad_table = np.concatenate(
            [
                grown((np.cos(grad) * weight[:, None]).T, self.grad_up, fu),
                grown((-np.sin(grad) * weight[:, None]).T, self.grad_up, fu),
            ],
            1,
        )
        return dict(
            mask_cols=left_stack(complex_table(mask, -1.0, fu, self.mask_up, 0)),
            field_even=left_stack(grown((np.cos(half) * weight[:, None]).T, hu, fu)),
            field_odd=left_stack(grown((np.sin(half) * weight[:, None]).T, hu, fu)),
            source_even=self.source_stack(np.cos(half)),
            source_odd=self.source_stack(-np.sin(half)),
            grad_cols=left_stack(grad_table),
            tap_cols=left_stack(complex_table(taps, 1.0, fu, KS, 1)),
        )


def row_tables():
    freq = np.arange(ROWS)

    def complex_table(phase, sign):
        cos, sin = np.cos(phase), sign * np.sin(phase)
        return np.block([[cos, sin], [-sin, cos]])

    def side(table):
        high, low = halves(table)
        return np.concatenate([high, low], 1)

    places = np.arange(64) + H
    field = complex_table(angles(freq, places, ROWS), 1.0)
    field_swapped = np.concatenate([field[:, 64:], field[:, :64]], 1)
    source = complex_table(angles(np.arange(64), freq, ROWS), -1.0)
    source_swapped = np.concatenate([source[64:], source[:64]], 0)
    taps = angles(np.arange(KS) - H, freq, ROWS)
    tap = np.concatenate([np.cos(taps), -np.sin(taps)], 1)
    zero = np.zeros_like(tap)
    return dict(
        mask_rows=right_stack(complex_table(angles(freq, freq, ROWS), -1.0)),
        field_rows=side(field),
        field_rows_swapped=side(field_swapped),
        source_rows=right_stack(source),
        source_rows_swapped=right_stack(source_swapped),
        grad_rows=right_stack(complex_table(angles(freq, freq - H, ROWS), 1.0)),
        tap_rows=right_stack(np.block([[tap, zero], [zero, tap]])),
    )


def split(value):
    high = value.astype(bf16)
    return high, (value - high.astype(f32)).astype(bf16)


def dot(left, right):
    return lax.dot_general(
        left, right, (((1,), (0,)), ((), ())), preferred_element_type=f32
    )


def chunks(count, parts):
    units = count // 16
    edges = [16 * (units * i // parts) for i in range(parts + 1)]
    return list(zip(edges[:-1], edges[1:]))


def left_dot(table, value, parts=1):
    high, low = split(value)
    stacked = jnp.concatenate([high, low, high], 0)
    rows = [table[a:b, :] for a, b in chunks(table.shape[0], parts)]
    return jnp.concatenate([dot(part, stacked) for part in rows], 0)


def source_dot(geo, table, value):
    if not geo.dense():
        return left_dot(table[...], value)
    fit = 512 - 2 * geo.half_up
    spare = geo.half_up - geo.half
    high, low = split(value)
    tail_high, tail_low = high[fit:].astype(f32)[: geo.half - fit], low[fit:].astype(f32)
    first = jnp.concatenate([tail_high, tail_high[:spare]], 0).astype(bf16)
    rest = tail_high[spare:]
    blank = jnp.zeros((spare - rest.shape[0], value.shape[1]), f32)
    second = jnp.concatenate([tail_low[: geo.half - fit], rest, blank], 0).astype(bf16)
    stacked = jnp.concatenate([high[:fit], first, low[:fit], second, high[:fit]], 0)
    return dot(table[...], stacked)


def right_dot(value, table, parts=1):
    high, low = split(value)
    stacked = jnp.concatenate([high, low, high], 1)
    rows = [stacked[a:b] for a, b in chunks(value.shape[0], parts)]
    return jnp.concatenate([dot(part, table) for part in rows], 0)


def sigmoid(value):
    return 1.0 / (1.0 + jnp.exp(-value))


def swap_halves(value):
    return pltpu.roll(value, 64, 1)


def is_even(place, axis, shape):
    return jnp.broadcast_to(place[axis : axis + 1, : shape[1]], shape) % 2 == 0


def window(shape, first_col, first_row, whole_cols, whole_rows):
    col = lax.broadcasted_iota(jnp.int32, shape, 0) + first_col
    row = lax.broadcasted_iota(jnp.int32, shape, 1) + first_row
    return (col >= 0) & (col < whole_cols) & (row >= 0) & (row < whole_rows)


def column_spectra(geo, half, table, out):
    count = geo.freqs_up
    for k in range(out.shape[0] // (2 * count)):
        part = half[k * KS : (k + 1) * KS, :]
        turned = jnp.concatenate(
            [part[:, 128:256], -part[:, 0:128], part[:, 384:512], -part[:, 256:384]], 1
        )
        spec = left_dot(table[...], jnp.concatenate([part, turned], 0))
        out[2 * k * count : (2 * k + 1) * count, :] = spec[:, :256]
        out[(2 * k + 1) * count : (2 * k + 2) * count, :] = spec[:, 256:]


def bring(sources, targets, sems):
    copies = [
        pltpu.make_async_copy(source, target, sems.at[index])
        for index, (source, target) in enumerate(zip(sources, targets))
    ]
    for copy in copies:
        copy.start()
    return copies


def setup_kernel(geo, held, kern_real, kern_imag, tap_rows, tap_cols, *rest):
    sources, (half, out), rest = rest[:held], rest[held : held + 2], rest[held + 2 :]
    copies = bring(sources, rest[:held], rest[held])
    both = jnp.concatenate([kern_real[...], kern_imag[...]], 0)
    for start in range(0, both.shape[1], 128):
        part = both[:, start : start + 128].T
        half[start : start + 128, :] = right_dot(part, tap_rows[...])
    column_spectra(geo, half, tap_cols, out)
    for copy in copies:
        copy.wait()


def slim_kernel(geo, held, half, tap_cols, *rest):
    sources, out, rest = rest[:held], rest[held], rest[held + 1 :]
    copies = bring(sources, rest[:held], rest[held])
    column_spectra(geo, half, tap_cols, out)
    for copy in copies:
        copy.wait()


def one_step(geo, mask, target, inside, weights, spec, tabs, fields):
    count = geo.freqs_up
    kernels = fields.shape[1]
    across = left_dot(tabs["mask_cols"], mask, 2)
    mask_spec = right_dot(
        jnp.concatenate([across[:count], across[count:]], 1), tabs["mask_rows"][...], 2
    )

    def place(index, start, stop):
        value = spec[index * count + start : index * count + stop, :]
        return value[:, :128], value[:, 128:]

    evens, odds = [], []
    for start, stop in chunks(count, 2 if geo.dense() else 1):
        size = stop - start
        lane = lanes((size, 128))
        mask_re, mask_im = mask_spec[start:stop, :128], mask_spec[start:stop, 128:]

        def down(indices, table):
            products = []
            for index in indices:
                re, im = place(index, start, stop)
                products.append(
                    jnp.concatenate(
                        [re * mask_re - im * mask_im, re * mask_im + im * mask_re], 1
                    )
                )
            high, low = split(jnp.concatenate(products, 0))
            wide = dot(high, table[...])
            got = wide[:, :128] + wide[:, 128:] + dot(low, table[:, :128])
            return [got[i * size : (i + 1) * size] for i in range(len(indices))]

        firsts = down(range(0, 2 * kernels, 2), tabs["field_rows"])
        seconds = down(range(1, 2 * kernels, 2), tabs["field_rows_swapped"])
        pairs = list(zip(firsts, seconds))
        evens.append(jnp.concatenate([jnp.where(lane, a, b) for a, b in pairs], 1))
        odds.append(
            jnp.concatenate([swap_halves(jnp.where(lane, b, a)) for a, b in pairs], 1)
        )
    even = left_dot(tabs["field_even"][...], jnp.concatenate(evens, 0))
    odd = left_dot(tabs["field_odd"][...], jnp.concatenate(odds, 0))
    zero = jnp.zeros((geo.half_up, 128), f32)
    intensity = [zero, zero]
    for side, field in enumerate((even - odd, even + odd)):
        for j in range(kernels):
            own = field[:, j * 128 : (j + 1) * 128]
            fields[side, j] = own
            intensity[side] = intensity[side] + weights[j : j + 1, :] * (own * own)
    cotangent = []
    for side in (0, 1):
        intensity[side] = intensity[side] + swap_halves(intensity[side])
        resist = sigmoid(steepness * (intensity[side] - threshold))
        slope = 2.0 * (resist - target[side]) * steepness * resist * (1.0 - resist)
        cotangent.append(jnp.where(inside[side], slope, 0.0))
    right, left = (
        jnp.concatenate(
            [
                (2.0 * weights[j : j + 1, :] * cotangent[side]) * fields[side, j]
                for j in range(kernels)
            ],
            1,
        )
        for side in (0, 1)
    )
    even = source_dot(geo, tabs["source_even"], right + left)
    odd = source_dot(geo, tabs["source_odd"], right - left)
    totals = []
    for start, stop in chunks(count, 2):
        size = stop - start
        lane = lanes((size, 128))
        res = [even[start:stop, j * 128 : (j + 1) * 128] for j in range(kernels)]
        ims = [swap_halves(odd[start:stop, j * 128 : (j + 1) * 128]) for j in range(kernels)]
        total_re = jnp.zeros((size, 128), f32)
        total_im = jnp.zeros((size, 128), f32)
        for index, values, table in (
            (0, [jnp.where(lane, a, b) for a, b in zip(res, ims)], tabs["source_rows"]),
            (1, [jnp.where(lane, b, a) for a, b in zip(res, ims)], tabs["source_rows_swapped"]),
        ):
            got = right_dot(jnp.concatenate(values, 0), table[...])
            for j in range(kernels):
                got_re = got[j * size : (j + 1) * size, :128]
                got_im = got[j * size : (j + 1) * size, 128:]
                re, im = place(2 * j + index, start, stop)
                total_re = total_re + (re * got_re + im * got_im)
                total_im = total_im + (re * got_im - im * got_re)
        totals.append(jnp.concatenate([total_re, total_im], 1))
    back = right_dot(jnp.concatenate(totals, 0), tabs["grad_rows"][...], 2)
    grad = left_dot(
        tabs["grad_cols"], jnp.concatenate([back[:, :128], back[:, 128:]], 0), 2
    )
    return intensity, grad


COLUMN_TABLES = (
    "mask_cols",
    "field_even",
    "field_odd",
    "source_even",
    "source_odd",
    "grad_cols",
)
ROW_TABLES = (
    "mask_rows",
    "field_rows",
    "field_rows_swapped",
    "source_rows",
    "source_rows_swapped",
    "grad_rows",
)
STEP_TABLES = COLUMN_TABLES + ROW_TABLES


def lanes(shape):
    return lax.broadcasted_iota(jnp.int32, shape, 1) < 64


def early_kernel(own, bits, params, target, tall):
    cols = own.shape[1]
    tall[...] = jnp.zeros_like(tall)
    tall[32:96, :cols] = own[...]
    params[...] = tall[...].T[:cols]
    words = bits.shape[0]
    width = cols // words
    shift = lax.broadcasted_iota(jnp.int32, (width, 128), 0)
    for index in range(words):
        word = bits[index : index + 1, :]
        word = jnp.broadcast_to(jnp.concatenate([word, word], 1), (width, 128))
        bit = jnp.bitwise_and(jnp.right_shift(word, shift), 1).astype(f32)
        target[index * width : (index + 1) * width, :] = bit


def prep_kernel(place, own, target, across, within, params, to_first, to_second, tall):
    even = is_even(place, 0, (32, own.shape[0]))
    cols = own.shape[0]
    tall[...] = jnp.zeros_like(tall)
    tall[0:32, :cols] = jnp.where(even, across[32:64, :], within[32:64, :])
    tall[96:128, :cols] = jnp.where(even, within[0:32, :], across[0:32, :])
    params[...] = own[...] + tall[...].T[:cols]
    right = is_even(place, 1, (176, 128))
    left_lanes = lanes((48, 128))

    def packed(start):
        return jnp.where(left_lanes, target[start : start + 48], target[start + 48 : start + 96])

    to_left = jnp.concatenate([params[0:128, :], packed(0)], 0)
    to_right = jnp.concatenate([params[cols - 128 : cols, :], packed(cols - 96)], 0)
    to_first[...] = jnp.where(right, to_right, to_left)
    to_second[...] = jnp.where(right, to_left, to_right)


def spread_out(place, grad, spread, to_far, to_near):
    even = is_even(place, 0, grad.shape)
    half = to_far.shape[0]
    spread[...] = grad
    turned = swap_halves(grad)
    straight = jnp.where(even, grad, turned)
    crossed = jnp.where(even, turned, grad)
    left_lanes = lanes((half, 128))
    to_far[...] = jnp.where(left_lanes, straight[:half], crossed[half:])
    to_near[...] = jnp.where(left_lanes, crossed[:half], straight[half:])


def last_spread_out(place, grad, spread, to_far, to_near):
    size = to_far.shape[0]
    quarter = lax.broadcasted_iota(jnp.int32, (size, 128), 1) // 32
    spread[...] = grad
    top = bottom = jnp.zeros((size, 128), f32)
    for index in range(4):
        part = grad[index * size : (index + 1) * size]
        here = quarter == index
        top = jnp.where(here, pltpu.roll(part, 32 * index, 1), top)
        bottom = jnp.where(here, pltpu.roll(part, (32 * index + 32) % 128, 1), bottom)
    even = is_even(place, 0, (size, 128))
    to_far[...] = jnp.where(even, top, bottom)
    to_near[...] = jnp.where(even, bottom, top)


def last_gathered(place, spread, far, near):
    size = far.shape[0]
    even = is_even(place, 0, far.shape)
    above = jnp.where(even, far[...], near[...])
    below = jnp.where(even, near[...], far[...])
    upper = lanes(far.shape)
    parts = [
        jnp.where(
            upper,
            pltpu.roll(above, (160 - 32 * index) % 128, 1),
            pltpu.roll(below, (192 - 32 * index) % 128, 1),
        )
        for index in range(4)
    ]
    return spread[...] + jnp.concatenate(parts, 0)


def gathered(place, spread, far, near):
    even = is_even(place, 0, spread.shape)
    far, near = far[...], near[...]
    left_lanes = lanes(far.shape)
    far_turned, near_turned = swap_halves(far), swap_halves(near)
    straight = jnp.concatenate(
        [jnp.where(left_lanes, far, near_turned), jnp.where(left_lanes, far_turned, near)], 0
    )
    crossed = jnp.concatenate(
        [jnp.where(left_lanes, near, far_turned), jnp.where(left_lanes, near_turned, far)], 0
    )
    return spread[...] + jnp.where(even, straight, crossed)


def stepped(params, grad):
    field = sigmoid(sharpness * params)
    return params - step_size * sharpness * field * (1.0 - field) * grad


def masked(place, tile, whole, params, col_offset):
    first_col = place[1:2, :128] * tile[1] + col_offset
    first_row = place[0:1, :128] * tile[0] - H
    inside = window(params.shape, first_col, first_row, whole[1], whole[0])
    return jnp.where(inside, sigmoid(sharpness * params), 0.0)


def field_window(geo, place, tile, whole, col_offset):
    middle = place[1:2, :128] * tile[1] + col_offset + H + geo.centre
    step = lax.broadcasted_iota(jnp.int32, (geo.half_up, 128), 0)
    return [(col >= 0) & (col < whole[1]) for col in (middle + step, middle - 1 - step)]


def first_kernel(
    geo, tile, whole, place, weights, own, target, first, second, spec, mirror, *rest
):
    tabs = dict(zip(STEP_TABLES, rest))
    rest = rest[len(STEP_TABLES) :]
    spread, to_far, to_near, params_out, goal_out, params, goal, fields = rest
    cols = own.shape[0]
    right_first = is_even(place, 1, first.shape)
    left = jnp.where(right_first, second[...], first[...])
    right = jnp.where(right_first, first[...], second[...])
    params[...] = jnp.zeros_like(params)
    params[0:128, :] = left[0:128, :]
    params[128 : 128 + cols, :] = own[...]
    params[128 + cols : 256 + cols, :] = right[0:128, :]
    left_lanes = lanes((48, 128))
    goal[...] = jnp.zeros_like(goal)
    for start, side in ((0, left), (96 + cols, right)):
        packed = side[128:176, :]
        turned = swap_halves(packed)
        goal[start : start + 48, :] = jnp.where(left_lanes, packed, turned)
        goal[start + 48 : start + 96, :] = jnp.where(left_lanes, turned, packed)
    goal[96 : 96 + cols, :] = target[...]
    goals = [
        goal[geo.centre : geo.centre + geo.half_up, :],
        dot(mirror[...], goal[0 : mirror.shape[1], :].astype(bf16)),
    ]
    for side in (0, 1):
        goal_out[side] = goals[side][: goal_out.shape[1]]
    params_out[...] = params[64 : 64 + params_out.shape[0], :]
    mask = masked(place, tile, whole, params[...], -128)
    inside = field_window(geo, place, tile, whole, -128)
    _, grad = one_step(geo, mask, goals, inside, weights, spec, tabs, fields)
    spread_out(place, grad, spread, to_far, to_near)


def second_kernel(geo, tile, whole, place, weights, own, far, near, old, goal, spec, *rest):
    tabs = dict(zip(STEP_TABLES, rest))
    spread, to_far, to_near, params_out, fields = rest[len(STEP_TABLES) :]
    params = stepped(old[...], gathered(place, own, far, near))
    params_out[...] = params[64 : 64 + params_out.shape[0], :]
    mask = masked(place, tile, whole, params, -64)
    inside = field_window(geo, place, tile, whole, -64)
    goals = [goal[0], goal[1]]
    _, grad = one_step(geo, mask, goals, inside, weights, spec, tabs, fields)
    spread_out(place, grad, spread, to_far, to_near)


def update_kernel(cols, place, own, far, near, old, params, to_first, to_second):
    params[...] = stepped(old[...], gathered(place, own, far, near))
    right = is_even(place, 1, (64, 128))
    to_left, to_right = params[0:64, :], params[cols - 64 : cols, :]
    to_first[...] = jnp.where(right, to_right, to_left)
    to_second[...] = jnp.where(right, to_left, to_right)


def third_kernel(
    geo, tile, whole, place, weights, own, first, second, goal, spec, *rest
):
    tabs = dict(zip(STEP_TABLES, rest))
    rest = rest[len(STEP_TABLES) :]
    spread, to_far, to_near, intensity_out, params, fields = rest
    cols = tile[1]
    right_first = is_even(place, 1, (64, 128))
    params[...] = jnp.zeros_like(params)
    params[0:64, :] = jnp.where(right_first, second[...], first[...])
    params[64 : 64 + cols, :] = own[0:cols, :]
    params[64 + cols : 128 + cols, :] = jnp.where(right_first, first[...], second[...])
    mask = masked(place, tile, whole, params[...], -64)
    inside = field_window(geo, place, tile, whole, -64)
    goals = [goal[0], goal[1]]
    intensity, grad = one_step(geo, mask, goals, inside, weights, spec, tabs, fields)
    last_spread_out(place, grad, spread, to_far, to_near)
    for side in (0, 1):
        intensity_out[side] = intensity[side]


def intensity_kernel(cols, intensity, mirror, out, flat):
    high, low = split(intensity[1])
    rest = (intensity[1] - high.astype(f32) - low.astype(f32)).astype(bf16)
    turned = dot(mirror[...], high) + (dot(mirror[...], low) + dot(mirror[...], rest))
    flat[...] = jnp.zeros_like(flat)
    flat[0 : cols // 2, :] = turned[0 : cols // 2]
    flat[cols // 2 : cols, :] = intensity[0][0 : cols // 2]
    out[...] = flat[...].T[:64, :cols]


def final_kernel(cols, place, own, far, near, out, wide):
    wide[...] = jnp.zeros_like(wide)
    wide[0 : own.shape[0], :] = last_gathered(place, own, far, near)
    out[...] = wide[...].T[H : H + 64, :cols]


def mirror_table(rows, rows_up, cols_up):
    table = np.zeros((rows_up, cols_up), np.float32)
    table[np.arange(rows), rows - 1 - np.arange(rows)] = 1.0
    return table.astype(ml_dtypes.bfloat16)


def call(kernel, name, out_shapes, scratch, args, space=pltpu.VMEM):
    return pl.pallas_call(
        kernel,
        name=name,
        out_shape=[
            shape if isinstance(shape, jax.ShapeDtypeStruct) else pltpu.VMEM(shape, f32)
            for shape in out_shapes
        ],
        in_specs=[pl.BlockSpec(memory_space=pltpu.VMEM)] * len(args),
        out_specs=[pl.BlockSpec(memory_space=pltpu.VMEM)] * len(out_shapes),
        scratch_shapes=[pltpu.VMEM(shape, f32) for shape in scratch],
        compiler_params=pltpu.CompilerParams(vmem_limit_bytes=VMEM_LIMIT),
    )(*[pltpu.with_memory_space_constraint(arg, space) for arg in args])


def per_device(rows, cols, mask_params, target_bits, kern_real, kern_imag, socs_weights):
    tile = mask_params.shape
    whole = (tile[0] * rows, tile[1] * cols)
    kernels = kern_real.shape[1] // KS
    axis = lax.broadcasted_iota(jnp.int32, (8, 256), 0)
    place = jnp.where(axis == 0, lax.axis_index("row"), lax.axis_index("col"))
    weights = jnp.broadcast_to(socs_weights[:, None], (kernels, 128))

    def swaps(count, start):
        pairs = [(i, i + 1) for i in range(start, count - 1, 2)]
        return pairs + [(b, a) for a, b in pairs]

    def row_exchange(to_far, to_near):
        far = lax.ppermute(to_far, "row", swaps(rows, 1))
        return far, lax.ppermute(to_near, "row", swaps(rows, 0))

    def col_exchange(to_first, to_second):
        first = lax.ppermute(to_first, "col", swaps(cols, 0))
        return first, lax.ppermute(to_second, "col", swaps(cols, 1))

    wide, slim = Geometry(tile[1] + 8 * H, 1), Geometry(tile[1] + 4 * H, 0)
    shared = row_tables()
    shared["wide_mirror"] = mirror_table(wide.centre, wide.half_up, wide.half_up)
    shared["slim_mirror"] = mirror_table(tile[1] // 2, up(tile[1] // 2, 16), slim.half_up)
    n = tile[1]
    far, near = row_exchange(mask_params, mask_params)
    params, target = call(
        early_kernel,
        "early",
        [(n, 128), (n, 128)],
        [(128, 256)],
        [mask_params, target_bits.T],
        pltpu.HBM,
    )
    near, place, weights = lax.optimization_barrier((near, place, weights))
    params, to_first, to_second = call(
        prep_kernel,
        "prep",
        [(n, 128), (176, 128), (176, 128)],
        [(128, 256)],
        [place, params, target, far, near],
    )
    first, second = col_exchange(to_first, to_second)
    made = {"wide": wide.tables(), "slim": slim.tables(), "shared": shared}
    place_of = {}

    def loader(kernel, name, geo, out_shapes, inputs, spaces, names):
        tables = [jnp.asarray(made[label][part]) for label, part in names]
        arrays = list(zip(inputs + tables, spaces + [pltpu.HBM] * len(tables)))
        outs = pl.pallas_call(
            functools.partial(kernel, geo, len(tables)),
            name=name,
            out_shape=[pltpu.VMEM(shape, f32) for shape in out_shapes]
            + [pltpu.VMEM(table.shape, table.dtype) for table in tables],
            in_specs=[pl.BlockSpec(memory_space=pltpu.VMEM)] * len(inputs)
            + [pl.BlockSpec(memory_space=pltpu.HBM)] * len(tables),
            out_specs=[pl.BlockSpec(memory_space=pltpu.VMEM)]
            * (len(out_shapes) + len(tables)),
            scratch_shapes=[pltpu.SemaphoreType.DMA((len(tables),))],
            compiler_params=pltpu.CompilerParams(vmem_limit_bytes=VMEM_LIMIT),
        )(*[pltpu.with_memory_space_constraint(*pair) for pair in arrays])
        place_of.update(zip(names, outs[len(out_shapes) :]))
        return outs[: len(out_shapes)]

    half_spec, wide_spec = loader(
        setup_kernel,
        "spectra",
        wide,
        [(kernels * KS, 512), (2 * kernels * wide.freqs_up, 256)],
        [
            kern_real,
            kern_imag,
            jnp.asarray(shared["tap_rows"]),
            jnp.asarray(made["wide"]["tap_cols"]),
        ],
        [pltpu.HBM] * 4,
        [("wide", part) for part in COLUMN_TABLES]
        + [("shared", part) for part in ROW_TABLES + ("wide_mirror",)],
    )

    def tabs(label):
        return [place_of[label, name] for name in COLUMN_TABLES] + [
            place_of["shared", name] for name in ROW_TABLES
        ]

    def spreads(geo):
        return [(geo.grad_up, 128)] + [(geo.grad_up // 2, 128)] * 2

    def fields(geo):
        return (2, kernels, geo.half_up, 128)

    spread, to_far, to_near, params, goal = call(
        functools.partial(first_kernel, wide, tile, whole),
        "first",
        spreads(wide) + [(slim.mask_up, 128), (2, slim.half_up, 128)],
        [(wide.mask_up, 128), (wide.centre + wide.half_up, 128), fields(wide)],
        [place, weights, params, target, first, second, wide_spec]
        + [place_of["shared", "wide_mirror"], *tabs("wide")],
    )
    far, near = row_exchange(to_far, to_near)
    (slim_spec,) = loader(
        slim_kernel,
        "slim",
        slim,
        [(2 * kernels * slim.freqs_up, 256)],
        [half_spec, jnp.asarray(made["slim"]["tap_cols"])],
        [pltpu.VMEM, pltpu.HBM],
        [("slim", part) for part in COLUMN_TABLES] + [("shared", "slim_mirror")],
    )
    spread, to_far, to_near, params = call(
        functools.partial(second_kernel, slim, tile, whole),
        "second",
        spreads(slim) + [(slim.grad_up, 128)],
        [fields(slim)],
        [place, weights, spread, far, near, params, goal, slim_spec, *tabs("slim")],
    )
    far, near = row_exchange(to_far, to_near)
    params, to_first, to_second = call(
        functools.partial(update_kernel, n),
        "update",
        [(slim.grad_up, 128), (64, 128), (64, 128)],
        [],
        [place, spread, far, near, params],
    )
    first, second = col_exchange(to_first, to_second)
    spread, to_far, to_near, intensity = call(
        functools.partial(third_kernel, slim, tile, whole),
        "third",
        spreads(slim)[:1] + [(slim.grad_up // 4, 128)] * 2 + [(2, slim.half_up, 128)],
        [(slim.mask_up, 128), fields(slim)],
        [place, weights, params, first, second, goal, slim_spec, *tabs("slim")],
    )
    far, near = row_exchange(to_far, to_near)
    (intensity,) = call(
        functools.partial(intensity_kernel, n),
        "intensity",
        [jax.ShapeDtypeStruct(tile, f32)],
        [(256, 128)],
        [intensity, place_of["shared", "slim_mirror"]],
    )
    (mask_grad,) = call(
        functools.partial(final_kernel, n),
        "final",
        [jax.ShapeDtypeStruct(tile, f32)],
        [(256, 128)],
        [place, spread, far, near],
    )
    return mask_grad, intensity


def solution(mesh):
    placed = (P("row", "col"), P("row", "col"), P(), P(), P())
    return jax.shard_map(
        functools.partial(per_device, mesh.shape["row"], mesh.shape["col"]),
        mesh=mesh,
        in_specs=placed,
        out_specs=(P("row", "col"), P("row", "col")),
        check_vma=False,
    )
```
